32 devices in a mesh: lon: 2 (over x), lat: 4 (over y, core), lev: 4 (over z).
Axes of the slice: x: 2, y: 2, z: 4, core: 2. Of those that a mesh axis runs over, the one named last changes fastest.
Arguments:
- adjoint_field: float32 [12, 12, 128, 256], P(None, 'lev', 'lat', 'lon'), may hold values from -6 to 6
- east_courant: float32 [12, 128, 256], P('lev', 'lat', 'lon'), may hold values from -0.2 to 0.2
- north_courant: float32 [12, 128, 256], P('lev', 'lat', 'lon'), may hold values from -0.2 to 0.2
- pole_courant: float32 [12, 256], P('lev', 'lon'), may hold values from -0.2 to 0.2
- mix_fraction: float32 [12, 128, 256], P('lev', 'lat', 'lon'), may hold values from 0.05 to 0.6
- detrain_share: float32 [12, 128, 256], P('lev', 'lat', 'lon'), may hold values from 0.1 to 3
- sounding_owner: int32 [2, 2048, 1], P(None, ('lon', 'lat')), may hold values from 0 to 7; in each aligned block of 256 rows (0 to 255, 256 to 511, ..., all dimensions but the last counted through in order) at most 64 rows name the same one
- sounding_cell: int32 [2, 2048], P(None, ('lon', 'lat')), may hold values from 0 to 4095
- sounding_count: int32 [2, 8], P(None, ('lon', 'lat')), may hold values from 1 to 256, 1280 in all within a row
- sounding_forcing: float32 [2, 12, 2048], P(None, 'lev', ('lon', 'lat')), may hold values from -6 to 6
Outputs:
- earlier_adjoint: float32 [12, 12, 128, 256], P(None, 'lev', 'lat', 'lon')
The draws below stay inside these ranges and needn't reach their ends.
Inputs may be any that keep to these rules, and one draw needn't show every extreme that they name: `sounding_owner`: in each aligned block of 256 slots of one step (the slots of one device) no owner is named more than 64 times, a bound that some block reaches. `sounding_count`: each step's counts sum to 1280; at each step some device has exactly 256.
All inputs are finite; a program needn't handle non-finite values.
Results may differ from the reference program's by a relative error of at most 0.0001.
Values sent between devices are 32-bit elements; how exact they have to be, the bound alone decides.
No kernel may reach another device: no remote copies, remote signals or barrier semaphores. Data moves between devices by JAX's collectives and lax.ppermute only.
A program may use at most 128 MiB of HBM per device.

```python
import math
import jax
import jax.numpy as jnp
import numpy as np
from jax import lax

NTR = 12
CLAT = 32
CLON = 128
STEPS = 2
S_DEV = 256
OWNERS = 8
CAP = 64
SOUNDINGS = 2048
LIVE = 1280
NLEV = 12
NLAT = 128
NLON = 256
N_LAT = 4


def with_ends(values, rng, least, largest):
    place = [jax.random.randint(jax.random.fold_in(rng, axis), (), 0, length) for axis, length in enumerate(values.shape)]
    longest = values.shape.index(max(values.shape))
    neighbour = place[:longest] + [(place[longest] + 1) % values.shape[longest]] + place[longest + 1:]
    return values.at[tuple(place)].set(least).at[tuple(neighbour)].set(largest)


def block_scale(own_key, dims, pieces, least, top_value):
    loudness, own = 1.0, jax.random.fold_in(own_key, 6)
    for dim, shards_of in pieces:
        steps = jnp.exp(jax.random.uniform(jax.random.fold_in(own, dim), (shards_of,), jnp.float32, least / len(pieces), top_value / len(pieces)))
        loudness = loudness * jnp.repeat(steps, dims[dim] // shards_of).reshape([-1 if axis == dim else 1 for axis in range(len(dims))])
    return loudness


def profile(amount, total, reach, slope):
    loads = [(1 << 20) // math.isqrt(rank ** slope) + 1 for rank in range(2, amount + 1)]
    surplus, counts = total - reach - (amount - 1), [1] * (amount - 1)
    while surplus > 0:
        free = [i for i in range(amount - 1) if counts[i] < reach]
        mass, left = sum([loads[i] for i in free]), surplus
        for i in free:
            addition = min(reach - counts[i], max(1, left * loads[i] // mass), surplus)
            counts[i] = counts[i] + addition
            surplus = surplus - addition
    return np.array([reach] + counts)


def uneven_parts(stream_key, number_of, total, limit, skew):
    if number_of == 2:
        one = jax.random.randint(stream_key, (), max(1, total - limit), min(limit, total - 1) + 1)
        return jnp.stack([one, total - one])
    sizes = jnp.asarray(profile(number_of, total, limit, skew), jnp.int32)
    couples = (number_of - 1) // 2
    source_of, taker = sizes[1:1 + 2 * couples:2], sizes[2:2 + 2 * couples:2]
    room = jnp.minimum(source_of - 1, limit - taker)
    shifted = jax.random.randint(jax.random.fold_in(stream_key, 1), (couples,), 0, 1 << 20) % (room + 1)
    sizes = sizes.at[1:1 + 2 * couples:2].set(source_of - shifted).at[2:2 + 2 * couples:2].set(taker + shifted)
    return sizes[jax.random.permutation(jax.random.fold_in(stream_key, 2), number_of)]


def deal_out(own_key, own, number, rows, amount, top, most, lean):
    ranking = jax.random.permutation(own_key, amount)
    heavy_load, common = portions_of(amount, rows * top, most, lean, True), portions_of(amount, rows * top, most, lean, False)
    places = jnp.arange(amount)

    def named(tallies, turn):
        used = int((tallies > 0).sum())
        fixed = max(1, used // 4)
        passed = fixed + (places - fixed + turn * (used - fixed)) % max(1, amount - fixed)
        return jnp.zeros((amount,), jnp.int32).at[ranking[jnp.where(places < fixed, places, passed)]].set(jnp.asarray(tallies, jnp.int32))

    tallies = jnp.where(number % 4 == 0, named(heavy_load, number // 4), named(common, number - number // 4 - 1))
    mixed = jax.random.permutation(jax.random.fold_in(own, 3), amount)
    donor, taker = mixed[0:amount // 2 * 2:2], mixed[1:amount // 2 * 2:2]
    margin = jnp.minimum(tallies[donor] - 1, most - tallies[taker]) // 2
    margin = jnp.where((donor == ranking[0]) | (taker == ranking[0]) | (tallies[taker] == 0), 0, jnp.maximum(margin, 0))
    passed = jax.random.randint(jax.random.fold_in(own, 4), (amount // 2,), 0, 1 << 20) % (margin + 1)
    tallies = tallies.at[donor].add(-passed).at[taker].add(passed)
    labels = jnp.searchsorted(jnp.cumsum(tallies), jnp.arange(rows * top), side="right").astype(jnp.int32)
    grid = labels.reshape(top, rows).T
    grid = grid[jax.random.permutation(jax.random.fold_in(own, 1), rows)]
    turn = jax.random.randint(jax.random.fold_in(own, 2), (rows, 1), 0, top)
    return jnp.take_along_axis(grid, (jnp.arange(top)[None, :] + turn) % top, axis=1)


def portions_of(number_of, total, most, lean, full):
    portions = [(1 << 20) // math.isqrt(rank ** lean) + 1 for rank in range(1, number_of + 1)]
    largest = most if full else min(most, max(-(-total // number_of), total * portions[0] // sum(portions)))
    least = 1 if total - largest >= number_of - 1 else 0
    counts, rest = [largest] + [least] * (number_of - 1), total - largest - least * (number_of - 1)
    while rest > 0:
        movable = [i for i in range(1, number_of) if counts[i] < largest] or [i for i in range(1, number_of) if counts[i] < most]
        whole, budget = sum([portions[i] for i in movable]), rest
        for i in movable:
            addition = min(most - counts[i], max(1, budget * portions[i] // whole), rest)
            counts[i] = counts[i] + addition
            rest = rest - addition
    return np.array(counts)


def centred(key, shape, scale, most, cuts=(), held_as=jnp.bfloat16):
    drawn = scale * jax.random.normal(key, shape, jnp.float32)
    if cuts:
        drawn = drawn * block_scale(key, shape, cuts, -0.22, 0.18)
    return jnp.clip(drawn, -most, most).astype(held_as)


def setup_inputs(seed: int = 0) -> dict:
    streams_of = jax.random.split(jax.random.key(seed), 11)
    adjoint_field = centred(streams_of[0], (NTR, NLEV, NLAT, NLON), 1.0, 6.0, ((1, 4), (2, 4), (3, 2)), jnp.float32)
    east_courant = jnp.clip(jax.random.uniform(streams_of[1], (NLEV, NLAT, NLON), jnp.float32, -0.2, 0.2) * block_scale(streams_of[1], (NLEV, NLAT, NLON), ((0, 4), (1, 4), (2, 2)), -0.4, 0.0), -0.2, 0.2)
    north_courant = jnp.clip(jax.random.uniform(streams_of[2], (NLEV, NLAT, NLON), jnp.float32, -0.2, 0.2) * block_scale(streams_of[2], (NLEV, NLAT, NLON), ((0, 4), (1, 4), (2, 2)), -0.4, 0.0), -0.2, 0.2)
    pole_courant = jnp.clip(jax.random.uniform(streams_of[3], (NLEV, NLON), jnp.float32, -0.2, 0.2) * block_scale(streams_of[3], (NLEV, NLON), ((0, 4), (1, 2)), -0.4, 0.0), -0.2, 0.2)
    mix_fraction = jnp.clip(0.05 + 0.55 * jax.random.uniform(streams_of[4], (NLEV, NLAT, NLON), jnp.float32) ** block_scale(streams_of[4], (NLEV, NLAT, NLON), ((0, 4), (1, 4), (2, 2)), -0.2, 0.2), 0.05, 0.6)
    detrain_share = jnp.clip(jnp.exp(math.log(3.0) - 3.4011974 * jax.random.uniform(streams_of[5], (NLEV, NLAT, NLON), jnp.float32) ** block_scale(streams_of[5], (NLEV, NLAT, NLON), ((0, 4), (1, 4), (2, 2)), -0.2, 0.2)), 0.1, 3.0)
    sounding_owner_keys = jax.random.split(jax.random.fold_in(streams_of[6], 1), STEPS * SOUNDINGS // S_DEV)
    sounding_owner_turns = jax.random.permutation(jax.random.fold_in(streams_of[6], 3), STEPS * SOUNDINGS // S_DEV)
    sounding_owner = jax.vmap(lambda own, number: deal_out(jax.random.fold_in(streams_of[6], 2), own, number, S_DEV, OWNERS, 1, CAP, 2))(sounding_owner_keys, sounding_owner_turns).reshape((STEPS, SOUNDINGS, 1))
    sounding_cell = with_ends(jax.random.randint(streams_of[7], (STEPS, SOUNDINGS), 0, CLAT * CLON), jax.random.fold_in(streams_of[7], 1), 0, (CLAT * CLON) - 1).astype(jnp.int32)
    sounding_count = jax.vmap(lambda own: uneven_parts(own, OWNERS, LIVE, S_DEV, 2))(jax.random.split(streams_of[8], STEPS)).reshape((STEPS, OWNERS)).astype(jnp.int32)
    sounding_forcing = centred(streams_of[9], (STEPS, NLEV, SOUNDINGS), 1.0, 6.0, ((1, 4), (2, 8)), jnp.float32)
    return dict(adjoint_field=adjoint_field, east_courant=east_courant, north_courant=north_courant, pole_courant=pole_courant, mix_fraction=mix_fraction, detrain_share=detrain_share, sounding_owner=sounding_owner, sounding_cell=sounding_cell, sounding_count=sounding_count, sounding_forcing=sounding_forcing)


def reference(adjoint_field, east_courant, north_courant, pole_courant, mix_fraction, detrain_share, sounding_owner, sounding_cell, sounding_count, sounding_forcing):
    half_circle = NLON // 2
    upwind_east = jnp.maximum(east_courant, 0.0)
    upwind_west = -jnp.minimum(jnp.roll(east_courant, 1, axis=2), 0.0)
    lat_index = jnp.arange(NLAT, dtype=jnp.int32)[None, :, None]
    partner_top = jnp.roll(north_courant[:, -1, :], half_circle, axis=1)
    partner_pole = jnp.roll(pole_courant, half_circle, axis=1)
    upwind_north = jnp.maximum(north_courant, 0.0) + jnp.where(lat_index == NLAT - 1, -jnp.minimum(partner_top, 0.0)[:, None, :], 0.0)
    south_wind = jnp.concatenate([jnp.zeros_like(north_courant[:, :1, :]), north_courant[:, :-1, :]], axis=1)
    upwind_south = jnp.where(lat_index == 0, (jnp.maximum(pole_courant, 0.0) - jnp.minimum(partner_pole, 0.0))[:, None, :], -jnp.minimum(south_wind, 0.0))

    slot_index = jnp.arange(SOUNDINGS, dtype=jnp.int32)
    holder = (slot_index // S_DEV).astype(jnp.int32)
    live_slots = (slot_index % S_DEV)[None, :] < sounding_count[:, holder]
    owner_ids = sounding_owner[:, :, 0]
    grid_row = (owner_ids % N_LAT) * CLAT + sounding_cell // CLON
    grid_col = (owner_ids // N_LAT) * CLON + sounding_cell % CLON
    flat_index = (grid_row * NLON + grid_col).astype(jnp.int32)
    values = jnp.where(live_slots[:, None, :], sounding_forcing, 0.0)
    step_ids = jnp.arange(STEPS, dtype=jnp.int32)[:, None]
    forcing_grid = jnp.zeros((STEPS, NLEV, NLAT * NLON), jnp.float32).at[step_ids, :, flat_index].add(jnp.swapaxes(values, 1, 2))
    forcing_grid = forcing_grid.reshape(STEPS, NLEV, NLAT, NLON)
    column_total = jnp.sum(detrain_share, axis=0)

    def one_tracer(adjoint):
        for position in range(STEPS):
            step_now = STEPS - 1 - position
            adjoint = adjoint + forcing_grid[step_now]
            column_sum = jnp.sum(detrain_share * adjoint, axis=0)
            adjoint = (1.0 - mix_fraction) * adjoint + mix_fraction * (column_sum / column_total)[None]
            east_side = jnp.roll(adjoint, -1, axis=2)
            west_side = jnp.roll(adjoint, 1, axis=2)
            north_side = jnp.concatenate([adjoint[:, 1:, :], jnp.roll(adjoint[:, -1:, :], half_circle, axis=2)], axis=1)
            south_side = jnp.concatenate([jnp.roll(adjoint[:, :1, :], half_circle, axis=2), adjoint[:, :-1, :]], axis=1)
            adjoint = adjoint + upwind_east * (east_side - adjoint) + upwind_west * (west_side - adjoint) + upwind_north * (north_side - adjoint) + upwind_south * (south_side - adjoint)
        return adjoint

    return lax.map(one_tracer, adjoint_field)
```

```python
import functools

import jax
import jax.numpy as jnp
from jax import lax
from jax.experimental import pallas as pl
from jax.experimental.pallas import tpu as pltpu
from jax.sharding import PartitionSpec as P

F32 = jnp.float32
LANES = 128
TOP, BOTTOM, ASCENDING, PARITY, SELF, NORTH, SOUTH, EAST, WEST, NORTH_ROW, SOUTH_ROW = range(11)


def swap_over(value, axis, bit):
    return lax.ppermute(value, axis, [(i, i ^ bit) for i in range(lax.axis_size(axis))])


def shift_over(value, axis, steps):
    count = lax.axis_size(axis)
    return lax.ppermute(value, axis, [(i, (i + steps) % count) for i in range(count)])


def meridian_rings(lon_count, lat_count, steps):
    pairs = []
    for lon in range(lon_count // 2):
        ring = [lon * lat_count + lat for lat in range(lat_count)]
        ring += [(lon + lon_count // 2) * lat_count + lat for lat in reversed(range(lat_count))]
        pairs += [(ring[i], ring[(i + steps) % len(ring)]) for i in range(len(ring))]
    return pairs


def exchange_rows(forward, back):
    lon_count, lat_count = lax.axis_size("lon"), lax.axis_size("lat")
    return (
        lax.ppermute(forward, ("lon", "lat"), meridian_rings(lon_count, lat_count, 1)),
        lax.ppermute(back, ("lon", "lat"), meridian_rings(lon_count, lat_count, -1)),
    )


def exchange_columns(columns):
    if lax.axis_size("lon") == 2:
        other = swap_over(columns, "lon", 1)
        return other, other
    return shift_over(columns, "lon", -1), shift_over(columns, "lon", 1)


def gather_blocks(block):
    blocks = block[None]
    for axis in ("lat", "lon"):
        count = lax.axis_size(axis)
        if count & (count - 1) == 0 and count <= 4:
            bit = 1
            while bit < count:
                blocks = jnp.concatenate([blocks, swap_over(blocks, axis, bit)], axis=0)
                bit *= 2
        else:
            blocks = lax.all_gather(blocks, axis, axis=0, tiled=True)
    return blocks


def lane_and_row(rows):
    return (
        lax.broadcasted_iota(jnp.int32, (rows, LANES), 1),
        lax.broadcasted_iota(jnp.int32, (rows, LANES), 0),
    )


def shifted(x, side, north, south):
    rows = x.shape[0]
    lane, row = lane_and_row(rows)
    east = jnp.where(lane == LANES - 1, side, pltpu.roll(x, LANES - 1, 1))
    west = jnp.where(lane == 0, side, pltpu.roll(x, 1, 1))
    above = jnp.where(row == rows - 1, north, pltpu.roll(x, rows - 1, 0))
    below = jnp.where(row == 0, south, pltpu.roll(x, 1, 0))
    return east, west, above, below


def stencil(coefs, x, side, north, south):
    east, west, above, below = shifted(x, side, north, south)
    own, to_east, to_west, to_north, to_south = coefs
    return own * x + to_east * east + to_west * west + to_north * above + to_south * below


class Columns:
    def __init__(self, rows):
        self.rows = rows
        self.per = LANES // rows
        self.blocks = [jnp.zeros((rows, LANES), F32)] * self.per
        self.lane = lane_and_row(rows)[0]

    def put(self, index, slab):
        group, place = divmod(index, self.per)
        turned = pltpu.roll(slab, 2 * group + 1, 1)
        self.blocks[place] = jnp.where(self.lane // 2 == group, turned, self.blocks[place])

    def get(self, rows):
        return jnp.transpose(jnp.concatenate(self.blocks, axis=0))[:rows]


def sides_of(eastern, western):
    rows = eastern.shape[0]
    row = lane_and_row(rows)[1]
    return jnp.where(row % 2 == 0, pltpu.roll(eastern, rows - 1, 0), pltpu.roll(western, 1, 0))


def turn(rows):
    pad = jnp.zeros((LANES - rows.shape[0], LANES), F32)
    return jnp.transpose(jnp.concatenate([rows, pad], axis=0))


def side_of(turned, index, rows):
    group, place = divmod(index, LANES // rows)
    return pltpu.roll(turned[place * rows : (place + 1) * rows], (LANES - 2 * group - 1) % LANES, 1)


def first_kernel(
    tracers, levels, rows, flags, field, detrain, mix, east, north, pole, keep, send, forward, back, columns, halves, ring
):
    half = tracers // 2
    slabs = tracers * levels
    weights = [detrain[k] for k in range(levels)]
    stay = [1.0 - mix[k] for k in range(levels)]
    cols = Columns(rows)
    ring[...] = jnp.zeros(ring.shape, F32)

    def edge_rows(place, slab):
        ring[0, place : place + 1, :] = slab[rows - 1 : rows]
        ring[1, place : place + 1, :] = slab[:1]

    for t in range(tracers):
        partial = None
        for k in range(levels):
            slab = field[t, k]
            term = weights[k] * slab
            partial = term if partial is None else partial + term
            slab = stay[k] * slab
            cols.put(t * levels + k, slab)
            edge_rows(t * levels + k, slab)
        halves[t // half, (t % half) * rows : (t % half + 1) * rows, :] = partial
        cols.put(slabs + t, partial)
        edge_rows(slabs + t, partial)
    total = functools.reduce(lambda a, b: a + b, weights)
    for h in range(2):
        halves[h, half * rows :, :] = total[h * rows // 2 : (h + 1) * rows // 2]
    cols.put(slabs + tracers, total)
    edge_rows(slabs + tracers, total)
    base = slabs + tracers + 1
    per = LANES // rows
    group = -(-base // per)
    for k in range(levels):
        edge_rows(base + k, mix[k])
        edge_rows(base + levels + k, detrain[k])
        ring[0, base + 2 * levels + k : base + 2 * levels + k + 1, :] = north[k, rows - 1 : rows, :]
        ring[1, base + 2 * levels + k : base + 2 * levels + k + 1, :] = pole[k : k + 1, :]
        cols.put(group * per + k, mix[k])
        cols.put((group + 1) * per + k, detrain[k])
        cols.put((group + 2) * per + k, east[k])
    parity = flags[PARITY]
    keep[...] = halves[parity]
    send[...] = halves[1 - parity]
    ascending = flags[ASCENDING]
    forward[...] = ring[1 - ascending]
    back[...] = ring[ascending]
    columns[...] = cols.get(columns.shape[0])


def second_kernel(
    tracers, levels, rows, flags, field, detrain, mix, east, north, pole, forward, back, eastern, western,
    keep, send, coefs, edges, turned, halves,
):
    half = tracers // 2
    slabs = tracers * levels
    base = slabs + tracers + 1
    per = LANES // rows
    group = -(-base // per)
    ascending = flags[ASCENDING] == 1
    from_north = jnp.where(ascending, back[...], forward[...])
    from_south = jnp.where(ascending, forward[...], back[...])
    edges[0] = from_north
    edges[1] = from_south
    sides = sides_of(eastern[...], western[...])
    around = turn(sides)
    turned[...] = around
    lane, row = lane_and_row(rows)
    top = jnp.logical_and(row == rows - 1, flags[TOP] == 1)
    bottom = jnp.logical_and(row == 0, flags[BOTTOM] == 1)
    weighted, stay = [], []
    mixed = None
    for k in range(levels):
        place = base + 2 * levels + k
        wind = east[k]
        behind = jnp.where(lane == 0, side_of(around, (group + 2) * per + k, rows), pltpu.roll(wind, 1, 1))
        to_east = jnp.maximum(wind, 0.0)
        to_west = jnp.maximum(-behind, 0.0)
        wind = north[k]
        across_north = jnp.maximum(-from_north[place : place + 1], 0.0)
        to_north = jnp.maximum(wind, 0.0) + jnp.where(top, across_north, 0.0)
        below = from_south[place : place + 1]
        across_south = jnp.maximum(pole[k : k + 1, :], 0.0) + jnp.maximum(-below, 0.0)
        behind = jnp.where(row == 0, below, pltpu.roll(wind, 1, 0))
        to_south = jnp.where(bottom, across_south, jnp.maximum(-behind, 0.0))
        own = 1.0 - to_east - to_west - to_north - to_south
        five = [own, to_east, to_west, to_north, to_south]
        for i in range(5):
            coefs[i, k] = five[i]
        weighted.append([detrain[k] * c for c in five])
        stay.append(1.0 - mix[k])
        share = mix[k]
        around_share = shifted(
            share,
            side_of(around, group * per + k, rows),
            from_north[base + k : base + k + 1],
            from_south[base + k : base + k + 1],
        )
        terms = [c * s for c, s in zip(weighted[k], (share,) + around_share)]
        mixed = terms if mixed is None else [a + b for a, b in zip(mixed, terms)]
    for t in range(tracers):
        partial = None
        for k in range(levels):
            place = t * levels + k
            term = stencil(
                weighted[k],
                stay[k] * field[t, k],
                side_of(around, place, rows),
                from_north[place : place + 1],
                from_south[place : place + 1],
            )
            partial = term if partial is None else partial + term
        halves[t // half, (t % half) * rows : (t % half + 1) * rows, :] = partial
    start = half * rows
    for i in range(5):
        for h in range(2):
            at = start + i * (rows // 2)
            halves[h, at : at + rows // 2, :] = mixed[i][h * rows // 2 : (h + 1) * rows // 2]
    start += 5 * (rows // 2)
    halves[:, start:, :] = jnp.zeros((2, halves.shape[1] - start, LANES), F32)
    lon_rows = 2 * (group - slabs // per)
    halves[0, start : start + lon_rows, :] = sides[2 * (slabs // per) : 2 * group]
    start += lon_rows
    halves[0, start : start + tracers + 1, :] = from_north[slabs : slabs + tracers + 1]
    halves[1, start : start + tracers + 1, :] = from_south[slabs : slabs + tracers + 1]
    parity = flags[PARITY]
    keep[...] = halves[parity]
    send[...] = halves[1 - parity]


def pieces(x):
    high = x.astype(jnp.bfloat16)
    rest = x - high.astype(F32)
    middle = rest.astype(jnp.bfloat16)
    low = (rest - middle.astype(F32)).astype(jnp.bfloat16)
    return [high, middle, low]


def product(a, b):
    return lax.dot_general(a, b, (((1,), (1,)), ((), ())), preferred_element_type=F32)


def forcing_kernel(levels, rows, steps, flags, slots, detrain, mix, coefs, edges, turned, base, grids, edge_rows, sums):
    count = slots.shape[2]
    per = LANES // rows
    row_ids = lax.broadcasted_iota(jnp.int32, (rows, count), 0)
    lane_ids = lax.broadcasted_iota(jnp.int32, (LANES, count), 0)
    group = -(-base // per)

    def add_block(index, carry):
        late, early, ring_sides = carry
        block = slots[index]
        results = []
        for step in range(steps):
            first = step * (levels + 2)
            values = [block[first + k : first + k + 1] for k in range(levels)]
            owner = block[first + levels : first + levels + 1].astype(jnp.int32)
            cell = block[first + levels + 1 : first + levels + 2].astype(jnp.int32)
            slot_row, slot_lane = cell // LANES, cell % LANES
            lanes = (lane_ids == slot_lane).astype(F32).astype(jnp.bfloat16)
            here = jnp.logical_and(row_ids == slot_row, owner == flags[SELF])
            left = [jnp.where(here, value, 0.0) for value in values]
            if step == steps - 1:
                in_north = jnp.logical_and(owner == flags[NORTH], slot_row == flags[NORTH_ROW])
                in_south = jnp.logical_and(owner == flags[SOUTH], slot_row == flags[SOUTH_ROW])
                left += [jnp.where(in_north, value, 0.0) for value in values]
                left += [jnp.where(in_south, value, 0.0) for value in values]
                left += [jnp.zeros((8 - 2 * levels, count), F32)]
            left = jnp.concatenate(left, axis=0)
            results.append(sum(product(piece, lanes) for piece in pieces(left)))
            if step == steps - 1:
                in_east = jnp.logical_and(owner == flags[EAST], slot_lane == 0)
                in_west = jnp.logical_and(owner == flags[WEST], slot_lane == LANES - 1)
                right = [jnp.where(in_east, value, 0.0) for value in values]
                right += [jnp.where(in_west, value, 0.0) for value in values]
                right += [jnp.zeros((8 - 2 * levels, count), F32)]
                right = jnp.concatenate(right, axis=0)
                at_row = (row_ids == slot_row).astype(F32).astype(jnp.bfloat16)
                ring_sides = ring_sides + sum(product(at_row, piece) for piece in pieces(right))
        return late + results[1], early + results[0], ring_sides

    late, early, ring_sides = lax.fori_loop(
        0,
        slots.shape[0],
        add_block,
        (
            jnp.zeros((levels * rows + 8, LANES), F32),
            jnp.zeros((levels * rows, LANES), F32),
            jnp.zeros((rows, 8), F32),
        ),
    )
    lane, _ = lane_and_row(rows)
    north_rows = late[levels * rows : levels * rows + levels]
    south_rows = late[levels * rows + levels : levels * rows + 2 * levels]
    edge_rows[...] = late[levels * rows :]
    around = turned[...]
    at_end = at_first = None
    ring = jnp.zeros((rows, LANES), F32)
    ring_north = jnp.zeros((1, LANES), F32)
    ring_south = jnp.zeros((1, LANES), F32)
    for k in range(levels):
        own = late[k * rows : (k + 1) * rows]
        now = early[k * rows : (k + 1) * rows]
        east_side = jnp.broadcast_to(ring_sides[:, k : k + 1], (rows, LANES))
        west_side = jnp.broadcast_to(ring_sides[:, levels + k : levels + k + 1], (rows, LANES))
        side = jnp.where(lane == LANES - 1, east_side, jnp.where(lane == 0, west_side, 0.0))
        grids[k] = own
        grids[levels + k] = now
        grids[2 * levels + k] = side
        mix_side = side_of(around, group * per + k, rows)
        detrain_side = side_of(around, (group + 1) * per + k, rows)
        north, south = north_rows[k : k + 1], south_rows[k : k + 1]
        moved = stencil(
            [coefs[i, k] for i in range(5)],
            (1.0 - mix[k]) * own,
            (1.0 - mix_side) * side,
            (1.0 - edges[0, base + k : base + k + 1, :]) * north,
            (1.0 - edges[1, base + k : base + k + 1, :]) * south,
        )
        first = detrain[k] * own
        second = detrain[k] * (moved + now)
        at_first = first if at_first is None else at_first + first
        at_end = second if at_end is None else at_end + second
        ring = ring + detrain_side * side
        place = base + levels + k
        ring_north = ring_north + edges[0, place : place + 1, :] * north
        ring_south = ring_south + edges[1, place : place + 1, :] * south
    sums[:rows] = at_first
    sums[rows : 2 * rows] = at_end
    flat = jnp.transpose(jnp.concatenate([ring] + [jnp.zeros((rows, LANES), F32)] * (per - 1), axis=0))
    sums[2 * rows :] = jnp.concatenate(
        [ring_north, ring_south, flat[LANES - 1 :], flat[:1], jnp.zeros((4, LANES), F32)], axis=0
    )


def third_kernel(
    tracers, levels, rows, flags, field, mix, coefs, edges, turned, grids, edge_rows,
    mine_first, other_first, mine_second, other_second,
    mixed_out, forward, back, columns, first, second, ring,
):
    half = tracers // 2
    slabs = tracers * levels
    base = slabs + tracers + 1
    per = LANES // rows
    group = -(-base // per)
    parity = flags[PARITY]
    second_rows = second.shape[1]
    first[parity] = mine_first[...]
    first[1 - parity] = other_first[...]
    second[parity] = mine_second[:second_rows]
    second[1 - parity] = other_second[:second_rows]
    forced = mine_second[second_rows:] + other_second[second_rows:]
    forced_first, forced_second = forced[:rows], forced[rows : 2 * rows]
    forced_ring = forced[2 * rows :]

    start = half * rows
    total = jnp.concatenate([first[0, start:, :], first[1, start:, :]], axis=0)
    inverse = 1.0 / total
    spread = []
    for i in range(5):
        at = start + i * (rows // 2)
        spread.append(jnp.concatenate([second[h, at : at + rows // 2, :] for h in range(2)], axis=0))
    start += 5 * (rows // 2)
    groups = tracers // per
    lon_sums = second[0, start : start + 2 * (group - slabs // per), :]
    start += 2 * (group - slabs // per)
    north_sums = second[0, start : start + tracers, :] + forced_ring[0:1]
    north_column = north_sums / second[0, start + tracers : start + tracers + 1, :]
    south_sums = second[1, start : start + tracers, :] + forced_ring[1:2]
    south_column = south_sums / second[1, start + tracers : start + tracers + 1, :]

    def tiled(x):
        lane = lax.broadcasted_iota(jnp.int32, x.shape, 1)
        x = jnp.where(lane < rows, x, 0.0)
        width = rows
        while width < LANES:
            x = x + pltpu.roll(x, width, 1)
            width *= 2
        return x

    side_total = tiled(lon_sums[2 * groups : 2 * groups + 2])
    side_forced = tiled(forced_ring[2:4])
    side_rows = [(lon_sums[2 * g : 2 * g + 2] + side_forced) / side_total for g in range(groups)]
    around_column = turn(jnp.concatenate(side_rows + [jnp.zeros((8 - 2 * groups, LANES), F32)], axis=0))
    around = turned[...]

    stay = [1.0 - mix[k] for k in range(levels)]
    mix_side = [side_of(around, group * per + k, rows) for k in range(levels)]
    forced_side = [(1.0 - mix_side[k]) * grids[2 * levels + k] for k in range(levels)]
    mix_edge = [[edges[e, base + k : base + k + 1, :] for k in range(levels)] for e in range(2)]
    forced_edge = [
        [(1.0 - mix_edge[e][k]) * edge_rows[e * levels + k : e * levels + k + 1, :] for k in range(levels)]
        for e in range(2)
    ]
    five = [[coefs[i, k] for i in range(5)] for k in range(levels)]
    cols = Columns(rows)
    ring[...] = jnp.zeros(ring.shape, F32)
    for t in range(tracers):
        h, at = t // half, (t % half) * rows
        column = (first[h, at : at + rows, :] + forced_first) * inverse
        column_side = side_of(around_column, t, rows)
        column_north, column_south = north_column[t : t + 1], south_column[t : t + 1]
        later = second[h, at : at + rows, :] + forced_second
        later = (later + stencil(spread, column, column_side, column_north, column_south)) * inverse
        for k in range(levels):
            place = t * levels + k
            now = stay[k] * (field[t, k] + grids[k]) + mix[k] * column
            side = side_of(around, place, rows) + forced_side[k] + mix_side[k] * column_side
            north = edges[0, place : place + 1, :] + forced_edge[0][k] + mix_edge[0][k] * column_north
            south = edges[1, place : place + 1, :] + forced_edge[1][k] + mix_edge[1][k] * column_south
            moved = stencil(five[k], now, side, north, south)
            moved = stay[k] * (moved + grids[levels + k]) + mix[k] * later
            mixed_out[t, k] = moved
            cols.put(place, moved)
            ring[0, place : place + 1, :] = moved[rows - 1 : rows]
            ring[1, place : place + 1, :] = moved[:1]
    ascending = flags[ASCENDING]
    forward[...] = ring[1 - ascending]
    back[...] = ring[ascending]
    columns[...] = cols.get(columns.shape[0])


def last_kernel(tracers, levels, rows, flags, mixed, coefs, forward, back, eastern, western, out):
    ascending = flags[ASCENDING] == 1
    from_north = jnp.where(ascending, back[...], forward[...])
    from_south = jnp.where(ascending, forward[...], back[...])
    around = turn(sides_of(eastern[...], western[...]))
    five = [[coefs[i, k] for i in range(5)] for k in range(levels)]
    for t in range(tracers):
        for k in range(levels):
            place = t * levels + k
            out[t, k] = stencil(
                five[k],
                mixed[t, k],
                side_of(around, place, rows),
                from_north[place : place + 1],
                from_south[place : place + 1],
            )


def up8(count):
    return -(-count // 8) * 8


def call(kernel, flags, args, outs, scratch=()):
    vmem = pl.BlockSpec(memory_space=pltpu.VMEM)
    shapes = [jax.ShapeDtypeStruct(shape, F32) for shape in outs]
    return pl.pallas_call(
        kernel,
        out_shape=shapes,
        in_specs=[pl.BlockSpec(memory_space=pltpu.SMEM)] + [vmem] * len(args),
        out_specs=[vmem] * len(shapes),
        scratch_shapes=[pltpu.VMEM(shape, F32) for shape in scratch],
        compiler_params=pltpu.CompilerParams(vmem_limit_bytes=32 * 1024 * 1024),
    )(flags, *args)


def on_device(
    adjoint_field,
    east_courant,
    north_courant,
    pole_courant,
    mix_fraction,
    detrain_share,
    sounding_owner,
    sounding_cell,
    sounding_count,
    sounding_forcing,
):
    lon_count, lat_count = lax.axis_size("lon"), lax.axis_size("lat")
    lon, lat, lev = lax.axis_index("lon"), lax.axis_index("lat"), lax.axis_index("lev")
    tracers, levels, rows, lanes = adjoint_field.shape
    steps, slot_count = sounding_cell.shape
    slabs = tracers * levels
    base = slabs + tracers + 1
    per = lanes // rows
    size = (tracers, levels, rows)

    top, bottom = lat == lat_count - 1, lat == 0
    partner = (lon + lon_count // 2) % lon_count
    flags = [
        top,
        bottom,
        lon < lon_count // 2,
        lev % 2,
        lon * lat_count + lat,
        jnp.where(top, partner * lat_count + lat, lon * lat_count + lat + 1),
        jnp.where(bottom, partner * lat_count + lat, lon * lat_count + lat - 1),
        (lon + 1) % lon_count * lat_count + lat,
        (lon + lon_count - 1) % lon_count * lat_count + lat,
        jnp.where(top, rows - 1, 0),
        jnp.where(bottom, 0, rows - 1),
    ]
    flags = jnp.stack([jnp.asarray(flag, jnp.int32) for flag in flags])

    live = jnp.arange(slot_count, dtype=jnp.int32)[None, :] < sounding_count
    values = jnp.where(live[:, None, :], sounding_forcing, 0.0)
    places = jnp.stack([sounding_owner[:, :, 0], sounding_cell], axis=1).astype(F32)
    slots = jnp.concatenate([values, places], axis=1).reshape(steps * (levels + 2), slot_count)
    slots = jnp.pad(slots, ((0, up8(slots.shape[0]) - slots.shape[0]), (0, 0)))

    ring_rows = up8(base + 3 * levels)
    column_rows = up8(2 * (-(-base // per) + 3))
    first_rows = tracers // 2 * rows + rows // 2
    keep, send, forward, back, columns = call(
        functools.partial(first_kernel, *size),
        flags,
        [adjoint_field, detrain_share, mix_fraction, east_courant, north_courant, pole_courant],
        [(first_rows, lanes)] * 2 + [(ring_rows, lanes)] * 2 + [(column_rows, lanes)],
        [(2, first_rows, lanes), (2, ring_rows, lanes)],
    )
    forward, back = exchange_rows(forward, back)
    eastern, western = exchange_columns(columns)
    first = keep + swap_over(send, "lev", 1)
    slots = gather_blocks(slots)

    lon_rows = 2 * (-(-base // per) - slabs // per)
    second_rows = tracers // 2 * rows + 5 * (rows // 2) + up8(lon_rows + tracers + 1)
    keep, send, coefs, edges, turned = call(
        functools.partial(second_kernel, *size),
        flags,
        [
            adjoint_field, detrain_share, mix_fraction, east_courant, north_courant, pole_courant,
            forward, back, eastern, western,
        ],
        [(second_rows, lanes)] * 2 + [(5, levels, rows, lanes), (2, ring_rows, lanes), (lanes, lanes)],
        [(2, second_rows, lanes)],
    )
    second = keep + swap_over(send, "lev", 1)
    first = first + swap_over(first, "lev", 2)

    grids, edge_rows, sums = call(
        lambda *refs: forcing_kernel(levels, rows, steps, *refs[:7], base, *refs[7:]),
        flags,
        [slots, detrain_share, mix_fraction, coefs, edges, turned],
        [(3 * levels, rows, lanes), (8, lanes), (2 * rows + 8, lanes)],
    )
    second = jnp.concatenate([second, sums], axis=0)
    second = second + swap_over(second, "lev", 2)
    other_first = swap_over(first, "lev", 1)
    other_second = swap_over(second, "lev", 1)

    slab_rows = up8(slabs)
    mixed, forward, back, columns = call(
        functools.partial(third_kernel, *size),
        flags,
        [
            adjoint_field, mix_fraction, coefs, edges, turned, grids, edge_rows,
            first, other_first, second, other_second,
        ],
        [adjoint_field.shape] + [(slab_rows, lanes)] * 2 + [(up8(2 * (slabs // per)), lanes)],
        [(2, first_rows, lanes), (2, second_rows, lanes), (2, slab_rows, lanes)],
    )
    forward, back = exchange_rows(forward, back)
    eastern, western = exchange_columns(columns)
    (out,) = call(
        functools.partial(last_kernel, *size),
        flags,
        [mixed, coefs, forward, back, eastern, western],
        [adjoint_field.shape],
    )
    return out


def solution(mesh):
    return jax.shard_map(
        on_device,
        mesh=mesh,
        in_specs=(
            P(None, "lev", "lat", "lon"),
            P("lev", "lat", "lon"),
            P("lev", "lat", "lon"),
            P("lev", "lon"),
            P("lev", "lat", "lon"),
            P("lev", "lat", "lon"),
            P(None, ("lon", "lat"), None),
            P(None, ("lon", "lat")),
            P(None, ("lon", "lat")),
            P(None, "lev", ("lon", "lat")),
        ),
        out_specs=P(None, "lev", "lat", "lon"),
        check_vma=False,
    )
```

```python
import functools

import jax
import jax.numpy as jnp
from jax import lax
from jax.experimental import pallas as pl
from jax.experimental.pallas import tpu as pltpu
from jax.sharding import PartitionSpec as P

F32 = jnp.float32
WEIGHTS = [0, 0, 0, 20, 20]
LANES = 128
TOP, BOTTOM, ASCENDING, PARITY, SELF, NORTH, SOUTH, EAST, WEST, NORTH_ROW, SOUTH_ROW = range(11)


def swap_over(value, axis, bit):
    return lax.ppermute(value, axis, [(i, i ^ bit) for i in range(lax.axis_size(axis))])


def shift_over(value, axis, steps):
    count = lax.axis_size(axis)
    return lax.ppermute(value, axis, [(i, (i + steps) % count) for i in range(count)])


def meridian_rings(lon_count, lat_count, steps):
    pairs = []
    for lon in range(lon_count // 2):
        ring = [lon * lat_count + lat for lat in range(lat_count)]
        ring += [(lon + lon_count // 2) * lat_count + lat for lat in reversed(range(lat_count))]
        pairs += [(ring[i], ring[(i + steps) % len(ring)]) for i in range(len(ring))]
    return pairs


def exchange_rows(forward, back):
    lon_count, lat_count = lax.axis_size("lon"), lax.axis_size("lat")
    return (
        lax.ppermute(forward, ("lon", "lat"), meridian_rings(lon_count, lat_count, 1)),
        lax.ppermute(back, ("lon", "lat"), meridian_rings(lon_count, lat_count, -1)),
    )


def exchange_columns(columns):
    if lax.axis_size("lon") == 2:
        other = swap_over(columns, "lon", 1)
        return other, other
    return shift_over(columns, "lon", -1), shift_over(columns, "lon", 1)


def pair_kernel(a, b, *refs):
    refs[-1][0] = a[...]
    refs[-1][1] = b[...]


def pair(a, b, *after):
    vmem = pl.BlockSpec(memory_space=pltpu.VMEM)
    return pl.pallas_call(
        pair_kernel,
        out_shape=jax.ShapeDtypeStruct((2, *a.shape), a.dtype),
        in_specs=[vmem, vmem] + [pl.BlockSpec(memory_space=pl.ANY)] * len(after),
        out_specs=vmem,
        compiler_params=pltpu.CompilerParams(vmem_limit_bytes=4 * 1024 * 1024),
    )(a, b, *after)


def gather_blocks(blocks, axis):
    count = lax.axis_size(axis)
    if count not in (2, 4):
        return lax.all_gather(blocks, axis, axis=0, tiled=True)
    return jnp.concatenate([blocks] + [swap_over(blocks, axis, bit) for bit in range(1, count)], axis=0)


def add_kernel(waited, a, b, *refs):
    refs[-1][...] = a[...] + b[...]


def add(a, b, *after):
    vmem = pl.BlockSpec(memory_space=pltpu.VMEM)
    return pl.pallas_call(
        functools.partial(add_kernel, len(after)),
        out_shape=jax.ShapeDtypeStruct(a.shape, a.dtype),
        in_specs=[vmem, vmem] + [pl.BlockSpec(memory_space=pl.ANY)] * len(after),
        out_specs=vmem,
        compiler_params=pltpu.CompilerParams(vmem_limit_bytes=4 * 1024 * 1024),
    )(a, b, *after)


def lane_and_row(rows):
    return (
        lax.broadcasted_iota(jnp.int32, (rows, LANES), 1),
        lax.broadcasted_iota(jnp.int32, (rows, LANES), 0),
    )


def shifted(x, side, north, south):
    rows = x.shape[0]
    lane, row = lane_and_row(rows)
    east = jnp.where(lane == LANES - 1, side, pltpu.roll(x, LANES - 1, 1))
    west = jnp.where(lane == 0, side, pltpu.roll(x, 1, 1))
    above = jnp.where(row == rows - 1, north, pltpu.roll(x, rows - 1, 0))
    below = jnp.where(row == 0, south, pltpu.roll(x, 1, 0))
    return east, west, above, below


def turned_round(x):
    rows = x.shape[0]
    return pltpu.roll(x, LANES - 1, 1), pltpu.roll(x, 1, 1), pltpu.roll(x, rows - 1, 0), pltpu.roll(x, 1, 0)


def stencil(coefs, x, side, north, south):
    east, west, above, below = shifted(x, side, north, south)
    own, to_east, to_west, to_north, to_south = coefs
    return own * x + to_east * east + to_west * west + to_north * above + to_south * below


class Columns:
    def __init__(self, rows):
        self.rows = rows
        self.per = LANES // rows
        self.blocks = [jnp.zeros((rows, LANES), F32)] * self.per
        self.lane = lane_and_row(rows)[0]

    def put(self, index, slab):
        group, place = divmod(index, self.per)
        turned = pltpu.roll(slab, 2 * group + 1, 1)
        self.blocks[place] = jnp.where(self.lane // 2 == group, turned, self.blocks[place])

    def get(self, rows):
        return jnp.transpose(jnp.concatenate(self.blocks, axis=0))[:rows]


def sides_of(eastern, western):
    rows = eastern.shape[0]
    row = lane_and_row(rows)[1]
    return jnp.where(row % 2 == 0, pltpu.roll(eastern, rows - 1, 0), pltpu.roll(western, 1, 0))


def turn(rows):
    pad = jnp.zeros((LANES - rows.shape[0], LANES), F32)
    return jnp.transpose(jnp.concatenate([rows, pad], axis=0))


def side_of(turned, index, rows):
    group, place = divmod(index, LANES // rows)
    return pltpu.roll(turned[place * rows : (place + 1) * rows], (LANES - 2 * group - 1) % LANES, 1)


def tiled(x, rows, block=0):
    if block:
        x = pltpu.roll(x, LANES - block * rows, 1)
    x = jnp.where(lax.broadcasted_iota(jnp.int32, x.shape, 1) < rows, x, 0.0)
    width = rows
    while width < LANES:
        x = x + pltpu.roll(x, width, 1)
        width *= 2
    return x


def first_kernel(
    tracers, levels, rows, flags, counts, owners_in, cells_in, forcing_in, field_in, detrain_in, mix_in, east_in, north_in,
    pole_in, keep_first, send_first, keep_second, send_second, slots, field, detrain, mix, east, north, pole,
    first, second, owners, cells, forcing, sems,
):
    pairs = [(detrain_in, detrain), (mix_in, mix), (east_in, east), (north_in, north)]
    pairs += [(owners_in, owners), (cells_in, cells), (forcing_in, forcing), (pole_in, pole)]
    pairs += [(field_in.at[t], field.at[t]) for t in range(tracers)]
    copies = [pltpu.make_async_copy(source, target, sems.at[i]) for i, (source, target) in enumerate(pairs)]
    for copy in copies:
        copy.start()
    static, loads = copies[:8], copies[8:]
    half = tracers // 2
    for copy in static:
        copy.wait()
    slots[...] = jnp.zeros(slots.shape, F32)
    steps, slot_count = cells.shape
    slot_rows = slots.shape[0] * LANES // slot_count
    slot = lax.broadcasted_iota(jnp.int32, (levels, LANES), 1)
    for part in range(slot_count // LANES):
        lanes = slice(part * LANES, (part + 1) * LANES)
        for step in range(steps):
            at = part * slot_rows + step * (levels + 2)
            live = slot + part * LANES < counts[step]
            slots[at : at + levels, :] = jnp.where(live, forcing[:, step, lanes], 0.0)
            slots[at + levels : at + levels + 1, :] = owners[step, :, lanes].astype(F32)
            slots[at + levels + 1 : at + levels + 2, :] = cells[step : step + 1, lanes].astype(F32)
    lane, row = lane_and_row(rows)
    weights = [detrain[k] for k in range(levels)]
    stay = [1.0 - mix[k] for k in range(levels)]
    inside, spread = [], None
    for k in range(levels):
        to_east = jnp.maximum(east[k], 0.0)
        to_west = jnp.where(lane == 0, 0.0, jnp.maximum(-pltpu.roll(east[k], 1, 1), 0.0))
        to_north = jnp.maximum(north[k], 0.0)
        to_south = jnp.where(row == 0, 0.0, jnp.maximum(-pltpu.roll(north[k], 1, 0), 0.0))
        own = 1.0 - to_east - to_west - to_north - to_south
        five = [
            own,
            jnp.where(lane == LANES - 1, 0.0, to_east),
            to_west,
            jnp.where(row == rows - 1, 0.0, to_north),
            to_south,
        ]
        inside.append([weights[k] * c for c in five])
        terms = [c * s for c, s in zip(inside[k], (mix[k],) + turned_round(mix[k]))]
        spread = terms if spread is None else [p + q for p, q in zip(spread, terms)]
    start = half * rows
    for i in range(5):
        for h in range(2):
            at = start + i * (rows // 2)
            second[h, at : at + rows // 2, :] = spread[i][h * rows // 2 : (h + 1) * rows // 2]
    total = functools.reduce(lambda p, q: p + q, weights)
    for h in range(2):
        first[h, start:, :] = total[h * rows // 2 : (h + 1) * rows // 2]
    for t in range(tracers):
        loads[t].wait()
        partial = later = None
        for k in range(levels):
            slab = field[t, k]
            term = weights[k] * slab
            partial = term if partial is None else partial + term
            slab = stay[k] * slab
            for c, x in zip(inside[k], (slab,) + turned_round(slab)):
                later = c * x if later is None else later + c * x
        at = (t % half) * rows
        first[t // half, at : at + rows, :] = partial
        second[t // half, at : at + rows, :] = later
    parity = flags[PARITY]
    keep_first[...] = first[parity]
    send_first[...] = first[1 - parity]
    keep_second[...] = second[parity]
    send_second[...] = second[1 - parity]


def edge_kernel(
    tracers, levels, rows, flags, slots, field, kept, detrain, mix, east, north, pole, forward, back, columns, ring
):
    slabs = tracers * levels
    base = slabs + tracers + 1
    per = LANES // rows
    group = -(-base // per)
    column_rows = up8(2 * (group + 3))
    columns[column_rows:] = slots[...]
    ring[...] = jnp.zeros(ring.shape, F32)
    weights = [detrain[k] for k in range(levels)]
    cols = Columns(rows)

    def edge_rows(place, slab):
        ring[0, place : place + 1, :] = slab[rows - 1 : rows]
        ring[1, place : place + 1, :] = slab[:1]

    total = functools.reduce(lambda p, q: p + q, weights)
    cols.put(slabs + tracers, total)
    edge_rows(slabs + tracers, total)
    for k in range(levels):
        edge_rows(base + k, mix[k])
        edge_rows(base + levels + k, detrain[k])
        ring[0, base + 2 * levels + k : base + 2 * levels + k + 1, :] = north[k, rows - 1 : rows, :]
        ring[1, base + 2 * levels + k : base + 2 * levels + k + 1, :] = pole[k : k + 1, :]
        cols.put(group * per + k, mix[k])
        cols.put((group + 1) * per + k, detrain[k])
        cols.put((group + 2) * per + k, east[k])
    for t in range(tracers):
        partial = None
        for k in range(levels):
            term = weights[k] * field[t, k]
            partial = term if partial is None else partial + term
            slab = kept[t, k]
            cols.put(k * tracers + t, slab)
            edge_rows(k * tracers + t, slab)
        cols.put(slabs + t, partial)
        edge_rows(slabs + t, partial)
    ascending = flags[ASCENDING]
    forward[...] = ring[1 - ascending]
    back[...] = ring[ascending]
    columns[:column_rows] = cols.get(column_rows)


def second_kernel(
    tracers, levels, rows, flags, first, second, detrain, mix, east, north, pole,
    own_forward, own_back, own_columns, forward, back, eastern, western,
    late, coefs, edges, turned,
):
    slabs = tracers * levels
    base = slabs + tracers + 1
    per = LANES // rows
    group = -(-base // per)
    ascending = flags[ASCENDING] == 1
    from_north = jnp.where(ascending, back[...], forward[...])
    from_south = jnp.where(ascending, forward[...], back[...])
    own_north = jnp.where(ascending, own_forward[...], own_back[...])
    own_south = jnp.where(ascending, own_back[...], own_forward[...])
    edges[0] = from_north
    edges[1] = from_south
    sides = sides_of(eastern[...], western[...])
    mine = own_columns[...]
    around = turn(sides)
    turned[...] = around
    lane, row = lane_and_row(rows)
    top, bottom = flags[TOP] == 1, flags[BOTTOM] == 1
    is_top = jnp.logical_and(row == rows - 1, top)
    is_bottom = jnp.logical_and(row == 0, bottom)
    west_row = lane_and_row(2)[1] == 1
    groups = tracers // per
    zero = jnp.zeros((1, LANES), F32)
    add_north = add_south = spread_north = spread_south = less_north = less_south = 0.0
    add_sides = [0.0] * groups
    spread_sides = less_sides = 0.0
    for k in range(levels):
        place = base + 2 * levels + k
        wind = east[k]
        behind = jnp.where(lane == 0, side_of(around, (group + 2) * per + k, rows), pltpu.roll(wind, 1, 1))
        to_east = jnp.maximum(wind, 0.0)
        to_west = jnp.maximum(-behind, 0.0)
        wind = north[k]
        pole_north = jnp.where(top, jnp.maximum(-from_north[place : place + 1], 0.0), zero)
        to_north = jnp.maximum(wind, 0.0) + jnp.where(is_top, pole_north, 0.0)
        below = from_south[place : place + 1]
        pole_south = jnp.maximum(pole[k : k + 1, :], 0.0) + jnp.maximum(-below, 0.0)
        behind = jnp.where(row == 0, below, pltpu.roll(wind, 1, 0))
        to_south = jnp.where(is_bottom, pole_south, jnp.maximum(-behind, 0.0))
        for i, c in enumerate([1.0 - to_east - to_west - to_north - to_south, to_east, to_west, to_north, to_south]):
            coefs[i, k] = c

        level = slice(k * tracers, (k + 1) * tracers)
        weight = detrain[k, rows - 1 : rows, :]
        taken, given = weight * to_north[rows - 1 : rows], weight * pole_north
        add_north = add_north + taken * from_north[level] - given * own_north[level]
        spread_north = spread_north + taken * from_north[base + k : base + k + 1]
        less_north = less_north - given * mix[k, rows - 1 : rows, :]
        taken = detrain[k, :1, :] * to_south[:1]
        add_south = add_south + taken * (from_south[level] - own_south[level])
        spread_south = spread_south + taken * from_south[base + k : base + k + 1]
        less_south = less_south - taken * mix[k, :1, :]

        winds = slice(2 * (group + 2), 2 * (group + 3))
        shares = slice(2 * group, 2 * (group + 1))
        weight = tiled(mine[2 * (group + 1) : 2 * (group + 2)], rows, k)
        wind = jnp.where(west_row, jnp.maximum(-sides[winds], 0.0), jnp.maximum(mine[winds], 0.0))
        taken = weight * tiled(wind, rows, k)
        given = jnp.where(west_row, taken, 0.0)
        for g in range(groups):
            pair = slice(2 * (k * groups + g), 2 * (k * groups + g + 1))
            add_sides[g] = add_sides[g] + taken * sides[pair] - given * mine[pair]
        spread_sides = spread_sides + taken * tiled(sides[shares], rows, k)
        less_sides = less_sides - given * tiled(mine[shares], rows, k)
    parts = [sides[2 * (slabs // per) : 2 * group]] + add_sides
    parts += [spread_sides, less_sides, spread_north, spread_south, less_north, less_south]
    parts += [add_north, add_south, from_north[slabs : slabs + tracers + 1], from_south[slabs : slabs + tracers + 1]]
    at = 0
    for part in parts:
        late[at : at + part.shape[0]] = part
        at += part.shape[0]
    if at < late.shape[0]:
        late[at:] = jnp.zeros((late.shape[0] - at, LANES), F32)


def pieces(x):
    high = x.astype(jnp.bfloat16)
    rest = x - high.astype(F32)
    middle = rest.astype(jnp.bfloat16)
    low = (rest - middle.astype(F32)).astype(jnp.bfloat16)
    return [high, middle, low]


def product(a, b):
    return lax.dot_general(a, b, (((1,), (1,)), ((), ())), preferred_element_type=F32)


def forcing_kernel(levels, rows, steps, flags, slots, detrain, mix, coefs, edges, turned, base, grids, edge_rows, sums):
    parts = min(8, slots.shape[0])
    count = parts * LANES
    per = LANES // rows
    row_ids = lax.broadcasted_iota(jnp.int32, (rows, count), 0)
    lane_ids = lax.broadcasted_iota(jnp.int32, (LANES, count), 0)
    group = -(-base // per)

    def add_block(index, carry):
        late, early, ring_sides = carry
        block = jnp.concatenate([slots[parts * index + part] for part in range(parts)], axis=1)
        results = []
        for step in range(steps):
            first = step * (levels + 2)
            values = [block[first + k : first + k + 1] for k in range(levels)]
            owner = block[first + levels : first + levels + 1].astype(jnp.int32)
            cell = block[first + levels + 1 : first + levels + 2].astype(jnp.int32)
            slot_row, slot_lane = cell // LANES, cell % LANES
            lanes = (lane_ids == slot_lane).astype(F32).astype(jnp.bfloat16)
            here = jnp.logical_and(row_ids == slot_row, owner == flags[SELF])
            left = [jnp.where(here, value, 0.0) for value in values]
            if step == steps - 1:
                in_north = jnp.logical_and(owner == flags[NORTH], slot_row == flags[NORTH_ROW])
                in_south = jnp.logical_and(owner == flags[SOUTH], slot_row == flags[SOUTH_ROW])
                left += [jnp.where(in_north, value, 0.0) for value in values]
                left += [jnp.where(in_south, value, 0.0) for value in values]
                left += [jnp.zeros((8 - 2 * levels, count), F32)]
            left = jnp.concatenate(left, axis=0)
            results.append(sum(product(piece, lanes) for piece in pieces(left)))
            if step == steps - 1:
                in_east = jnp.logical_and(owner == flags[EAST], slot_lane == 0)
                in_west = jnp.logical_and(owner == flags[WEST], slot_lane == LANES - 1)
                right = [jnp.where(in_east, value, 0.0) for value in values]
                right += [jnp.where(in_west, value, 0.0) for value in values]
                right += [jnp.zeros((8 - 2 * levels, count), F32)]
                right = jnp.concatenate(right, axis=0)
                at_row = (row_ids == slot_row).astype(F32).astype(jnp.bfloat16)
                ring_sides = ring_sides + sum(product(at_row, piece) for piece in pieces(right))
        return late + results[1], early + results[0], ring_sides

    late, early, ring_sides = lax.fori_loop(
        0,
        slots.shape[0] // parts,
        add_block,
        (
            jnp.zeros((levels * rows + 8, LANES), F32),
            jnp.zeros((levels * rows, LANES), F32),
            jnp.zeros((rows, 8), F32),
        ),
    )
    lane, _ = lane_and_row(rows)
    north_rows = late[levels * rows : levels * rows + levels]
    south_rows = late[levels * rows + levels : levels * rows + 2 * levels]
    edge_rows[...] = late[levels * rows :]
    around = turned[...]
    at_end = at_first = None
    ring = jnp.zeros((rows, LANES), F32)
    ring_north = jnp.zeros((1, LANES), F32)
    ring_south = jnp.zeros((1, LANES), F32)
    for k in range(levels):
        own = late[k * rows : (k + 1) * rows]
        now = early[k * rows : (k + 1) * rows]
        east_side = jnp.broadcast_to(ring_sides[:, k : k + 1], (rows, LANES))
        west_side = jnp.broadcast_to(ring_sides[:, levels + k : levels + k + 1], (rows, LANES))
        side = jnp.where(lane == LANES - 1, east_side, jnp.where(lane == 0, west_side, 0.0))
        grids[k] = own
        grids[levels + k] = now
        grids[2 * levels + k] = side
        mix_side = side_of(around, group * per + k, rows)
        detrain_side = side_of(around, (group + 1) * per + k, rows)
        north, south = north_rows[k : k + 1], south_rows[k : k + 1]
        moved = stencil(
            [coefs[i, k] for i in range(5)],
            (1.0 - mix[k]) * own,
            (1.0 - mix_side) * side,
            (1.0 - edges[0, base + k : base + k + 1, :]) * north,
            (1.0 - edges[1, base + k : base + k + 1, :]) * south,
        )
        first = detrain[k] * own
        second = detrain[k] * (moved + now)
        at_first = first if at_first is None else at_first + first
        at_end = second if at_end is None else at_end + second
        ring = ring + detrain_side * side
        place = base + levels + k
        ring_north = ring_north + edges[0, place : place + 1, :] * north
        ring_south = ring_south + edges[1, place : place + 1, :] * south
    sums[:rows] = at_first
    sums[rows : 2 * rows] = at_end
    flat = jnp.transpose(jnp.concatenate([ring] + [jnp.zeros((rows, LANES), F32)] * (per - 1), axis=0))
    sums[2 * rows :] = jnp.concatenate(
        [ring_north, ring_south, flat[LANES - 1 :], flat[:1], jnp.zeros((4, LANES), F32)], axis=0
    )


def third_kernel(
    tracers, levels, rows, flags, field, mix, coefs, edges, turned, mine, other, moved_out, column_out, inverse_out, first,
):
    half = tracers // 2
    parity = flags[PARITY]
    first[parity] = mine[...]
    first[1 - parity] = other[...]
    total = jnp.concatenate([first[0, half * rows :, :], first[1, half * rows :, :]], axis=0)
    inverse = 1.0 / total
    inverse_out[...] = inverse
    around = turned[...]
    stay = [1.0 - mix[k] for k in range(levels)]
    five = [[coefs[i, k] for i in range(5)] for k in range(levels)]
    for t in range(tracers):
        column = first[t // half, (t % half) * rows : (t % half + 1) * rows, :] * inverse
        column_out[t] = column
        for k in range(levels):
            place = k * tracers + t
            moved = stencil(
                five[k],
                stay[k] * field[t, k] + mix[k] * column,
                side_of(around, place, rows),
                edges[0, place : place + 1, :],
                edges[1, place : place + 1, :],
            )
            moved_out[t, k] = stay[k] * moved


def fourth_kernel(
    tracers, levels, rows, flags, moved, column, inverse_in, mix, coefs, edges, turned, grids, edge_rows,
    mine, other, forced_1, forced_2, forced_3, forced_4, mixed_out, forward, back, columns, second, ring,
):
    half = tracers // 2
    slabs = tracers * levels
    base = slabs + tracers + 1
    per = LANES // rows
    group = -(-base // per)
    groups = tracers // per
    parity = flags[PARITY]
    second_rows = second.shape[1]
    second[parity] = mine[:second_rows]
    second[1 - parity] = other[:second_rows]
    late = mine[second_rows:] + other[second_rows:]
    forced = (forced_1[...] + forced_2[...]) + (forced_3[...] + forced_4[...])
    inverse = inverse_in[...]
    lane, row = lane_and_row(rows)
    at_side = jnp.logical_or(lane == 0, lane == LANES - 1)
    last, initial = row == rows - 1, row == 0

    at = 2 * (group - slabs // per)
    inverse_side = 1.0 / tiled(late[2 * groups : 2 * groups + 2], rows)
    forced_sides = tiled(forced[2 * rows + 2 : 2 * rows + 4], rows)
    side_rows = [(late[2 * g : 2 * g + 2] + forced_sides) * inverse_side for g in range(groups)]
    side_rows += [late[at : at + 2 * groups + 4]]
    at += 2 * groups + 4
    around_late = turn(jnp.concatenate(side_rows, axis=0))
    spread_side = side_of(around_late, 2 * groups * per, rows)
    less_side = side_of(around_late, (2 * groups + 1) * per, rows)
    north, south, less_north, less_south = [late[at + i : at + i + 1] for i in range(4)]
    at += 4
    add_ends = [late[at + e * tracers : at + (e + 1) * tracers] for e in range(2)]
    at += 2 * tracers
    column_ends = []
    for e in range(2):
        sums = late[at : at + tracers + 1]
        column_ends.append((sums[:tracers] + forced[2 * rows + e : 2 * rows + e + 1]) / sums[tracers:])
        at += tracers + 1

    spread = []
    start = half * rows
    for i in range(5):
        at = start + i * (rows // 2)
        spread.append(jnp.concatenate([second[h, at : at + rows // 2, :] for h in range(2)], axis=0))
    spread[0] = spread[0] + jnp.where(last, less_north, 0.0) + jnp.where(initial, less_south, 0.0)
    spread[0] = spread[0] + jnp.where(lane == 0, less_side, 0.0)
    spread[1] = jnp.where(lane == LANES - 1, spread_side, spread[1])
    spread[2] = spread[2] + jnp.where(lane == 0, spread_side, 0.0)
    spread[3] = jnp.where(last, north, spread[3])
    spread[4] = spread[4] + jnp.where(initial, south, 0.0)

    forced_column = forced[:rows] * inverse
    forced_later = forced[rows : 2 * rows]
    around = turned[...]
    stay = [1.0 - mix[k] for k in range(levels)]
    forced_moved, to_sides, to_ends = [], [], []
    for k in range(levels):
        five = [coefs[i, k] for i in range(5)]
        mix_side = side_of(around, group * per + k, rows)
        shares = [edges[e, base + k : base + k + 1, :] for e in range(2)]
        ends = [(1.0 - shares[e]) * edge_rows[e * levels + k : e * levels + k + 1, :] for e in range(2)]
        moved_forcing = stencil(
            five,
            stay[k] * grids[k] + mix[k] * forced_column,
            (1.0 - mix_side) * grids[2 * levels + k],
            ends[0],
            ends[1],
        )
        forced_moved.append(stay[k] * (moved_forcing + grids[levels + k]))
        to_side = jnp.where(lane == LANES - 1, five[1], jnp.where(lane == 0, five[2], 0.0))
        to_sides.append(stay[k] * to_side * mix_side)
        to_ends.append(
            [
                jnp.where(last, stay[k] * five[3] * shares[0], 0.0)[rows - 8 :],
                jnp.where(initial, stay[k] * five[4] * shares[1], 0.0)[:8],
            ]
        )

    cols = Columns(rows)
    ring[...] = jnp.zeros(ring.shape, F32)
    for t in range(tracers):
        h, at = t // half, (t % half) * rows
        column_side = side_of(around_late, t, rows)
        column_north, column_south = column_ends[0][t : t + 1], column_ends[1][t : t + 1]
        later = second[h, at : at + rows, :] + forced_later
        later = later + jnp.where(at_side, side_of(around_late, (groups + t // per) * per + t % per, rows), 0.0)
        later = later + jnp.where(last, add_ends[0][t : t + 1], 0.0)
        later = later + jnp.where(initial, add_ends[1][t : t + 1], 0.0)
        later = later + stencil(spread, column[t] + forced_column, column_side, column_north, column_south)
        later = later * inverse
        for k in range(levels):
            place = k * tracers + t
            mixed = moved[t, k] + forced_moved[k] + mix[k] * later + to_sides[k] * column_side
            mixed = jnp.concatenate(
                [
                    mixed[:8] + to_ends[k][1] * column_south,
                    mixed[8 : rows - 8],
                    mixed[rows - 8 :] + to_ends[k][0] * column_north,
                ],
                axis=0,
            )
            mixed_out[t, k] = mixed
            cols.put(place, mixed)
            ring[0, place : place + 1, :] = mixed[rows - 1 : rows]
            ring[1, place : place + 1, :] = mixed[:1]
    ascending = flags[ASCENDING]
    forward[...] = ring[1 - ascending]
    back[...] = ring[ascending]
    columns[...] = cols.get(columns.shape[0])


def inner_kernel(tracers, levels, rows, flags, mixed, coefs, out):
    lane, row = lane_and_row(rows)
    for k in range(levels):
        own, to_east, to_west, to_north, to_south = [coefs[i, k] for i in range(5)]
        five = [
            own,
            jnp.where(lane == LANES - 1, 0.0, to_east),
            jnp.where(lane == 0, 0.0, to_west),
            jnp.where(row == rows - 1, 0.0, to_north),
            jnp.where(row == 0, 0.0, to_south),
        ]
        for t in range(tracers):
            slab = mixed[t, k]
            total = None
            for c, x in zip(five, (slab,) + turned_round(slab)):
                total = c * x if total is None else total + c * x
            out[t, k] = total


def last_kernel(tracers, levels, rows, flags, inner, coefs, forward, back, eastern, western, out, result, sems):
    ascending = flags[ASCENDING] == 1
    from_north = jnp.where(ascending, back[...], forward[...])
    from_south = jnp.where(ascending, forward[...], back[...])
    around = turn(sides_of(eastern[...], western[...]))
    lane, row = lane_and_row(rows)
    last, initial = row == rows - 1, row == 0
    to_sides = [
        jnp.where(lane == LANES - 1, coefs[1, k], jnp.where(lane == 0, coefs[2, k], 0.0)) for k in range(levels)
    ]
    to_north = [jnp.where(last, coefs[3, k], 0.0) for k in range(levels)]
    to_south = [jnp.where(initial, coefs[4, k], 0.0) for k in range(levels)]
    copies = []
    for t in range(tracers):
        for k in range(levels):
            place = k * tracers + t
            total = inner[t, k] + to_sides[k] * side_of(around, place, rows)
            total = total + to_north[k] * from_north[place : place + 1]
            result[t, k] = total + to_south[k] * from_south[place : place + 1]
        copy = pltpu.make_async_copy(result.at[t], out.at[t], sems.at[t])
        copy.start()
        copies.append(copy)
    for copy in copies:
        copy.wait()


def up8(count):
    return -(-count // 8) * 8


def call(kernel, scalars, args, outs, scratch=(), placed=(), copies=0, placed_out=False, weight=0):
    vmem, free = pl.BlockSpec(memory_space=pltpu.VMEM), pl.BlockSpec(memory_space=pl.ANY)
    return pl.pallas_call(
        kernel,
        out_shape=[jax.ShapeDtypeStruct(shape, F32) for shape in outs],
        in_specs=[pl.BlockSpec(memory_space=pltpu.SMEM)] * len(scalars) + [free] * len(placed) + [vmem] * len(args),
        out_specs=[free if placed_out else vmem] * len(outs),
        scratch_shapes=[pltpu.VMEM(x.shape, x.dtype) if hasattr(x, "dtype") else pltpu.VMEM(x, F32) for x in scratch]
        + ([pltpu.SemaphoreType.DMA((copies,))] if copies else []),
        compiler_params=pltpu.CompilerParams(vmem_limit_bytes=16 * 1024 * 1024),
        cost_estimate=pl.CostEstimate(flops=int(weight * 1e9), bytes_accessed=0, transcendentals=0),
    )(*scalars, *placed, *args)


def on_device(
    adjoint_field,
    east_courant,
    north_courant,
    pole_courant,
    mix_fraction,
    detrain_share,
    sounding_owner,
    sounding_cell,
    sounding_count,
    sounding_forcing,
):
    lon_count, lat_count = lax.axis_size("lon"), lax.axis_size("lat")
    lon, lat, lev = lax.axis_index("lon"), lax.axis_index("lat"), lax.axis_index("lev")
    tracers, levels, rows, lanes = adjoint_field.shape
    steps, slot_count = sounding_cell.shape
    slabs = tracers * levels
    base = slabs + tracers + 1
    per = lanes // rows
    size = (tracers, levels, rows)

    top, bottom = lat == lat_count - 1, lat == 0
    partner = (lon + lon_count // 2) % lon_count
    flags = [
        top,
        bottom,
        lon < lon_count // 2,
        (lev ^ (lev >> 1)) & 1,
        lon * lat_count + lat,
        jnp.where(top, partner * lat_count + lat, lon * lat_count + lat + 1),
        jnp.where(bottom, partner * lat_count + lat, lon * lat_count + lat - 1),
        (lon + 1) % lon_count * lat_count + lat,
        (lon + lon_count - 1) % lon_count * lat_count + lat,
        jnp.where(top, rows - 1, 0),
        jnp.where(bottom, 0, rows - 1),
    ]
    flags = jnp.stack([jnp.asarray(flag, jnp.int32) for flag in flags])

    ring_rows = up8(base + 3 * levels)
    column_rows = up8(2 * (-(-base // per) + 3))
    slot_rows = up8(steps * (levels + 2))
    first_rows = tracers // 2 * rows + rows // 2
    second_rows = tracers // 2 * rows + 5 * (rows // 2)
    soundings = [jnp.swapaxes(sounding_owner, 1, 2), sounding_cell, jnp.swapaxes(sounding_forcing, 0, 1)]
    static = [detrain_share, mix_fraction, east_courant, north_courant, pole_courant]
    keep_first, send_first, keep_second, send_second, slots, field, *static = call(
        functools.partial(first_kernel, *size),
        [flags, sounding_count[:, 0]],
        [],
        [(first_rows, lanes)] * 2
        + [(second_rows, lanes)] * 2
        + [(slot_count // lanes * slot_rows, lanes)]
        + [x.shape for x in [adjoint_field] + static],
        [(2, first_rows, lanes), (2, second_rows, lanes)] + soundings,
        [pltpu.with_memory_space_constraint(x, pltpu.HBM) for x in soundings + [adjoint_field] + static],
        tracers + len(soundings) + len(static),
        weight=WEIGHTS[0],
    )
    detrain, mix = static[:2]
    kept = (1.0 - mix)[None] * field
    own_forward, own_back, columns = call(
        functools.partial(edge_kernel, *size),
        [flags],
        [slots, field, kept] + static,
        [(ring_rows, lanes)] * 2 + [(column_rows + slots.shape[0], lanes)],
        [(2, ring_rows, lanes)],
        weight=WEIGHTS[1],
    )
    first = add(keep_first, swap_over(send_first, "lev", 1))
    second = add(keep_second, swap_over(send_second, "lev", 1))
    eastern, western = exchange_columns(columns)
    forward, back = exchange_rows(own_forward, own_back)
    other_first = swap_over(first, "lev", 3)

    late_rows = 2 * (-(-base // per) - slabs // per) + 2 * (tracers // per) + 8 + 4 * tracers + 2
    late, coefs, edges, turned = call(
        functools.partial(second_kernel, *size),
        [flags],
        static
        + [own_forward, own_back, columns[:column_rows]]
        + [forward, back, eastern[:column_rows], western[:column_rows]],
        [(up8(late_rows), lanes), (5, levels, rows, lanes), (2, ring_rows, lanes), (lanes, lanes)],
        placed=[first, second],
        weight=WEIGHTS[2],
    )
    second = jnp.concatenate([second, late], axis=0)
    other_second = swap_over(second, "lev", 3)
    slots = columns[column_rows:][None]
    if lon_count == 2:
        slots = pair(columns[column_rows:], eastern[column_rows:], first)
    else:
        slots = gather_blocks(slots, "lon")
    slots = gather_blocks(slots, "lat").reshape(-1, slot_rows, lanes)
    grids, edge_rows, sums = call(
        lambda *refs: forcing_kernel(levels, rows, steps, *refs[:7], base, *refs[7:]),
        [flags],
        [slots, detrain, mix, coefs, edges, turned],
        [(3 * levels, rows, lanes), (8, lanes), (2 * rows + 8, lanes)],
        weight=WEIGHTS[3],
    )
    sums = [sums] + [swap_over(sums, "lev", bit) for bit in (1, 2, 3)]
    first = add(first, other_first, sums[0])
    other_first = swap_over(first, "lev", 1)
    second = add(second, other_second, first)
    other_second = swap_over(second, "lev", 1)

    moved, column, inverse = call(
        functools.partial(third_kernel, *size),
        [flags],
        [field, mix, coefs, edges, turned, first, other_first],
        [adjoint_field.shape, (tracers, rows, lanes), (rows, lanes)],
        [(2, first_rows, lanes)],
        weight=WEIGHTS[4],
    )
    slab_rows = up8(slabs)
    mixed, forward, back, columns = call(
        functools.partial(fourth_kernel, *size),
        [flags],
        [
            moved, column, inverse, mix, coefs, edges, turned, grids, edge_rows,
            second, other_second, *sums,
        ],
        [adjoint_field.shape] + [(slab_rows, lanes)] * 2 + [(up8(2 * (slabs // per)), lanes)],
        [(2, second_rows, lanes), (2, slab_rows, lanes)],
    )
    eastern, western = exchange_columns(columns)
    forward, back = exchange_rows(forward, back)
    (inner,) = call(functools.partial(inner_kernel, *size), [flags], [mixed, coefs], [adjoint_field.shape])
    (out,) = call(
        functools.partial(last_kernel, *size),
        [flags],
        [inner, coefs, forward, back, eastern, western],
        [adjoint_field.shape],
        [adjoint_field.shape],
        copies=tracers,
        placed_out=True,
    )
    return out


def solution(mesh):
    return jax.shard_map(
        on_device,
        mesh=mesh,
        in_specs=(
            P(None, "lev", "lat", "lon"),
            P("lev", "lat", "lon"),
            P("lev", "lat", "lon"),
            P("lev", "lon"),
            P("lev", "lat", "lon"),
            P("lev", "lat", "lon"),
            P(None, ("lon", "lat"), None),
            P(None, ("lon", "lat")),
            P(None, ("lon", "lat")),
            P(None, "lev", ("lon", "lat")),
        ),
        out_specs=P(None, "lev", "lat", "lon"),
        check_vma=False,
    )
```

```python
import functools

import jax
import jax.numpy as jnp
from jax import lax
from jax.experimental import pallas as pl
from jax.experimental.pallas import tpu as pltpu
from jax.sharding import PartitionSpec as P

F32 = jnp.float32
WEIGHTS = [0, 0, 0, 20, 20]
LANES = 128
TOP, BOTTOM, ASCENDING, PARITY, SELF, NORTH, SOUTH, EAST, WEST, NORTH_ROW, SOUTH_ROW = range(11)


def swap_over(value, axis, bit):
    return lax.ppermute(value, axis, [(i, i ^ bit) for i in range(lax.axis_size(axis))])


def shift_over(value, axis, steps):
    count = lax.axis_size(axis)
    return lax.ppermute(value, axis, [(i, (i + steps) % count) for i in range(count)])


def meridian_rings(lon_count, lat_count, steps):
    pairs = []
    for lon in range(lon_count // 2):
        ring = [lon * lat_count + lat for lat in range(lat_count)]
        ring += [(lon + lon_count // 2) * lat_count + lat for lat in reversed(range(lat_count))]
        pairs += [(ring[i], ring[(i + steps) % len(ring)]) for i in range(len(ring))]
    return pairs


def exchange_rows(forward, back):
    lon_count, lat_count = lax.axis_size("lon"), lax.axis_size("lat")
    return (
        lax.ppermute(forward, ("lon", "lat"), meridian_rings(lon_count, lat_count, 1)),
        lax.ppermute(back, ("lon", "lat"), meridian_rings(lon_count, lat_count, -1)),
    )


def exchange_columns(columns):
    if lax.axis_size("lon") == 2:
        other = swap_over(columns, "lon", 1)
        return other, other
    return shift_over(columns, "lon", -1), shift_over(columns, "lon", 1)


def pair_kernel(a, b, *refs):
    refs[-1][0] = a[...]
    refs[-1][1] = b[...]


def pair(a, b, *after):
    vmem = pl.BlockSpec(memory_space=pltpu.VMEM)
    return pl.pallas_call(
        pair_kernel,
        out_shape=jax.ShapeDtypeStruct((2, *a.shape), a.dtype),
        in_specs=[vmem, vmem] + [pl.BlockSpec(memory_space=pl.ANY)] * len(after),
        out_specs=vmem,
        compiler_params=pltpu.CompilerParams(vmem_limit_bytes=4 * 1024 * 1024),
    )(a, b, *after)


def gather_blocks(blocks, axis):
    count = lax.axis_size(axis)
    if count not in (2, 4):
        return lax.all_gather(blocks, axis, axis=0, tiled=True)
    return jnp.concatenate([blocks] + [swap_over(blocks, axis, bit) for bit in range(1, count)], axis=0)


def add_kernel(waited, a, b, *refs):
    refs[-1][...] = a[...] + b[...]


def add(a, b, *after):
    vmem = pl.BlockSpec(memory_space=pltpu.VMEM)
    return pl.pallas_call(
        functools.partial(add_kernel, len(after)),
        out_shape=jax.ShapeDtypeStruct(a.shape, a.dtype),
        in_specs=[vmem, vmem] + [pl.BlockSpec(memory_space=pl.ANY)] * len(after),
        out_specs=vmem,
        compiler_params=pltpu.CompilerParams(vmem_limit_bytes=4 * 1024 * 1024),
    )(a, b, *after)


def lane_and_row(rows):
    return (
        lax.broadcasted_iota(jnp.int32, (rows, LANES), 1),
        lax.broadcasted_iota(jnp.int32, (rows, LANES), 0),
    )


def shifted(x, side, north, south):
    rows = x.shape[0]
    lane, row = lane_and_row(rows)
    east = jnp.where(lane == LANES - 1, side, pltpu.roll(x, LANES - 1, 1))
    west = jnp.where(lane == 0, side, pltpu.roll(x, 1, 1))
    above = jnp.where(row == rows - 1, north, pltpu.roll(x, rows - 1, 0))
    below = jnp.where(row == 0, south, pltpu.roll(x, 1, 0))
    return east, west, above, below


def turned_round(x):
    rows = x.shape[0]
    return pltpu.roll(x, LANES - 1, 1), pltpu.roll(x, 1, 1), pltpu.roll(x, rows - 1, 0), pltpu.roll(x, 1, 0)


def stencil(coefs, x, side, north, south):
    east, west, above, below = shifted(x, side, north, south)
    own, to_east, to_west, to_north, to_south = coefs
    return own * x + to_east * east + to_west * west + to_north * above + to_south * below


class Columns:
    def __init__(self, rows):
        self.rows = rows
        self.per = LANES // rows
        self.blocks = [jnp.zeros((rows, LANES), F32)] * self.per
        self.lane = lane_and_row(rows)[0]

    def put(self, index, slab):
        group, place = divmod(index, self.per)
        turned = pltpu.roll(slab, 2 * group + 1, 1)
        self.blocks[place] = jnp.where(self.lane // 2 == group, turned, self.blocks[place])

    def get(self, rows):
        return jnp.transpose(jnp.concatenate(self.blocks, axis=0))[:rows]


def sides_of(eastern, western):
    rows = eastern.shape[0]
    row = lane_and_row(rows)[1]
    return jnp.where(row % 2 == 0, pltpu.roll(eastern, rows - 1, 0), pltpu.roll(western, 1, 0))


def turn(rows):
    pad = jnp.zeros((LANES - rows.shape[0], LANES), F32)
    return jnp.transpose(jnp.concatenate([rows, pad], axis=0))


def side_of(turned, index, rows):
    group, place = divmod(index, LANES // rows)
    return pltpu.roll(turned[place * rows : (place + 1) * rows], (LANES - 2 * group - 1) % LANES, 1)


def tiled(x, rows, block=0):
    if block:
        x = pltpu.roll(x, LANES - block * rows, 1)
    x = jnp.where(lax.broadcasted_iota(jnp.int32, x.shape, 1) < rows, x, 0.0)
    width = rows
    while width < LANES:
        x = x + pltpu.roll(x, width, 1)
        width *= 2
    return x


def first_kernel(
    tracers, levels, rows, flags, counts_in, owners_in, cells_in, forcing_in, detrain_in, field_in, mix_in, east_in,
    north_in, pole_in, keep, send, slots, detrain, field, mix, east, north, pole,
    halves, counts, owners, cells, forcing, sems,
):
    pairs = [(counts_in, counts), (owners_in, owners), (cells_in, cells), (forcing_in, forcing), (detrain_in, detrain)]
    pairs += [(field_in.at[t], field.at[t]) for t in range(tracers)]
    pairs += [(mix_in, mix), (east_in, east), (north_in, north), (pole_in, pole)]
    copies = [pltpu.make_async_copy(source, target, sems.at[i]) for i, (source, target) in enumerate(pairs)]
    for copy in copies:
        copy.start()
    half = tracers // 2
    slots[...] = jnp.zeros(slots.shape, F32)
    for copy in copies[:5]:
        copy.wait()
    steps, slot_count = cells.shape
    slot_rows = slots.shape[0] * LANES // slot_count
    slot = lax.broadcasted_iota(jnp.int32, (levels, LANES), 1)
    for part in range(slot_count // LANES):
        lanes = slice(part * LANES, (part + 1) * LANES)
        for step in range(steps):
            at = part * slot_rows + step * (levels + 2)
            live = slot + part * LANES < jnp.broadcast_to(counts[:, step : step + 1], slot.shape)
            slots[at : at + levels, :] = jnp.where(live, forcing[:, step, lanes], 0.0)
            slots[at + levels : at + levels + 1, :] = owners[step, :, lanes].astype(F32)
            slots[at + levels + 1 : at + levels + 2, :] = cells[step : step + 1, lanes].astype(F32)
    weights = [detrain[k] for k in range(levels)]
    total = functools.reduce(lambda p, q: p + q, weights)
    for h in range(2):
        halves[h, half * rows :, :] = total[h * rows // 2 : (h + 1) * rows // 2]
    for t in range(tracers):
        copies[5 + t].wait()
        at = (t % half) * rows
        halves[t // half, at : at + rows, :] = functools.reduce(
            lambda p, q: p + q, [weights[k] * field[t, k] for k in range(levels)]
        )
    parity = flags[PARITY]
    keep[...] = halves[parity]
    send[...] = halves[1 - parity]
    for copy in copies[5 + tracers :]:
        copy.wait()


def inside_kernel(tracers, levels, rows, flags, after, field, kept, detrain, mix, east, north, keep, send, halves):
    half = tracers // 2
    lane, row = lane_and_row(rows)
    inside, spread = [], None
    for k in range(levels):
        weight = detrain[k]
        to_east = jnp.maximum(east[k], 0.0)
        to_west = jnp.where(lane == 0, 0.0, jnp.maximum(-pltpu.roll(east[k], 1, 1), 0.0))
        to_north = jnp.maximum(north[k], 0.0)
        to_south = jnp.where(row == 0, 0.0, jnp.maximum(-pltpu.roll(north[k], 1, 0), 0.0))
        five = [
            1.0 - to_east - to_west - to_north - to_south,
            jnp.where(lane == LANES - 1, 0.0, to_east),
            to_west,
            jnp.where(row == rows - 1, 0.0, to_north),
            to_south,
        ]
        inside.append([weight * c for c in five])
        terms = [c * s for c, s in zip(inside[k], (mix[k],) + turned_round(mix[k]))]
        spread = terms if spread is None else [p + q for p, q in zip(spread, terms)]
    for i in range(5):
        for h in range(2):
            at = half * rows + i * (rows // 2)
            halves[h, at : at + rows // 2, :] = spread[i][h * rows // 2 : (h + 1) * rows // 2]
    for t in range(tracers):
        total = None
        for k in range(levels):
            slab = kept[t, k]
            for c, x in zip(inside[k], (slab,) + turned_round(slab)):
                total = c * x if total is None else total + c * x
        at = (t % half) * rows
        halves[t // half, at : at + rows, :] = total
    parity = flags[PARITY]
    keep[...] = halves[parity]
    send[...] = halves[1 - parity]


def edge_kernel(
    tracers, levels, rows, flags, slots, field, kept, detrain, mix, east, north, pole, forward, back, columns, ring
):
    slabs = tracers * levels
    base = slabs + tracers + 1
    per = LANES // rows
    group = -(-base // per)
    column_rows = up8(2 * (group + 3))
    columns[column_rows:] = slots[...]
    ring[...] = jnp.zeros(ring.shape, F32)
    weights = [detrain[k] for k in range(levels)]
    cols = Columns(rows)

    def edge_rows(place, slab):
        ring[0, place : place + 1, :] = slab[rows - 1 : rows]
        ring[1, place : place + 1, :] = slab[:1]

    total = functools.reduce(lambda p, q: p + q, weights)
    cols.put(slabs + tracers, total)
    edge_rows(slabs + tracers, total)
    for k in range(levels):
        edge_rows(base + k, mix[k])
        edge_rows(base + levels + k, detrain[k])
        ring[0, base + 2 * levels + k : base + 2 * levels + k + 1, :] = north[k, rows - 1 : rows, :]
        ring[1, base + 2 * levels + k : base + 2 * levels + k + 1, :] = pole[k : k + 1, :]
        cols.put(group * per + k, mix[k])
        cols.put((group + 1) * per + k, detrain[k])
        cols.put((group + 2) * per + k, east[k])
    for t in range(tracers):
        partial = None
        for k in range(levels):
            term = weights[k] * field[t, k]
            partial = term if partial is None else partial + term
            slab = kept[t, k]
            cols.put(k * tracers + t, slab)
            edge_rows(k * tracers + t, slab)
        cols.put(slabs + t, partial)
        edge_rows(slabs + t, partial)
    ascending = flags[ASCENDING]
    forward[...] = ring[1 - ascending]
    back[...] = ring[ascending]
    columns[:column_rows] = cols.get(column_rows)


def second_kernel(
    tracers, levels, rows, flags, first, second, detrain, mix, east, north, pole,
    own_forward, own_back, own_columns, forward, back, eastern, western,
    late, coefs, edges, turned,
):
    slabs = tracers * levels
    base = slabs + tracers + 1
    per = LANES // rows
    group = -(-base // per)
    ascending = flags[ASCENDING] == 1
    from_north = jnp.where(ascending, back[...], forward[...])
    from_south = jnp.where(ascending, forward[...], back[...])
    own_north = jnp.where(ascending, own_forward[...], own_back[...])
    own_south = jnp.where(ascending, own_back[...], own_forward[...])
    edges[0] = from_north
    edges[1] = from_south
    sides = sides_of(eastern[...], western[...])
    mine = own_columns[...]
    around = turn(sides)
    turned[...] = around
    lane, row = lane_and_row(rows)
    top, bottom = flags[TOP] == 1, flags[BOTTOM] == 1
    is_top = jnp.logical_and(row == rows - 1, top)
    is_bottom = jnp.logical_and(row == 0, bottom)
    west_row = lane_and_row(2)[1] == 1
    groups = tracers // per
    zero = jnp.zeros((1, LANES), F32)
    add_north = add_south = spread_north = spread_south = less_north = less_south = 0.0
    add_sides = [0.0] * groups
    spread_sides = less_sides = 0.0
    for k in range(levels):
        place = base + 2 * levels + k
        wind = east[k]
        behind = jnp.where(lane == 0, side_of(around, (group + 2) * per + k, rows), pltpu.roll(wind, 1, 1))
        to_east = jnp.maximum(wind, 0.0)
        to_west = jnp.maximum(-behind, 0.0)
        wind = north[k]
        pole_north = jnp.where(top, jnp.maximum(-from_north[place : place + 1], 0.0), zero)
        to_north = jnp.maximum(wind, 0.0) + jnp.where(is_top, pole_north, 0.0)
        below = from_south[place : place + 1]
        pole_south = jnp.maximum(pole[k : k + 1, :], 0.0) + jnp.maximum(-below, 0.0)
        behind = jnp.where(row == 0, below, pltpu.roll(wind, 1, 0))
        to_south = jnp.where(is_bottom, pole_south, jnp.maximum(-behind, 0.0))
        for i, c in enumerate([1.0 - to_east - to_west - to_north - to_south, to_east, to_west, to_north, to_south]):
            coefs[i, k] = c

        level = slice(k * tracers, (k + 1) * tracers)
        weight = detrain[k, rows - 1 : rows, :]
        taken, given = weight * to_north[rows - 1 : rows], weight * pole_north
        add_north = add_north + taken * from_north[level] - given * own_north[level]
        spread_north = spread_north + taken * from_north[base + k : base + k + 1]
        less_north = less_north - given * mix[k, rows - 1 : rows, :]
        taken = detrain[k, :1, :] * to_south[:1]
        add_south = add_south + taken * (from_south[level] - own_south[level])
        spread_south = spread_south + taken * from_south[base + k : base + k + 1]
        less_south = less_south - taken * mix[k, :1, :]

        winds = slice(2 * (group + 2), 2 * (group + 3))
        shares = slice(2 * group, 2 * (group + 1))
        weight = tiled(mine[2 * (group + 1) : 2 * (group + 2)], rows, k)
        wind = jnp.where(west_row, jnp.maximum(-sides[winds], 0.0), jnp.maximum(mine[winds], 0.0))
        taken = weight * tiled(wind, rows, k)
        given = jnp.where(west_row, taken, 0.0)
        for g in range(groups):
            pair = slice(2 * (k * groups + g), 2 * (k * groups + g + 1))
            add_sides[g] = add_sides[g] + taken * sides[pair] - given * mine[pair]
        spread_sides = spread_sides + taken * tiled(sides[shares], rows, k)
        less_sides = less_sides - given * tiled(mine[shares], rows, k)
    parts = [sides[2 * (slabs // per) : 2 * group]] + add_sides
    parts += [spread_sides, less_sides, spread_north, spread_south, less_north, less_south]
    parts += [add_north, add_south, from_north[slabs : slabs + tracers + 1], from_south[slabs : slabs + tracers + 1]]
    at = 0
    for part in parts:
        late[at : at + part.shape[0]] = part
        at += part.shape[0]
    if at < late.shape[0]:
        late[at:] = jnp.zeros((late.shape[0] - at, LANES), F32)


def pieces(x):
    high = x.astype(jnp.bfloat16)
    return [high, (x - high.astype(F32)).astype(jnp.bfloat16)]


def product(a, b):
    return lax.dot_general(a, b, (((1,), (1,)), ((), ())), preferred_element_type=F32)


def forcing_kernel(levels, rows, steps, flags, slots, detrain, mix, coefs, edges, turned, base, grids, edge_rows, sums):
    parts = min(8, slots.shape[0])
    count = parts * LANES
    per = LANES // rows
    row_ids = lax.broadcasted_iota(jnp.int32, (rows, count), 0)
    lane_ids = lax.broadcasted_iota(jnp.int32, (LANES, count), 0)
    group = -(-base // per)

    def add_block(index, carry):
        late, early, ring_sides = carry
        block = jnp.concatenate([slots[parts * index + part] for part in range(parts)], axis=1)
        results = []
        for step in range(steps):
            first = step * (levels + 2)
            values = [block[first + k : first + k + 1] for k in range(levels)]
            owner = block[first + levels : first + levels + 1].astype(jnp.int32)
            cell = block[first + levels + 1 : first + levels + 2].astype(jnp.int32)
            slot_row, slot_lane = cell // LANES, cell % LANES
            lanes = (lane_ids == slot_lane).astype(F32).astype(jnp.bfloat16)
            here = jnp.logical_and(row_ids == slot_row, owner == flags[SELF])
            left = [jnp.where(here, value, 0.0) for value in values]
            if step == steps - 1:
                in_north = jnp.logical_and(owner == flags[NORTH], slot_row == flags[NORTH_ROW])
                in_south = jnp.logical_and(owner == flags[SOUTH], slot_row == flags[SOUTH_ROW])
                left += [jnp.where(in_north, value, 0.0) for value in values]
                left += [jnp.where(in_south, value, 0.0) for value in values]
                left += [jnp.zeros((8 - 2 * levels, count), F32)]
            left = jnp.concatenate(left, axis=0)
            results.append(sum(product(piece, lanes) for piece in pieces(left)))
            if step == steps - 1:
                in_east = jnp.logical_and(owner == flags[EAST], slot_lane == 0)
                in_west = jnp.logical_and(owner == flags[WEST], slot_lane == LANES - 1)
                right = [jnp.where(in_east, value, 0.0) for value in values]
                right += [jnp.where(in_west, value, 0.0) for value in values]
                right += [jnp.zeros((8 - 2 * levels, count), F32)]
                right = jnp.concatenate(right, axis=0)
                at_row = (row_ids == slot_row).astype(F32).astype(jnp.bfloat16)
                ring_sides = ring_sides + sum(product(at_row, piece) for piece in pieces(right))
        return late + results[1], early + results[0], ring_sides

    late, early, ring_sides = lax.fori_loop(
        0,
        slots.shape[0] // parts,
        add_block,
        (
            jnp.zeros((levels * rows + 8, LANES), F32),
            jnp.zeros((levels * rows, LANES), F32),
            jnp.zeros((rows, 8), F32),
        ),
        unroll=slots.shape[0] // parts <= 2,
    )
    lane, _ = lane_and_row(rows)
    north_rows = late[levels * rows : levels * rows + levels]
    south_rows = late[levels * rows + levels : levels * rows + 2 * levels]
    edge_rows[...] = late[levels * rows :]
    around = turned[...]
    at_end = at_first = None
    ring = jnp.zeros((rows, LANES), F32)
    ring_north = jnp.zeros((1, LANES), F32)
    ring_south = jnp.zeros((1, LANES), F32)
    for k in range(levels):
        own = late[k * rows : (k + 1) * rows]
        now = early[k * rows : (k + 1) * rows]
        east_side = jnp.broadcast_to(ring_sides[:, k : k + 1], (rows, LANES))
        west_side = jnp.broadcast_to(ring_sides[:, levels + k : levels + k + 1], (rows, LANES))
        side = jnp.where(lane == LANES - 1, east_side, jnp.where(lane == 0, west_side, 0.0))
        grids[k] = own
        grids[levels + k] = now
        grids[2 * levels + k] = side
        mix_side = side_of(around, group * per + k, rows)
        detrain_side = side_of(around, (group + 1) * per + k, rows)
        north, south = north_rows[k : k + 1], south_rows[k : k + 1]
        moved = stencil(
            [coefs[i, k] for i in range(5)],
            (1.0 - mix[k]) * own,
            (1.0 - mix_side) * side,
            (1.0 - edges[0, base + k : base + k + 1, :]) * north,
            (1.0 - edges[1, base + k : base + k + 1, :]) * south,
        )
        first = detrain[k] * own
        second = detrain[k] * (moved + now)
        at_first = first if at_first is None else at_first + first
        at_end = second if at_end is None else at_end + second
        ring = ring + detrain_side * side
        place = base + levels + k
        ring_north = ring_north + edges[0, place : place + 1, :] * north
        ring_south = ring_south + edges[1, place : place + 1, :] * south
    sums[:rows] = at_first
    sums[rows : 2 * rows] = at_end
    flat = jnp.transpose(jnp.concatenate([ring] + [jnp.zeros((rows, LANES), F32)] * (per - 1), axis=0))
    sums[2 * rows :] = jnp.concatenate(
        [ring_north, ring_south, flat[LANES - 1 :], flat[:1], jnp.zeros((4, LANES), F32)], axis=0
    )


def third_kernel(
    tracers, levels, rows, flags, field, mix, coefs, edges, turned, mine, other, moved_out, column_out, inverse_out, first,
):
    half = tracers // 2
    parity = flags[PARITY]
    first[parity] = mine[...]
    first[1 - parity] = other[...]
    total = jnp.concatenate([first[0, half * rows :, :], first[1, half * rows :, :]], axis=0)
    inverse = 1.0 / total
    inverse_out[...] = inverse
    around = turned[...]
    stay = [1.0 - mix[k] for k in range(levels)]
    five = [[coefs[i, k] for i in range(5)] for k in range(levels)]
    for t in range(tracers):
        column = first[t // half, (t % half) * rows : (t % half + 1) * rows, :] * inverse
        column_out[t] = column
        for k in range(levels):
            place = k * tracers + t
            moved = stencil(
                five[k],
                stay[k] * field[t, k] + mix[k] * column,
                side_of(around, place, rows),
                edges[0, place : place + 1, :],
                edges[1, place : place + 1, :],
            )
            moved_out[t, k] = stay[k] * moved


def fourth_kernel(
    tracers, levels, rows, flags, moved, column, inverse_in, mix, coefs, edges, turned, grids, edge_rows,
    mine, other, forced_1, forced_2, forced_3, forced_4, mixed_out, forward, back, columns, second, ring,
):
    half = tracers // 2
    slabs = tracers * levels
    base = slabs + tracers + 1
    per = LANES // rows
    group = -(-base // per)
    groups = tracers // per
    parity = flags[PARITY]
    second_rows = second.shape[1]
    second[parity] = mine[:second_rows]
    second[1 - parity] = other[:second_rows]
    late = mine[second_rows:] + other[second_rows:]
    forced = (forced_1[...] + forced_2[...]) + (forced_3[...] + forced_4[...])
    inverse = inverse_in[...]
    lane, row = lane_and_row(rows)
    at_side = jnp.logical_or(lane == 0, lane == LANES - 1)
    last, initial = row == rows - 1, row == 0

    at = 2 * (group - slabs // per)
    inverse_side = 1.0 / tiled(late[2 * groups : 2 * groups + 2], rows)
    forced_sides = tiled(forced[2 * rows + 2 : 2 * rows + 4], rows)
    side_rows = [(late[2 * g : 2 * g + 2] + forced_sides) * inverse_side for g in range(groups)]
    side_rows += [late[at : at + 2 * groups + 4]]
    at += 2 * groups + 4
    around_late = turn(jnp.concatenate(side_rows, axis=0))
    spread_side = side_of(around_late, 2 * groups * per, rows)
    less_side = side_of(around_late, (2 * groups + 1) * per, rows)
    north, south, less_north, less_south = [late[at + i : at + i + 1] for i in range(4)]
    at += 4
    add_ends = [late[at + e * tracers : at + (e + 1) * tracers] for e in range(2)]
    at += 2 * tracers
    column_ends = []
    for e in range(2):
        sums = late[at : at + tracers + 1]
        column_ends.append((sums[:tracers] + forced[2 * rows + e : 2 * rows + e + 1]) / sums[tracers:])
        at += tracers + 1

    spread = []
    start = half * rows
    for i in range(5):
        at = start + i * (rows // 2)
        spread.append(jnp.concatenate([second[h, at : at + rows // 2, :] for h in range(2)], axis=0))
    spread[0] = spread[0] + jnp.where(last, less_north, 0.0) + jnp.where(initial, less_south, 0.0)
    spread[0] = spread[0] + jnp.where(lane == 0, less_side, 0.0)
    spread[1] = jnp.where(lane == LANES - 1, spread_side, spread[1])
    spread[2] = spread[2] + jnp.where(lane == 0, spread_side, 0.0)
    spread[3] = jnp.where(last, north, spread[3])
    spread[4] = spread[4] + jnp.where(initial, south, 0.0)

    forced_column = forced[:rows] * inverse
    forced_later = forced[rows : 2 * rows]
    around = turned[...]
    stay = [1.0 - mix[k] for k in range(levels)]
    forced_moved, to_sides, to_ends = [], [], []
    for k in range(levels):
        five = [coefs[i, k] for i in range(5)]
        mix_side = side_of(around, group * per + k, rows)
        shares = [edges[e, base + k : base + k + 1, :] for e in range(2)]
        ends = [(1.0 - shares[e]) * edge_rows[e * levels + k : e * levels + k + 1, :] for e in range(2)]
        moved_forcing = stencil(
            five,
            stay[k] * grids[k] + mix[k] * forced_column,
            (1.0 - mix_side) * grids[2 * levels + k],
            ends[0],
            ends[1],
        )
        forced_moved.append(stay[k] * (moved_forcing + grids[levels + k]))
        to_side = jnp.where(lane == LANES - 1, five[1], jnp.where(lane == 0, five[2], 0.0))
        to_sides.append(stay[k] * to_side * mix_side)
        to_ends.append(
            [
                jnp.where(last, stay[k] * five[3] * shares[0], 0.0)[rows - 8 :],
                jnp.where(initial, stay[k] * five[4] * shares[1], 0.0)[:8],
            ]
        )

    cols = Columns(rows)
    ring[...] = jnp.zeros(ring.shape, F32)
    for t in range(tracers):
        h, at = t // half, (t % half) * rows
        column_side = side_of(around_late, t, rows)
        column_north, column_south = column_ends[0][t : t + 1], column_ends[1][t : t + 1]
        later = second[h, at : at + rows, :] + forced_later
        later = later + jnp.where(at_side, side_of(around_late, (groups + t // per) * per + t % per, rows), 0.0)
        later = later + jnp.where(last, add_ends[0][t : t + 1], 0.0)
        later = later + jnp.where(initial, add_ends[1][t : t + 1], 0.0)
        later = later + stencil(spread, column[t] + forced_column, column_side, column_north, column_south)
        later = later * inverse
        for k in range(levels):
            place = k * tracers + t
            mixed = moved[t, k] + forced_moved[k] + mix[k] * later + to_sides[k] * column_side
            mixed = jnp.concatenate(
                [
                    mixed[:8] + to_ends[k][1] * column_south,
                    mixed[8 : rows - 8],
                    mixed[rows - 8 :] + to_ends[k][0] * column_north,
                ],
                axis=0,
            )
            mixed_out[t, k] = mixed
            cols.put(place, mixed)
            ring[0, place : place + 1, :] = mixed[rows - 1 : rows]
            ring[1, place : place + 1, :] = mixed[:1]
    ascending = flags[ASCENDING]
    forward[...] = ring[1 - ascending]
    back[...] = ring[ascending]
    columns[...] = cols.get(columns.shape[0])


def inner_kernel(tracers, levels, rows, flags, mixed, coefs, out):
    lane, row = lane_and_row(rows)
    for k in range(levels):
        own, to_east, to_west, to_north, to_south = [coefs[i, k] for i in range(5)]
        five = [
            own,
            jnp.where(lane == LANES - 1, 0.0, to_east),
            jnp.where(lane == 0, 0.0, to_west),
            jnp.where(row == rows - 1, 0.0, to_north),
            jnp.where(row == 0, 0.0, to_south),
        ]
        for t in range(tracers):
            slab = mixed[t, k]
            total = None
            for c, x in zip(five, (slab,) + turned_round(slab)):
                total = c * x if total is None else total + c * x
            out[t, k] = total


def last_kernel(tracers, levels, rows, flags, inner, coefs, forward, back, eastern, western, out, result, sems):
    ascending = flags[ASCENDING] == 1
    from_north = jnp.where(ascending, back[...], forward[...])
    from_south = jnp.where(ascending, forward[...], back[...])
    around = turn(sides_of(eastern[...], western[...]))
    lane, row = lane_and_row(rows)
    last, initial = row == rows - 1, row == 0
    to_sides = [
        jnp.where(lane == LANES - 1, coefs[1, k], jnp.where(lane == 0, coefs[2, k], 0.0)) for k in range(levels)
    ]
    to_north = [jnp.where(last, coefs[3, k], 0.0)[rows - 8 :] for k in range(levels)]
    to_south = [jnp.where(initial, coefs[4, k], 0.0)[:8] for k in range(levels)]
    copies = []
    for t in range(tracers):
        for k in range(levels):
            place = k * tracers + t
            total = inner[t, k] + to_sides[k] * side_of(around, place, rows)
            result[t, k, :8, :] = total[:8] + to_south[k] * from_south[place : place + 1]
            result[t, k, 8 : rows - 8, :] = total[8 : rows - 8]
            result[t, k, rows - 8 :, :] = total[rows - 8 :] + to_north[k] * from_north[place : place + 1]
        copy = pltpu.make_async_copy(result.at[t], out.at[t], sems.at[t])
        copy.start()
        copies.append(copy)
    for copy in copies:
        copy.wait()


def up8(count):
    return -(-count // 8) * 8


def call(kernel, scalars, args, outs, scratch=(), placed=(), copies=0, placed_out=False, weight=0):
    vmem, free = pl.BlockSpec(memory_space=pltpu.VMEM), pl.BlockSpec(memory_space=pl.ANY)
    return pl.pallas_call(
        kernel,
        out_shape=[jax.ShapeDtypeStruct(shape, F32) for shape in outs],
        in_specs=[pl.BlockSpec(memory_space=pltpu.SMEM)] * len(scalars) + [free] * len(placed) + [vmem] * len(args),
        out_specs=[free if placed_out else vmem] * len(outs),
        scratch_shapes=[pltpu.VMEM(x.shape, x.dtype) if hasattr(x, "dtype") else pltpu.VMEM(x, F32) for x in scratch]
        + ([pltpu.SemaphoreType.DMA((copies,))] if copies else []),
        compiler_params=pltpu.CompilerParams(vmem_limit_bytes=16 * 1024 * 1024),
        cost_estimate=pl.CostEstimate(flops=int(weight * 1e9), bytes_accessed=0, transcendentals=0),
    )(*scalars, *placed, *args)


def on_device(
    adjoint_field,
    east_courant,
    north_courant,
    pole_courant,
    mix_fraction,
    detrain_share,
    sounding_owner,
    sounding_cell,
    sounding_count,
    sounding_forcing,
):
    lon_count, lat_count = lax.axis_size("lon"), lax.axis_size("lat")
    lon, lat, lev = lax.axis_index("lon"), lax.axis_index("lat"), lax.axis_index("lev")
    tracers, levels, rows, lanes = adjoint_field.shape
    steps, slot_count = sounding_cell.shape
    slabs = tracers * levels
    base = slabs + tracers + 1
    per = lanes // rows
    size = (tracers, levels, rows)

    top, bottom = lat == lat_count - 1, lat == 0
    partner = (lon + lon_count // 2) % lon_count
    flags = [
        top,
        bottom,
        lon < lon_count // 2,
        (lev ^ (lev >> 1)) & 1,
        lon * lat_count + lat,
        jnp.where(top, partner * lat_count + lat, lon * lat_count + lat + 1),
        jnp.where(bottom, partner * lat_count + lat, lon * lat_count + lat - 1),
        (lon + 1) % lon_count * lat_count + lat,
        (lon + lon_count - 1) % lon_count * lat_count + lat,
        jnp.where(top, rows - 1, 0),
        jnp.where(bottom, 0, rows - 1),
    ]
    flags = jnp.stack([jnp.asarray(flag, jnp.int32) for flag in flags])

    ring_rows = up8(base + 3 * levels)
    column_rows = up8(2 * (-(-base // per) + 3))
    slot_rows = up8(steps * (levels + 2))
    first_rows = tracers // 2 * rows + rows // 2
    second_rows = tracers // 2 * rows + 5 * (rows // 2)
    soundings = [
        jnp.swapaxes(sounding_count, 0, 1),
        jnp.swapaxes(sounding_owner, 1, 2),
        sounding_cell,
        jnp.swapaxes(sounding_forcing, 0, 1),
    ]
    inputs = [detrain_share, adjoint_field, mix_fraction, east_courant, north_courant, pole_courant]
    keep_first, send_first, slots, detrain, field, mix, east, north, pole = call(
        functools.partial(first_kernel, *size),
        [flags],
        [],
        [(first_rows, lanes)] * 2 + [(slot_count // lanes * slot_rows, lanes)] + [x.shape for x in inputs],
        [(2, first_rows, lanes)] + soundings,
        [pltpu.with_memory_space_constraint(x, pltpu.HBM) for x in soundings + inputs],
        tracers - 1 + len(soundings) + len(inputs),
    )
    static = [detrain, mix, east, north, pole]
    kept = (1.0 - mix)[None] * field
    own_forward, own_back, columns = call(
        functools.partial(edge_kernel, *size),
        [flags],
        [slots, field, kept] + static,
        [(ring_rows, lanes)] * 2 + [(column_rows + slots.shape[0], lanes)],
        [(2, ring_rows, lanes)],
        weight=WEIGHTS[1],
    )
    keep_second, send_second = call(
        functools.partial(inside_kernel, *size),
        [flags],
        [field, kept, detrain, mix, east, north],
        [(second_rows, lanes)] * 2,
        [(2, second_rows, lanes)],
        [columns],
        weight=WEIGHTS[0],
    )
    first = add(keep_first, swap_over(send_first, "lev", 1))
    second = add(keep_second, swap_over(send_second, "lev", 1))
    eastern, western = exchange_columns(columns)
    forward, back = exchange_rows(own_forward, own_back)
    other_first = swap_over(first, "lev", 3)

    late_rows = 2 * (-(-base // per) - slabs // per) + 2 * (tracers // per) + 8 + 4 * tracers + 2
    late, coefs, edges, turned = call(
        functools.partial(second_kernel, *size),
        [flags],
        static
        + [own_forward, own_back, columns[:column_rows]]
        + [forward, back, eastern[:column_rows], western[:column_rows]],
        [(up8(late_rows), lanes), (5, levels, rows, lanes), (2, ring_rows, lanes), (lanes, lanes)],
        placed=[first, second],
        weight=WEIGHTS[2],
    )
    second = jnp.concatenate([second, late], axis=0)
    other_second = swap_over(second, "lev", 3)
    slots = columns[column_rows:][None]
    if lon_count == 2:
        slots = pair(columns[column_rows:], eastern[column_rows:], first)
    else:
        slots = gather_blocks(slots, "lon")
    slots = gather_blocks(slots, "lat").reshape(-1, slot_rows, lanes)
    grids, edge_rows, sums = call(
        lambda *refs: forcing_kernel(levels, rows, steps, *refs[:7], base, *refs[7:]),
        [flags],
        [slots, detrain, mix, coefs, edges, turned],
        [(3 * levels, rows, lanes), (8, lanes), (2 * rows + 8, lanes)],
        weight=WEIGHTS[3],
    )
    sums = [sums] + [swap_over(sums, "lev", bit) for bit in (1, 2, 3)]
    first = add(first, other_first, sums[0])
    other_first = swap_over(first, "lev", 1)
    second = add(second, other_second, first)
    other_second = swap_over(second, "lev", 1)

    moved, column, inverse = call(
        functools.partial(third_kernel, *size),
        [flags],
        [field, mix, coefs, edges, turned, first, other_first],
        [adjoint_field.shape, (tracers, rows, lanes), (rows, lanes)],
        [(2, first_rows, lanes)],
        weight=WEIGHTS[4],
    )
    slab_rows = up8(slabs)
    mixed, forward, back, columns = call(
        functools.partial(fourth_kernel, *size),
        [flags],
        [
            moved, column, inverse, mix, coefs, edges, turned, grids, edge_rows,
            second, other_second, *sums,
        ],
        [adjoint_field.shape] + [(slab_rows, lanes)] * 2 + [(up8(2 * (slabs // per)), lanes)],
        [(2, second_rows, lanes), (2, slab_rows, lanes)],
    )
    eastern, western = exchange_columns(columns)
    forward, back = exchange_rows(forward, back)
    (inner,) = call(functools.partial(inner_kernel, *size), [flags], [mixed, coefs], [adjoint_field.shape])
    (out,) = call(
        functools.partial(last_kernel, *size),
        [flags],
        [inner, coefs, forward, back, eastern, western],
        [adjoint_field.shape],
        [adjoint_field.shape],
        copies=tracers,
        placed_out=True,
    )
    return out


def solution(mesh):
    return jax.shard_map(
        on_device,
        mesh=mesh,
        in_specs=(
            P(None, "lev", "lat", "lon"),
            P("lev", "lat", "lon"),
            P("lev", "lat", "lon"),
            P("lev", "lon"),
            P("lev", "lat", "lon"),
            P("lev", "lat", "lon"),
            P(None, ("lon", "lat"), None),
            P(None, ("lon", "lat")),
            P(None, ("lon", "lat")),
            P(None, "lev", ("lon", "lat")),
        ),
        out_specs=P(None, "lev", "lat", "lon"),
        check_vma=False,
    )
```

```python
import functools

import jax
import jax.numpy as jnp
from jax import lax
from jax.experimental import pallas as pl
from jax.experimental.pallas import tpu as pltpu
from jax.sharding import PartitionSpec as P

F32 = jnp.float32
WEIGHTS = [0, 0, 0, 20, 20]
LANES = 128
TOP, BOTTOM, ASCENDING, PARITY, SELF, NORTH, SOUTH, EAST, WEST, NORTH_ROW, SOUTH_ROW, LATER_PARITY = range(12)


def swap_over(value, axis, bit):
    return lax.ppermute(value, axis, [(i, i ^ bit) for i in range(lax.axis_size(axis))])


def shift_over(value, axis, steps):
    count = lax.axis_size(axis)
    return lax.ppermute(value, axis, [(i, (i + steps) % count) for i in range(count)])


def meridian_rings(lon_count, lat_count, steps):
    pairs = []
    for lon in range(lon_count // 2):
        ring = [lon * lat_count + lat for lat in range(lat_count)]
        ring += [(lon + lon_count // 2) * lat_count + lat for lat in reversed(range(lat_count))]
        pairs += [(ring[i], ring[(i + steps) % len(ring)]) for i in range(len(ring))]
    return pairs


def exchange_rows(forward, back):
    lon_count, lat_count = lax.axis_size("lon"), lax.axis_size("lat")
    return (
        lax.ppermute(forward, ("lon", "lat"), meridian_rings(lon_count, lat_count, 1)),
        lax.ppermute(back, ("lon", "lat"), meridian_rings(lon_count, lat_count, -1)),
    )


def exchange_columns(columns):
    if lax.axis_size("lon") == 2:
        other = swap_over(columns, "lon", 1)
        return other, other
    return shift_over(columns, "lon", -1), shift_over(columns, "lon", 1)


def pair_kernel(a, b, *refs):
    refs[-1][0] = a[...]
    refs[-1][1] = b[...]


def pair(a, b, *after):
    vmem = pl.BlockSpec(memory_space=pltpu.VMEM)
    return pl.pallas_call(
        pair_kernel,
        out_shape=jax.ShapeDtypeStruct((2, *a.shape), a.dtype),
        in_specs=[vmem, vmem] + [pl.BlockSpec(memory_space=pl.ANY)] * len(after),
        out_specs=vmem,
        compiler_params=pltpu.CompilerParams(vmem_limit_bytes=4 * 1024 * 1024),
    )(a, b, *after)


def gather_blocks(blocks, axis):
    count = lax.axis_size(axis)
    if count not in (2, 4):
        return lax.all_gather(blocks, axis, axis=0, tiled=True)
    return jnp.concatenate([blocks] + [swap_over(blocks, axis, bit) for bit in range(1, count)], axis=0)


def add_kernel(waited, a, b, *refs):
    refs[-1][...] = a[...] + b[...]


def add(a, b, *after):
    vmem = pl.BlockSpec(memory_space=pltpu.VMEM)
    return pl.pallas_call(
        functools.partial(add_kernel, len(after)),
        out_shape=jax.ShapeDtypeStruct(a.shape, a.dtype),
        in_specs=[vmem, vmem] + [pl.BlockSpec(memory_space=pl.ANY)] * len(after),
        out_specs=vmem,
        compiler_params=pltpu.CompilerParams(vmem_limit_bytes=4 * 1024 * 1024),
    )(a, b, *after)


def lane_and_row(rows):
    return (
        lax.broadcasted_iota(jnp.int32, (rows, LANES), 1),
        lax.broadcasted_iota(jnp.int32, (rows, LANES), 0),
    )


def shifted(x, side, north, south):
    rows = x.shape[0]
    lane, row = lane_and_row(rows)
    east = jnp.where(lane == LANES - 1, side, pltpu.roll(x, LANES - 1, 1))
    west = jnp.where(lane == 0, side, pltpu.roll(x, 1, 1))
    above = jnp.where(row == rows - 1, north, pltpu.roll(x, rows - 1, 0))
    below = jnp.where(row == 0, south, pltpu.roll(x, 1, 0))
    return east, west, above, below


def turned_round(x):
    rows = x.shape[0]
    return pltpu.roll(x, LANES - 1, 1), pltpu.roll(x, 1, 1), pltpu.roll(x, rows - 1, 0), pltpu.roll(x, 1, 0)


def stencil(coefs, x, side, north, south):
    east, west, above, below = shifted(x, side, north, south)
    own, to_east, to_west, to_north, to_south = coefs
    return own * x + to_east * east + to_west * west + to_north * above + to_south * below


class Columns:
    def __init__(self, rows):
        self.rows = rows
        self.per = LANES // rows
        self.blocks = [jnp.zeros((rows, LANES), F32)] * self.per
        self.lane = lane_and_row(rows)[0]

    def put(self, index, slab):
        group, place = divmod(index, self.per)
        turned = pltpu.roll(slab, 2 * group + 1, 1)
        self.blocks[place] = jnp.where(self.lane // 2 == group, turned, self.blocks[place])

    def get(self, rows):
        return jnp.transpose(jnp.concatenate(self.blocks, axis=0))[:rows]


def sides_of(eastern, western):
    rows = eastern.shape[0]
    row = lane_and_row(rows)[1]
    return jnp.where(row % 2 == 0, pltpu.roll(eastern, rows - 1, 0), pltpu.roll(western, 1, 0))


def turn(rows):
    pad = jnp.zeros((LANES - rows.shape[0], LANES), F32)
    return jnp.transpose(jnp.concatenate([rows, pad], axis=0))


def side_of(turned, index, rows):
    group, place = divmod(index, LANES // rows)
    return pltpu.roll(turned[place * rows : (place + 1) * rows], (LANES - 2 * group - 1) % LANES, 1)


def tiled(x, rows, block=0):
    if block:
        x = pltpu.roll(x, LANES - block * rows, 1)
    x = jnp.where(lax.broadcasted_iota(jnp.int32, x.shape, 1) < rows, x, 0.0)
    width = rows
    while width < LANES:
        x = x + pltpu.roll(x, width, 1)
        width *= 2
    return x


def first_kernel(
    tracers, levels, rows, flags, counts_in, owners_in, cells_in, forcing_in, detrain_in, field_in, mix_in, east_in,
    north_in, pole_in, keep, send, slots, detrain, field, mix, east, north, pole,
    halves, counts, owners, cells, forcing, sems,
):
    pairs = [(counts_in, counts), (owners_in, owners), (cells_in, cells), (forcing_in, forcing), (detrain_in, detrain)]
    pairs += [(field_in.at[t], field.at[t]) for t in range(tracers)]
    pairs += [(mix_in, mix), (east_in, east), (north_in, north), (pole_in, pole)]
    copies = [pltpu.make_async_copy(source, target, sems.at[i]) for i, (source, target) in enumerate(pairs)]
    for copy in copies:
        copy.start()
    half = tracers // 2
    slots[...] = jnp.zeros(slots.shape, F32)
    for copy in copies[:5]:
        copy.wait()
    steps, slot_count = cells.shape
    slot_rows = slots.shape[0] * LANES // slot_count
    slot = lax.broadcasted_iota(jnp.int32, (levels, LANES), 1)
    for part in range(slot_count // LANES):
        lanes = slice(part * LANES, (part + 1) * LANES)
        for step in range(steps):
            at = part * slot_rows + step * (levels + 2)
            live = slot + part * LANES < jnp.broadcast_to(counts[:, step : step + 1], slot.shape)
            slots[at : at + levels, :] = jnp.where(live, forcing[:, step, lanes], 0.0)
            slots[at + levels : at + levels + 1, :] = owners[step, :, lanes].astype(F32)
            slots[at + levels + 1 : at + levels + 2, :] = cells[step : step + 1, lanes].astype(F32)
    weights = [detrain[k] for k in range(levels)]
    total = functools.reduce(lambda p, q: p + q, weights)
    for h in range(2):
        halves[h, half * rows :, :] = total[h * rows // 2 : (h + 1) * rows // 2]
    for t in range(tracers):
        copies[5 + t].wait()
        at = (t % half) * rows
        halves[t // half, at : at + rows, :] = functools.reduce(
            lambda p, q: p + q, [weights[k] * field[t, k] for k in range(levels)]
        )
    parity = flags[PARITY]
    keep[...] = halves[parity]
    send[...] = halves[1 - parity]
    for copy in copies[5 + tracers :]:
        copy.wait()


def inside_kernel(tracers, levels, rows, flags, after, field, kept, detrain, mix, east, north, keep, send, halves):
    half = tracers // 2
    lane, row = lane_and_row(rows)
    inside, spread = [], None
    for k in range(levels):
        weight = detrain[k]
        to_east = jnp.maximum(east[k], 0.0)
        to_west = jnp.where(lane == 0, 0.0, jnp.maximum(-pltpu.roll(east[k], 1, 1), 0.0))
        to_north = jnp.maximum(north[k], 0.0)
        to_south = jnp.where(row == 0, 0.0, jnp.maximum(-pltpu.roll(north[k], 1, 0), 0.0))
        five = [
            1.0 - to_east - to_west - to_north - to_south,
            jnp.where(lane == LANES - 1, 0.0, to_east),
            to_west,
            jnp.where(row == rows - 1, 0.0, to_north),
            to_south,
        ]
        inside.append([weight * c for c in five])
        terms = [c * s for c, s in zip(inside[k], (mix[k],) + turned_round(mix[k]))]
        spread = terms if spread is None else [p + q for p, q in zip(spread, terms)]
    for i in range(5):
        for h in range(2):
            at = half * rows + i * (rows // 2)
            halves[h, at : at + rows // 2, :] = spread[i][h * rows // 2 : (h + 1) * rows // 2]
    for t in range(tracers):
        total = None
        for k in range(levels):
            slab = kept[t, k]
            for c, x in zip(inside[k], (slab,) + turned_round(slab)):
                total = c * x if total is None else total + c * x
        at = (t % half) * rows
        halves[t // half, at : at + rows, :] = total
    parity = flags[LATER_PARITY]
    keep[...] = halves[parity]
    send[...] = halves[1 - parity]


def edge_kernel(
    tracers, levels, rows, flags, slots, field, kept, detrain, mix, east, north, pole, forward, back, columns, ring
):
    slabs = tracers * levels
    base = slabs + tracers + 1
    per = LANES // rows
    group = -(-base // per)
    column_rows = up8(2 * (group + 3))
    columns[column_rows:] = slots[...]
    ring[...] = jnp.zeros(ring.shape, F32)
    weights = [detrain[k] for k in range(levels)]
    cols = Columns(rows)

    def edge_rows(place, slab):
        ring[0, place : place + 1, :] = slab[rows - 1 : rows]
        ring[1, place : place + 1, :] = slab[:1]

    total = functools.reduce(lambda p, q: p + q, weights)
    cols.put(slabs + tracers, total)
    edge_rows(slabs + tracers, total)
    for k in range(levels):
        edge_rows(base + k, mix[k])
        edge_rows(base + levels + k, detrain[k])
        ring[0, base + 2 * levels + k : base + 2 * levels + k + 1, :] = north[k, rows - 1 : rows, :]
        ring[1, base + 2 * levels + k : base + 2 * levels + k + 1, :] = pole[k : k + 1, :]
        cols.put(group * per + k, mix[k])
        cols.put((group + 1) * per + k, detrain[k])
        cols.put((group + 2) * per + k, east[k])
    for t in range(tracers):
        partial = None
        for k in range(levels):
            term = weights[k] * field[t, k]
            partial = term if partial is None else partial + term
            slab = kept[t, k]
            cols.put(k * tracers + t, slab)
            edge_rows(k * tracers + t, slab)
        cols.put(slabs + t, partial)
        edge_rows(slabs + t, partial)
    ascending = flags[ASCENDING]
    forward[...] = ring[1 - ascending]
    back[...] = ring[ascending]
    columns[:column_rows] = cols.get(column_rows)


def second_kernel(
    tracers, levels, rows, flags, first, second, detrain, mix, east, north, pole,
    own_forward, own_back, own_columns, forward, back, eastern, western,
    late, coefs, edges, turned,
):
    slabs = tracers * levels
    base = slabs + tracers + 1
    per = LANES // rows
    group = -(-base // per)
    ascending = flags[ASCENDING] == 1
    from_north = jnp.where(ascending, back[...], forward[...])
    from_south = jnp.where(ascending, forward[...], back[...])
    own_north = jnp.where(ascending, own_forward[...], own_back[...])
    own_south = jnp.where(ascending, own_back[...], own_forward[...])
    edges[0] = from_north
    edges[1] = from_south
    sides = sides_of(eastern[...], western[...])
    mine = own_columns[...]
    around = turn(sides)
    turned[...] = around
    lane, row = lane_and_row(rows)
    top, bottom = flags[TOP] == 1, flags[BOTTOM] == 1
    is_top = jnp.logical_and(row == rows - 1, top)
    is_bottom = jnp.logical_and(row == 0, bottom)
    west_row = lane_and_row(2)[1] == 1
    groups = tracers // per
    zero = jnp.zeros((1, LANES), F32)
    add_north = add_south = spread_north = spread_south = less_north = less_south = 0.0
    add_sides = [0.0] * groups
    spread_sides = less_sides = 0.0
    for k in range(levels):
        place = base + 2 * levels + k
        wind = east[k]
        behind = jnp.where(lane == 0, side_of(around, (group + 2) * per + k, rows), pltpu.roll(wind, 1, 1))
        to_east = jnp.maximum(wind, 0.0)
        to_west = jnp.maximum(-behind, 0.0)
        wind = north[k]
        pole_north = jnp.where(top, jnp.maximum(-from_north[place : place + 1], 0.0), zero)
        to_north = jnp.maximum(wind, 0.0) + jnp.where(is_top, pole_north, 0.0)
        below = from_south[place : place + 1]
        pole_south = jnp.maximum(pole[k : k + 1, :], 0.0) + jnp.maximum(-below, 0.0)
        behind = jnp.where(row == 0, below, pltpu.roll(wind, 1, 0))
        to_south = jnp.where(is_bottom, pole_south, jnp.maximum(-behind, 0.0))
        for i, c in enumerate([1.0 - to_east - to_west - to_north - to_south, to_east, to_west, to_north, to_south]):
            coefs[i, k] = c

        level = slice(k * tracers, (k + 1) * tracers)
        weight = detrain[k, rows - 1 : rows, :]
        taken, given = weight * to_north[rows - 1 : rows], weight * pole_north
        add_north = add_north + taken * from_north[level] - given * own_north[level]
        spread_north = spread_north + taken * from_north[base + k : base + k + 1]
        less_north = less_north - given * mix[k, rows - 1 : rows, :]
        taken = detrain[k, :1, :] * to_south[:1]
        add_south = add_south + taken * (from_south[level] - own_south[level])
        spread_south = spread_south + taken * from_south[base + k : base + k + 1]
        less_south = less_south - taken * mix[k, :1, :]

        winds = slice(2 * (group + 2), 2 * (group + 3))
        shares = slice(2 * group, 2 * (group + 1))
        weight = tiled(mine[2 * (group + 1) : 2 * (group + 2)], rows, k)
        wind = jnp.where(west_row, jnp.maximum(-sides[winds], 0.0), jnp.maximum(mine[winds], 0.0))
        taken = weight * tiled(wind, rows, k)
        given = jnp.where(west_row, taken, 0.0)
        for g in range(groups):
            pair = slice(2 * (k * groups + g), 2 * (k * groups + g + 1))
            add_sides[g] = add_sides[g] + taken * sides[pair] - given * mine[pair]
        spread_sides = spread_sides + taken * tiled(sides[shares], rows, k)
        less_sides = less_sides - given * tiled(mine[shares], rows, k)
    parts = [sides[2 * (slabs // per) : 2 * group]] + add_sides
    parts += [spread_sides, less_sides, spread_north, spread_south, less_north, less_south]
    parts += [add_north, add_south, from_north[slabs : slabs + tracers + 1], from_south[slabs : slabs + tracers + 1]]
    at = 0
    for part in parts:
        late[at : at + part.shape[0]] = part
        at += part.shape[0]
    if at < late.shape[0]:
        late[at:] = jnp.zeros((late.shape[0] - at, LANES), F32)


def pieces(x):
    high = x.astype(jnp.bfloat16)
    return [high, (x - high.astype(F32)).astype(jnp.bfloat16)]


def product(a, b):
    return lax.dot_general(a, b, (((1,), (1,)), ((), ())), preferred_element_type=F32)


def forcing_kernel(levels, rows, steps, flags, slots, detrain, mix, coefs, edges, turned, base, grids, edge_rows, sums):
    parts = min(8, slots.shape[0])
    count = parts * LANES
    per = LANES // rows
    row_ids = lax.broadcasted_iota(jnp.int32, (rows, count), 0)
    lane_ids = lax.broadcasted_iota(jnp.int32, (LANES, count), 0)
    group = -(-base // per)

    def add_block(index, carry):
        late, early, ring_sides = carry
        block = jnp.concatenate([slots[parts * index + part] for part in range(parts)], axis=1)
        results = []
        for step in range(steps):
            first = step * (levels + 2)
            values = [block[first + k : first + k + 1] for k in range(levels)]
            owner = block[first + levels : first + levels + 1].astype(jnp.int32)
            cell = block[first + levels + 1 : first + levels + 2].astype(jnp.int32)
            slot_row, slot_lane = cell // LANES, cell % LANES
            lanes = (lane_ids == slot_lane).astype(F32).astype(jnp.bfloat16)
            here = jnp.logical_and(row_ids == slot_row, owner == flags[SELF])
            left = [jnp.where(here, value, 0.0) for value in values]
            if step == steps - 1:
                in_north = jnp.logical_and(owner == flags[NORTH], slot_row == flags[NORTH_ROW])
                in_south = jnp.logical_and(owner == flags[SOUTH], slot_row == flags[SOUTH_ROW])
                left += [jnp.where(in_north, value, 0.0) for value in values]
                left += [jnp.where(in_south, value, 0.0) for value in values]
                left += [jnp.zeros((8 - 2 * levels, count), F32)]
            left = jnp.concatenate(left, axis=0)
            results.append(sum(product(piece, lanes) for piece in pieces(left)))
            if step == steps - 1:
                in_east = jnp.logical_and(owner == flags[EAST], slot_lane == 0)
                in_west = jnp.logical_and(owner == flags[WEST], slot_lane == LANES - 1)
                right = [jnp.where(in_east, value, 0.0) for value in values]
                right += [jnp.where(in_west, value, 0.0) for value in values]
                right += [jnp.zeros((8 - 2 * levels, count), F32)]
                right = jnp.concatenate(right, axis=0)
                at_row = (row_ids == slot_row).astype(F32).astype(jnp.bfloat16)
                ring_sides = ring_sides + sum(product(at_row, piece) for piece in pieces(right))
        return late + results[1], early + results[0], ring_sides

    late, early, ring_sides = lax.fori_loop(
        0,
        slots.shape[0] // parts,
        add_block,
        (
            jnp.zeros((levels * rows + 8, LANES), F32),
            jnp.zeros((levels * rows, LANES), F32),
            jnp.zeros((rows, 8), F32),
        ),
        unroll=slots.shape[0] // parts <= 2,
    )
    lane, _ = lane_and_row(rows)
    north_rows = late[levels * rows : levels * rows + levels]
    south_rows = late[levels * rows + levels : levels * rows + 2 * levels]
    edge_rows[...] = late[levels * rows :]
    around = turned[...]
    at_end = at_first = None
    ring = jnp.zeros((rows, LANES), F32)
    ring_north = jnp.zeros((1, LANES), F32)
    ring_south = jnp.zeros((1, LANES), F32)
    for k in range(levels):
        own = late[k * rows : (k + 1) * rows]
        now = early[k * rows : (k + 1) * rows]
        east_side = jnp.broadcast_to(ring_sides[:, k : k + 1], (rows, LANES))
        west_side = jnp.broadcast_to(ring_sides[:, levels + k : levels + k + 1], (rows, LANES))
        side = jnp.where(lane == LANES - 1, east_side, jnp.where(lane == 0, west_side, 0.0))
        grids[k] = own
        grids[levels + k] = now
        grids[2 * levels + k] = side
        mix_side = side_of(around, group * per + k, rows)
        detrain_side = side_of(around, (group + 1) * per + k, rows)
        north, south = north_rows[k : k + 1], south_rows[k : k + 1]
        moved = stencil(
            [coefs[i, k] for i in range(5)],
            (1.0 - mix[k]) * own,
            (1.0 - mix_side) * side,
            (1.0 - edges[0, base + k : base + k + 1, :]) * north,
            (1.0 - edges[1, base + k : base + k + 1, :]) * south,
        )
        first = detrain[k] * own
        second = detrain[k] * (moved + now)
        at_first = first if at_first is None else at_first + first
        at_end = second if at_end is None else at_end + second
        ring = ring + detrain_side * side
        place = base + levels + k
        ring_north = ring_north + edges[0, place : place + 1, :] * north
        ring_south = ring_south + edges[1, place : place + 1, :] * south
    sums[:rows] = at_first
    sums[rows : 2 * rows] = at_end
    flat = jnp.transpose(jnp.concatenate([ring] + [jnp.zeros((rows, LANES), F32)] * (per - 1), axis=0))
    sums[2 * rows :] = jnp.concatenate(
        [ring_north, ring_south, flat[LANES - 1 :], flat[:1], jnp.zeros((4, LANES), F32)], axis=0
    )


def third_kernel(
    tracers, levels, rows, flags, field, mix, coefs, edges, turned, mine, other, moved_out, column_out, inverse_out, first,
):
    half = tracers // 2
    parity = flags[PARITY]
    first[parity] = mine[...]
    first[1 - parity] = other[...]
    total = jnp.concatenate([first[0, half * rows :, :], first[1, half * rows :, :]], axis=0)
    inverse = 1.0 / total
    inverse_out[...] = inverse
    around = turned[...]
    stay = [1.0 - mix[k] for k in range(levels)]
    five = [[coefs[i, k] for i in range(5)] for k in range(levels)]
    for t in range(tracers):
        column = first[t // half, (t % half) * rows : (t % half + 1) * rows, :] * inverse
        column_out[t] = column
        for k in range(levels):
            place = k * tracers + t
            moved = stencil(
                five[k],
                stay[k] * field[t, k] + mix[k] * column,
                side_of(around, place, rows),
                edges[0, place : place + 1, :],
                edges[1, place : place + 1, :],
            )
            moved_out[t, k] = stay[k] * moved


def fourth_kernel(
    tracers, levels, rows, flags, moved, column, inverse_in, mix, coefs, edges, turned, grids, edge_rows,
    mine, other, forced_1, forced_2, forced_3, forced_4, mixed_out, forward, back, columns, second, ring,
):
    half = tracers // 2
    slabs = tracers * levels
    base = slabs + tracers + 1
    per = LANES // rows
    group = -(-base // per)
    groups = tracers // per
    parity = flags[LATER_PARITY]
    second_rows = second.shape[1]
    second[parity] = mine[:second_rows]
    second[1 - parity] = other[:second_rows]
    late = mine[second_rows:] + other[second_rows:]
    forced = (forced_1[...] + forced_2[...]) + (forced_3[...] + forced_4[...])
    inverse = inverse_in[...]
    lane, row = lane_and_row(rows)
    at_side = jnp.logical_or(lane == 0, lane == LANES - 1)
    last, initial = row == rows - 1, row == 0

    at = 2 * (group - slabs // per)
    inverse_side = 1.0 / tiled(late[2 * groups : 2 * groups + 2], rows)
    forced_sides = tiled(forced[2 * rows + 2 : 2 * rows + 4], rows)
    side_rows = [(late[2 * g : 2 * g + 2] + forced_sides) * inverse_side for g in range(groups)]
    side_rows += [late[at : at + 2 * groups + 4]]
    at += 2 * groups + 4
    around_late = turn(jnp.concatenate(side_rows, axis=0))
    spread_side = side_of(around_late, 2 * groups * per, rows)
    less_side = side_of(around_late, (2 * groups + 1) * per, rows)
    north, south, less_north, less_south = [late[at + i : at + i + 1] for i in range(4)]
    at += 4
    add_ends = [late[at + e * tracers : at + (e + 1) * tracers] for e in range(2)]
    at += 2 * tracers
    column_ends = []
    for e in range(2):
        sums = late[at : at + tracers + 1]
        column_ends.append((sums[:tracers] + forced[2 * rows + e : 2 * rows + e + 1]) / sums[tracers:])
        at += tracers + 1

    spread = []
    start = half * rows
    for i in range(5):
        at = start + i * (rows // 2)
        spread.append(jnp.concatenate([second[h, at : at + rows // 2, :] for h in range(2)], axis=0))
    spread[0] = spread[0] + jnp.where(last, less_north, 0.0) + jnp.where(initial, less_south, 0.0)
    spread[0] = spread[0] + jnp.where(lane == 0, less_side, 0.0)
    spread[1] = jnp.where(lane == LANES - 1, spread_side, spread[1])
    spread[2] = spread[2] + jnp.where(lane == 0, spread_side, 0.0)
    spread[3] = jnp.where(last, north, spread[3])
    spread[4] = spread[4] + jnp.where(initial, south, 0.0)

    forced_column = forced[:rows] * inverse
    forced_later = forced[rows : 2 * rows]
    around = turned[...]
    stay = [1.0 - mix[k] for k in range(levels)]
    forced_moved, to_sides, to_ends = [], [], []
    for k in range(levels):
        five = [coefs[i, k] for i in range(5)]
        mix_side = side_of(around, group * per + k, rows)
        shares = [edges[e, base + k : base + k + 1, :] for e in range(2)]
        ends = [(1.0 - shares[e]) * edge_rows[e * levels + k : e * levels + k + 1, :] for e in range(2)]
        moved_forcing = stencil(
            five,
            stay[k] * grids[k] + mix[k] * forced_column,
            (1.0 - mix_side) * grids[2 * levels + k],
            ends[0],
            ends[1],
        )
        forced_moved.append(stay[k] * (moved_forcing + grids[levels + k]))
        to_side = jnp.where(lane == LANES - 1, five[1], jnp.where(lane == 0, five[2], 0.0))
        to_sides.append(stay[k] * to_side * mix_side)
        to_ends.append(
            [
                jnp.where(last, stay[k] * five[3] * shares[0], 0.0)[rows - 8 :],
                jnp.where(initial, stay[k] * five[4] * shares[1], 0.0)[:8],
            ]
        )

    cols = Columns(rows)
    ring[...] = jnp.zeros(ring.shape, F32)
    for t in range(tracers):
        h, at = t // half, (t % half) * rows
        column_side = side_of(around_late, t, rows)
        column_north, column_south = column_ends[0][t : t + 1], column_ends[1][t : t + 1]
        later = second[h, at : at + rows, :] + forced_later
        later = later + jnp.where(at_side, side_of(around_late, (groups + t // per) * per + t % per, rows), 0.0)
        later = later + jnp.where(last, add_ends[0][t : t + 1], 0.0)
        later = later + jnp.where(initial, add_ends[1][t : t + 1], 0.0)
        later = later + stencil(spread, column[t] + forced_column, column_side, column_north, column_south)
        later = later * inverse
        for k in range(levels):
            place = k * tracers + t
            mixed = moved[t, k] + forced_moved[k] + mix[k] * later + to_sides[k] * column_side
            mixed = jnp.concatenate(
                [
                    mixed[:8] + to_ends[k][1] * column_south,
                    mixed[8 : rows - 8],
                    mixed[rows - 8 :] + to_ends[k][0] * column_north,
                ],
                axis=0,
            )
            mixed_out[t, k] = mixed
            cols.put(place, mixed)
            ring[0, place : place + 1, :] = mixed[rows - 1 : rows]
            ring[1, place : place + 1, :] = mixed[:1]
    ascending = flags[ASCENDING]
    forward[...] = ring[1 - ascending]
    back[...] = ring[ascending]
    columns[...] = cols.get(columns.shape[0])


def inner_kernel(tracers, levels, rows, flags, mixed, coefs, out):
    lane, row = lane_and_row(rows)
    for k in range(levels):
        own, to_east, to_west, to_north, to_south = [coefs[i, k] for i in range(5)]
        five = [
            own,
            jnp.where(lane == LANES - 1, 0.0, to_east),
            jnp.where(lane == 0, 0.0, to_west),
            jnp.where(row == rows - 1, 0.0, to_north),
            jnp.where(row == 0, 0.0, to_south),
        ]
        for t in range(tracers):
            slab = mixed[t, k]
            total = None
            for c, x in zip(five, (slab,) + turned_round(slab)):
                total = c * x if total is None else total + c * x
            out[t, k] = total


def last_kernel(tracers, levels, rows, flags, inner, coefs, forward, back, eastern, western, out, result, sems):
    ascending = flags[ASCENDING] == 1
    from_north = jnp.where(ascending, back[...], forward[...])
    from_south = jnp.where(ascending, forward[...], back[...])
    around = turn(sides_of(eastern[...], western[...]))
    lane, row = lane_and_row(rows)
    last, initial = row == rows - 1, row == 0
    to_sides = [
        jnp.where(lane == LANES - 1, coefs[1, k], jnp.where(lane == 0, coefs[2, k], 0.0)) for k in range(levels)
    ]
    to_north = [jnp.where(last, coefs[3, k], 0.0)[rows - 8 :] for k in range(levels)]
    to_south = [jnp.where(initial, coefs[4, k], 0.0)[:8] for k in range(levels)]
    copies = []
    for t in range(tracers):
        for k in range(levels):
            place = k * tracers + t
            total = inner[t, k] + to_sides[k] * side_of(around, place, rows)
            result[t, k, :8, :] = total[:8] + to_south[k] * from_south[place : place + 1]
            result[t, k, 8 : rows - 8, :] = total[8 : rows - 8]
            result[t, k, rows - 8 :, :] = total[rows - 8 :] + to_north[k] * from_north[place : place + 1]
        copy = pltpu.make_async_copy(result.at[t], out.at[t], sems.at[t])
        copy.start()
        copies.append(copy)
    for copy in copies:
        copy.wait()


def up8(count):
    return -(-count // 8) * 8


def call(kernel, scalars, args, outs, scratch=(), placed=(), copies=0, placed_out=False, weight=0):
    vmem, free = pl.BlockSpec(memory_space=pltpu.VMEM), pl.BlockSpec(memory_space=pl.ANY)
    return pl.pallas_call(
        kernel,
        out_shape=[jax.ShapeDtypeStruct(shape, F32) for shape in outs],
        in_specs=[pl.BlockSpec(memory_space=pltpu.SMEM)] * len(scalars) + [free] * len(placed) + [vmem] * len(args),
        out_specs=[free if placed_out else vmem] * len(outs),
        scratch_shapes=[pltpu.VMEM(x.shape, x.dtype) if hasattr(x, "dtype") else pltpu.VMEM(x, F32) for x in scratch]
        + ([pltpu.SemaphoreType.DMA((copies,))] if copies else []),
        compiler_params=pltpu.CompilerParams(vmem_limit_bytes=16 * 1024 * 1024),
        cost_estimate=pl.CostEstimate(flops=int(weight * 1e9), bytes_accessed=0, transcendentals=0),
    )(*scalars, *placed, *args)


def on_device(
    adjoint_field,
    east_courant,
    north_courant,
    pole_courant,
    mix_fraction,
    detrain_share,
    sounding_owner,
    sounding_cell,
    sounding_count,
    sounding_forcing,
):
    lon_count, lat_count = lax.axis_size("lon"), lax.axis_size("lat")
    lon, lat, lev = lax.axis_index("lon"), lax.axis_index("lat"), lax.axis_index("lev")
    tracers, levels, rows, lanes = adjoint_field.shape
    steps, slot_count = sounding_cell.shape
    slabs = tracers * levels
    base = slabs + tracers + 1
    per = lanes // rows
    size = (tracers, levels, rows)

    top, bottom = lat == lat_count - 1, lat == 0
    partner = (lon + lon_count // 2) % lon_count
    flags = [
        top,
        bottom,
        lon < lon_count // 2,
        lev & 1,
        lon * lat_count + lat,
        jnp.where(top, partner * lat_count + lat, lon * lat_count + lat + 1),
        jnp.where(bottom, partner * lat_count + lat, lon * lat_count + lat - 1),
        (lon + 1) % lon_count * lat_count + lat,
        (lon + lon_count - 1) % lon_count * lat_count + lat,
        jnp.where(top, rows - 1, 0),
        jnp.where(bottom, 0, rows - 1),
        (lev ^ (lev >> 1)) & 1,
    ]
    flags = jnp.stack([jnp.asarray(flag, jnp.int32) for flag in flags])

    ring_rows = up8(base + 3 * levels)
    column_rows = up8(2 * (-(-base // per) + 3))
    slot_rows = up8(steps * (levels + 2))
    first_rows = tracers // 2 * rows + rows // 2
    second_rows = tracers // 2 * rows + 5 * (rows // 2)
    soundings = [
        jnp.swapaxes(sounding_count, 0, 1),
        jnp.swapaxes(sounding_owner, 1, 2),
        sounding_cell,
        jnp.swapaxes(sounding_forcing, 0, 1),
    ]
    inputs = [detrain_share, adjoint_field, mix_fraction, east_courant, north_courant, pole_courant]
    keep_first, send_first, slots, detrain, field, mix, east, north, pole = call(
        functools.partial(first_kernel, *size),
        [flags],
        [],
        [(first_rows, lanes)] * 2 + [(slot_count // lanes * slot_rows, lanes)] + [x.shape for x in inputs],
        [(2, first_rows, lanes)] + soundings,
        [pltpu.with_memory_space_constraint(x, pltpu.HBM) for x in soundings + inputs],
        tracers - 1 + len(soundings) + len(inputs),
    )
    static = [detrain, mix, east, north, pole]
    kept = (1.0 - mix)[None] * field
    own_forward, own_back, columns = call(
        functools.partial(edge_kernel, *size),
        [flags],
        [slots, field, kept] + static,
        [(ring_rows, lanes)] * 2 + [(column_rows + slots.shape[0], lanes)],
        [(2, ring_rows, lanes)],
        weight=WEIGHTS[1],
    )
    keep_second, send_second = call(
        functools.partial(inside_kernel, *size),
        [flags],
        [field, kept, detrain, mix, east, north],
        [(second_rows, lanes)] * 2,
        [(2, second_rows, lanes)],
        [columns],
        weight=WEIGHTS[0],
    )
    first = add(keep_first, swap_over(send_first, "lev", 1))
    second = add(keep_second, swap_over(send_second, "lev", 1))
    eastern, western = exchange_columns(columns)
    forward, back = exchange_rows(own_forward, own_back)
    other_first = swap_over(first, "lev", 2)

    late_rows = 2 * (-(-base // per) - slabs // per) + 2 * (tracers // per) + 8 + 4 * tracers + 2
    late, coefs, edges, turned = call(
        functools.partial(second_kernel, *size),
        [flags],
        static
        + [own_forward, own_back, columns[:column_rows]]
        + [forward, back, eastern[:column_rows], western[:column_rows]],
        [(up8(late_rows), lanes), (5, levels, rows, lanes), (2, ring_rows, lanes), (lanes, lanes)],
        placed=[first, second],
        weight=WEIGHTS[2],
    )
    second = jnp.concatenate([second, late], axis=0)
    other_second = swap_over(second, "lev", 3)
    slots = columns[column_rows:][None]
    if lon_count == 2:
        slots = pair(columns[column_rows:], eastern[column_rows:], first)
    else:
        slots = gather_blocks(slots, "lon")
    slots = gather_blocks(slots, "lat").reshape(-1, slot_rows, lanes)
    grids, edge_rows, sums = call(
        lambda *refs: forcing_kernel(levels, rows, steps, *refs[:7], base, *refs[7:]),
        [flags],
        [slots, detrain, mix, coefs, edges, turned],
        [(3 * levels, rows, lanes), (8, lanes), (2 * rows + 8, lanes)],
        weight=WEIGHTS[3],
    )
    sums = [sums] + [swap_over(sums, "lev", bit) for bit in (1, 2, 3)]
    first = add(first, other_first, sums[0])
    other_first = swap_over(first, "lev", 1)
    second = add(second, other_second, first)
    other_second = swap_over(second, "lev", 1)

    moved, column, inverse = call(
        functools.partial(third_kernel, *size),
        [flags],
        [field, mix, coefs, edges, turned, first, other_first],
        [adjoint_field.shape, (tracers, rows, lanes), (rows, lanes)],
        [(2, first_rows, lanes)],
        weight=WEIGHTS[4],
    )
    slab_rows = up8(slabs)
    mixed, forward, back, columns = call(
        functools.partial(fourth_kernel, *size),
        [flags],
        [
            moved, column, inverse, mix, coefs, edges, turned, grids, edge_rows,
            second, other_second, *sums,
        ],
        [adjoint_field.shape] + [(slab_rows, lanes)] * 2 + [(up8(2 * (slabs // per)), lanes)],
        [(2, second_rows, lanes), (2, slab_rows, lanes)],
    )
    eastern, western = exchange_columns(columns)
    forward, back = exchange_rows(forward, back)
    (inner,) = call(functools.partial(inner_kernel, *size), [flags], [mixed, coefs], [adjoint_field.shape])
    (out,) = call(
        functools.partial(last_kernel, *size),
        [flags],
        [inner, coefs, forward, back, eastern, western],
        [adjoint_field.shape],
        [adjoint_field.shape],
        copies=tracers,
        placed_out=True,
    )
    return out


def solution(mesh):
    return jax.shard_map(
        on_device,
        mesh=mesh,
        in_specs=(
            P(None, "lev", "lat", "lon"),
            P("lev", "lat", "lon"),
            P("lev", "lat", "lon"),
            P("lev", "lon"),
            P("lev", "lat", "lon"),
            P("lev", "lat", "lon"),
            P(None, ("lon", "lat"), None),
            P(None, ("lon", "lat")),
            P(None, ("lon", "lat")),
            P(None, "lev", ("lon", "lat")),
        ),
        out_specs=P(None, "lev", "lat", "lon"),
        check_vma=False,
    )
```

```python
import functools

import jax
import jax.numpy as jnp
from jax import lax
from jax.experimental import pallas as pl
from jax.experimental.pallas import tpu as pltpu
from jax.sharding import PartitionSpec as P

F32 = jnp.float32
WEIGHTS = [0, 0, 0, 20, 20]
LANES = 128
TOP, BOTTOM, ASCENDING, PARITY, SELF, NORTH, SOUTH, EAST, WEST, NORTH_ROW, SOUTH_ROW, LATER_PARITY = range(12)


def swap_over(value, axis, bit):
    return lax.ppermute(value, axis, [(i, i ^ bit) for i in range(lax.axis_size(axis))])


def shift_over(value, axis, steps):
    count = lax.axis_size(axis)
    return lax.ppermute(value, axis, [(i, (i + steps) % count) for i in range(count)])


def meridian_rings(lon_count, lat_count, steps):
    pairs = []
    for lon in range(lon_count // 2):
        ring = [lon * lat_count + lat for lat in range(lat_count)]
        ring += [(lon + lon_count // 2) * lat_count + lat for lat in reversed(range(lat_count))]
        pairs += [(ring[i], ring[(i + steps) % len(ring)]) for i in range(len(ring))]
    return pairs


def exchange_rows(forward, back):
    lon_count, lat_count = lax.axis_size("lon"), lax.axis_size("lat")
    return (
        lax.ppermute(forward, ("lon", "lat"), meridian_rings(lon_count, lat_count, 1)),
        lax.ppermute(back, ("lon", "lat"), meridian_rings(lon_count, lat_count, -1)),
    )


def exchange_columns(columns):
    if lax.axis_size("lon") == 2:
        other = swap_over(columns, "lon", 1)
        return other, other
    return shift_over(columns, "lon", -1), shift_over(columns, "lon", 1)


def pair_kernel(a, b, *refs):
    refs[-1][0] = a[...]
    refs[-1][1] = b[...]


def pair(a, b, *after):
    vmem = pl.BlockSpec(memory_space=pltpu.VMEM)
    return pl.pallas_call(
        pair_kernel,
        out_shape=jax.ShapeDtypeStruct((2, *a.shape), a.dtype),
        in_specs=[vmem, vmem] + [pl.BlockSpec(memory_space=pl.ANY)] * len(after),
        out_specs=vmem,
        compiler_params=pltpu.CompilerParams(vmem_limit_bytes=4 * 1024 * 1024),
    )(a, b, *after)


def gather_blocks(blocks, axis):
    count = lax.axis_size(axis)
    if count not in (2, 4):
        return lax.all_gather(blocks, axis, axis=0, tiled=True)
    return jnp.concatenate([blocks] + [swap_over(blocks, axis, bit) for bit in range(1, count)], axis=0)


def add_kernel(waited, a, b, *refs):
    refs[-1][...] = a[...] + b[...]


def add(a, b, *after):
    vmem = pl.BlockSpec(memory_space=pltpu.VMEM)
    return pl.pallas_call(
        functools.partial(add_kernel, len(after)),
        out_shape=jax.ShapeDtypeStruct(a.shape, a.dtype),
        in_specs=[vmem, vmem] + [pl.BlockSpec(memory_space=pl.ANY)] * len(after),
        out_specs=vmem,
        compiler_params=pltpu.CompilerParams(vmem_limit_bytes=4 * 1024 * 1024),
    )(a, b, *after)


def lane_and_row(rows):
    return (
        lax.broadcasted_iota(jnp.int32, (rows, LANES), 1),
        lax.broadcasted_iota(jnp.int32, (rows, LANES), 0),
    )


def shifted(x, side, north, south):
    rows = x.shape[0]
    lane, row = lane_and_row(rows)
    east = jnp.where(lane == LANES - 1, side, pltpu.roll(x, LANES - 1, 1))
    west = jnp.where(lane == 0, side, pltpu.roll(x, 1, 1))
    above = jnp.where(row == rows - 1, north, pltpu.roll(x, rows - 1, 0))
    below = jnp.where(row == 0, south, pltpu.roll(x, 1, 0))
    return east, west, above, below


def turned_round(x):
    rows = x.shape[0]
    return pltpu.roll(x, LANES - 1, 1), pltpu.roll(x, 1, 1), pltpu.roll(x, rows - 1, 0), pltpu.roll(x, 1, 0)


def stencil(coefs, x, side, north, south):
    east, west, above, below = shifted(x, side, north, south)
    own, to_east, to_west, to_north, to_south = coefs
    return own * x + to_east * east + to_west * west + to_north * above + to_south * below


class Columns:
    def __init__(self, rows):
        self.rows = rows
        self.per = LANES // rows
        self.blocks = [jnp.zeros((rows, LANES), F32)] * self.per
        self.lane = lane_and_row(rows)[0]

    def put(self, index, slab):
        group, place = divmod(index, self.per)
        turned = pltpu.roll(slab, 2 * group + 1, 1)
        self.blocks[place] = jnp.where(self.lane // 2 == group, turned, self.blocks[place])

    def get(self, rows):
        return jnp.transpose(jnp.concatenate(self.blocks, axis=0))[:rows]


def sides_of(eastern, western):
    rows = eastern.shape[0]
    row = lane_and_row(rows)[1]
    return jnp.where(row % 2 == 0, pltpu.roll(eastern, rows - 1, 0), pltpu.roll(western, 1, 0))


def turn(rows):
    pad = jnp.zeros((LANES - rows.shape[0], LANES), F32)
    return jnp.transpose(jnp.concatenate([rows, pad], axis=0))


def side_of(turned, index, rows):
    group, place = divmod(index, LANES // rows)
    return pltpu.roll(turned[place * rows : (place + 1) * rows], (LANES - 2 * group - 1) % LANES, 1)


def tiled(x, rows, block=0):
    if block:
        x = pltpu.roll(x, LANES - block * rows, 1)
    x = jnp.where(lax.broadcasted_iota(jnp.int32, x.shape, 1) < rows, x, 0.0)
    width = rows
    while width < LANES:
        x = x + pltpu.roll(x, width, 1)
        width *= 2
    return x


def first_kernel(
    tracers, levels, rows, flags, counts_in, owners_in, cells_in, forcing_in, detrain_in, field_in, mix_in, east_in,
    north_in, pole_in, keep, send, slots, detrain, field, mix, east, north, pole,
    halves, counts, owners, cells, forcing, sems,
):
    pairs = [(counts_in, counts), (owners_in, owners), (cells_in, cells), (forcing_in, forcing), (detrain_in, detrain)]
    pairs += [(field_in.at[t], field.at[t]) for t in range(tracers)]
    pairs += [(mix_in, mix), (east_in, east), (north_in, north), (pole_in, pole)]
    copies = [pltpu.make_async_copy(source, target, sems.at[i]) for i, (source, target) in enumerate(pairs)]
    for copy in copies:
        copy.start()
    half = tracers // 2
    slots[...] = jnp.zeros(slots.shape, F32)
    for copy in copies[:5]:
        copy.wait()
    steps, slot_count = cells.shape
    slot_rows = slots.shape[0] * LANES // slot_count
    slot = lax.broadcasted_iota(jnp.int32, (levels, LANES), 1)
    for part in range(slot_count // LANES):
        lanes = slice(part * LANES, (part + 1) * LANES)
        for step in range(steps):
            at = part * slot_rows + step * (levels + 2)
            live = slot + part * LANES < jnp.broadcast_to(counts[:, step : step + 1], slot.shape)
            slots[at : at + levels, :] = jnp.where(live, forcing[:, step, lanes], 0.0)
            slots[at + levels : at + levels + 1, :] = owners[step, :, lanes].astype(F32)
            slots[at + levels + 1 : at + levels + 2, :] = cells[step : step + 1, lanes].astype(F32)
    weights = [detrain[k] for k in range(levels)]
    total = functools.reduce(lambda p, q: p + q, weights)
    for h in range(2):
        halves[h, half * rows :, :] = total[h * rows // 2 : (h + 1) * rows // 2]
    for t in range(tracers):
        copies[5 + t].wait()
        at = (t % half) * rows
        halves[t // half, at : at + rows, :] = functools.reduce(
            lambda p, q: p + q, [weights[k] * field[t, k] for k in range(levels)]
        )
    parity = flags[PARITY]
    keep[...] = halves[parity]
    send[...] = halves[1 - parity]
    for copy in copies[5 + tracers :]:
        copy.wait()


def inside_kernel(tracers, levels, rows, flags, after, field, kept, detrain, mix, east, north, keep, send, halves):
    half = tracers // 2
    lane, row = lane_and_row(rows)
    inside, spread = [], None
    for k in range(levels):
        weight = detrain[k]
        to_east = jnp.maximum(east[k], 0.0)
        to_west = jnp.where(lane == 0, 0.0, jnp.maximum(-pltpu.roll(east[k], 1, 1), 0.0))
        to_north = jnp.maximum(north[k], 0.0)
        to_south = jnp.where(row == 0, 0.0, jnp.maximum(-pltpu.roll(north[k], 1, 0), 0.0))
        five = [
            1.0 - to_east - to_west - to_north - to_south,
            jnp.where(lane == LANES - 1, 0.0, to_east),
            to_west,
            jnp.where(row == rows - 1, 0.0, to_north),
            to_south,
        ]
        inside.append([weight * c for c in five])
        terms = [c * s for c, s in zip(inside[k], (mix[k],) + turned_round(mix[k]))]
        spread = terms if spread is None else [p + q for p, q in zip(spread, terms)]
    for i in range(5):
        for h in range(2):
            at = half * rows + i * (rows // 2)
            halves[h, at : at + rows // 2, :] = spread[i][h * rows // 2 : (h + 1) * rows // 2]
    for t in range(tracers):
        total = None
        for k in range(levels):
            slab = kept[t, k]
            for c, x in zip(inside[k], (slab,) + turned_round(slab)):
                total = c * x if total is None else total + c * x
        at = (t % half) * rows
        halves[t // half, at : at + rows, :] = total
    parity = flags[LATER_PARITY]
    keep[...] = halves[parity]
    send[...] = halves[1 - parity]


def edge_kernel(
    tracers, levels, rows, flags, slots, field, kept, detrain, mix, east, north, pole, forward, back, columns, ring
):
    slabs = tracers * levels
    base = slabs + tracers + 1
    per = LANES // rows
    group = -(-base // per)
    column_rows = up8(2 * (group + 3))
    columns[column_rows:] = slots[...]
    ring[...] = jnp.zeros(ring.shape, F32)
    weights = [detrain[k] for k in range(levels)]
    cols = Columns(rows)

    def edge_rows(place, slab):
        ring[0, place : place + 1, :] = slab[rows - 1 : rows]
        ring[1, place : place + 1, :] = slab[:1]

    total = functools.reduce(lambda p, q: p + q, weights)
    cols.put(slabs + tracers, total)
    edge_rows(slabs + tracers, total)
    for k in range(levels):
        edge_rows(base + k, mix[k])
        edge_rows(base + levels + k, detrain[k])
        ring[0, base + 2 * levels + k : base + 2 * levels + k + 1, :] = north[k, rows - 1 : rows, :]
        ring[1, base + 2 * levels + k : base + 2 * levels + k + 1, :] = pole[k : k + 1, :]
        cols.put(group * per + k, mix[k])
        cols.put((group + 1) * per + k, detrain[k])
        cols.put((group + 2) * per + k, east[k])
    for t in range(tracers):
        partial = None
        for k in range(levels):
            term = weights[k] * field[t, k]
            partial = term if partial is None else partial + term
            slab = kept[t, k]
            cols.put(k * tracers + t, slab)
            edge_rows(k * tracers + t, slab)
        cols.put(slabs + t, partial)
        edge_rows(slabs + t, partial)
    ascending = flags[ASCENDING]
    forward[...] = ring[1 - ascending]
    back[...] = ring[ascending]
    columns[:column_rows] = cols.get(column_rows)


def second_kernel(
    tracers, levels, rows, flags, first, detrain, mix, east, north, pole,
    own_forward, own_back, own_columns, forward, back, eastern, western,
    late, coefs, edges, turned,
):
    slabs = tracers * levels
    base = slabs + tracers + 1
    per = LANES // rows
    group = -(-base // per)
    ascending = flags[ASCENDING] == 1
    from_north = jnp.where(ascending, back[...], forward[...])
    from_south = jnp.where(ascending, forward[...], back[...])
    own_north = jnp.where(ascending, own_forward[...], own_back[...])
    own_south = jnp.where(ascending, own_back[...], own_forward[...])
    edges[0] = from_north
    edges[1] = from_south
    sides = sides_of(eastern[...], western[...])
    mine = own_columns[...]
    around = turn(sides)
    turned[...] = around
    lane, row = lane_and_row(rows)
    top, bottom = flags[TOP] == 1, flags[BOTTOM] == 1
    is_top = jnp.logical_and(row == rows - 1, top)
    is_bottom = jnp.logical_and(row == 0, bottom)
    west_row = lane_and_row(2)[1] == 1
    groups = tracers // per
    zero = jnp.zeros((1, LANES), F32)
    add_north = add_south = spread_north = spread_south = less_north = less_south = 0.0
    add_sides = [0.0] * groups
    spread_sides = less_sides = 0.0
    for k in range(levels):
        place = base + 2 * levels + k
        wind = east[k]
        behind = jnp.where(lane == 0, side_of(around, (group + 2) * per + k, rows), pltpu.roll(wind, 1, 1))
        to_east = jnp.maximum(wind, 0.0)
        to_west = jnp.maximum(-behind, 0.0)
        wind = north[k]
        pole_north = jnp.where(top, jnp.maximum(-from_north[place : place + 1], 0.0), zero)
        to_north = jnp.maximum(wind, 0.0) + jnp.where(is_top, pole_north, 0.0)
        below = from_south[place : place + 1]
        pole_south = jnp.maximum(pole[k : k + 1, :], 0.0) + jnp.maximum(-below, 0.0)
        behind = jnp.where(row == 0, below, pltpu.roll(wind, 1, 0))
        to_south = jnp.where(is_bottom, pole_south, jnp.maximum(-behind, 0.0))
        for i, c in enumerate([1.0 - to_east - to_west - to_north - to_south, to_east, to_west, to_north, to_south]):
            coefs[i, k] = c

        level = slice(k * tracers, (k + 1) * tracers)
        weight = detrain[k, rows - 1 : rows, :]
        taken, given = weight * to_north[rows - 1 : rows], weight * pole_north
        add_north = add_north + taken * from_north[level] - given * own_north[level]
        spread_north = spread_north + taken * from_north[base + k : base + k + 1]
        less_north = less_north - given * mix[k, rows - 1 : rows, :]
        taken = detrain[k, :1, :] * to_south[:1]
        add_south = add_south + taken * (from_south[level] - own_south[level])
        spread_south = spread_south + taken * from_south[base + k : base + k + 1]
        less_south = less_south - taken * mix[k, :1, :]

        winds = slice(2 * (group + 2), 2 * (group + 3))
        shares = slice(2 * group, 2 * (group + 1))
        weight = tiled(mine[2 * (group + 1) : 2 * (group + 2)], rows, k)
        wind = jnp.where(west_row, jnp.maximum(-sides[winds], 0.0), jnp.maximum(mine[winds], 0.0))
        taken = weight * tiled(wind, rows, k)
        given = jnp.where(west_row, taken, 0.0)
        for g in range(groups):
            pair = slice(2 * (k * groups + g), 2 * (k * groups + g + 1))
            add_sides[g] = add_sides[g] + taken * sides[pair] - given * mine[pair]
        spread_sides = spread_sides + taken * tiled(sides[shares], rows, k)
        less_sides = less_sides - given * tiled(mine[shares], rows, k)
    parts = [sides[2 * (slabs // per) : 2 * group]] + add_sides
    parts += [spread_sides, less_sides, spread_north, spread_south, less_north, less_south]
    parts += [add_north, add_south, from_north[slabs : slabs + tracers + 1], from_south[slabs : slabs + tracers + 1]]
    at = 0
    for part in parts:
        late[at : at + part.shape[0]] = part
        at += part.shape[0]
    if at < late.shape[0]:
        late[at:] = jnp.zeros((late.shape[0] - at, LANES), F32)


def pieces(x):
    high = x.astype(jnp.bfloat16)
    return [high, (x - high.astype(F32)).astype(jnp.bfloat16)]


def product(a, b):
    return lax.dot_general(a, b, (((1,), (1,)), ((), ())), preferred_element_type=F32)


def forcing_kernel(levels, rows, steps, flags, slots, detrain, mix, coefs, edges, turned, base, grids, edge_rows, sums):
    parts = min(8, slots.shape[0])
    count = parts * LANES
    per = LANES // rows
    row_ids = lax.broadcasted_iota(jnp.int32, (rows, count), 0)
    lane_ids = lax.broadcasted_iota(jnp.int32, (LANES, count), 0)
    group = -(-base // per)

    def add_block(index, carry):
        late, early, ring_sides = carry
        block = jnp.concatenate([slots[parts * index + part] for part in range(parts)], axis=1)
        results = []
        for step in range(steps):
            first = step * (levels + 2)
            values = [block[first + k : first + k + 1] for k in range(levels)]
            owner = block[first + levels : first + levels + 1].astype(jnp.int32)
            cell = block[first + levels + 1 : first + levels + 2].astype(jnp.int32)
            slot_row, slot_lane = cell // LANES, cell % LANES
            lanes = (lane_ids == slot_lane).astype(F32).astype(jnp.bfloat16)
            here = jnp.logical_and(row_ids == slot_row, owner == flags[SELF])
            left = [jnp.where(here, value, 0.0) for value in values]
            if step == steps - 1:
                in_north = jnp.logical_and(owner == flags[NORTH], slot_row == flags[NORTH_ROW])
                in_south = jnp.logical_and(owner == flags[SOUTH], slot_row == flags[SOUTH_ROW])
                left += [jnp.where(in_north, value, 0.0) for value in values]
                left += [jnp.where(in_south, value, 0.0) for value in values]
                left += [jnp.zeros((8 - 2 * levels, count), F32)]
            left = jnp.concatenate(left, axis=0)
            results.append(sum(product(piece, lanes) for piece in pieces(left)))
            if step == steps - 1:
                in_east = jnp.logical_and(owner == flags[EAST], slot_lane == 0)
                in_west = jnp.logical_and(owner == flags[WEST], slot_lane == LANES - 1)
                right = [jnp.where(in_east, value, 0.0) for value in values]
                right += [jnp.where(in_west, value, 0.0) for value in values]
                right += [jnp.zeros((8 - 2 * levels, count), F32)]
                right = jnp.concatenate(right, axis=0)
                at_row = (row_ids == slot_row).astype(F32).astype(jnp.bfloat16)
                ring_sides = ring_sides + sum(product(at_row, piece) for piece in pieces(right))
        return late + results[1], early + results[0], ring_sides

    late, early, ring_sides = lax.fori_loop(
        0,
        slots.shape[0] // parts,
        add_block,
        (
            jnp.zeros((levels * rows + 8, LANES), F32),
            jnp.zeros((levels * rows, LANES), F32),
            jnp.zeros((rows, 8), F32),
        ),
        unroll=slots.shape[0] // parts <= 2,
    )
    lane, _ = lane_and_row(rows)
    north_rows = late[levels * rows : levels * rows + levels]
    south_rows = late[levels * rows + levels : levels * rows + 2 * levels]
    edge_rows[...] = late[levels * rows :]
    around = turned[...]
    at_end = at_first = None
    ring = jnp.zeros((rows, LANES), F32)
    ring_north = jnp.zeros((1, LANES), F32)
    ring_south = jnp.zeros((1, LANES), F32)
    for k in range(levels):
        own = late[k * rows : (k + 1) * rows]
        now = early[k * rows : (k + 1) * rows]
        east_side = jnp.broadcast_to(ring_sides[:, k : k + 1], (rows, LANES))
        west_side = jnp.broadcast_to(ring_sides[:, levels + k : levels + k + 1], (rows, LANES))
        side = jnp.where(lane == LANES - 1, east_side, jnp.where(lane == 0, west_side, 0.0))
        grids[k] = own
        grids[levels + k] = now
        grids[2 * levels + k] = side
        mix_side = side_of(around, group * per + k, rows)
        detrain_side = side_of(around, (group + 1) * per + k, rows)
        north, south = north_rows[k : k + 1], south_rows[k : k + 1]
        moved = stencil(
            [coefs[i, k] for i in range(5)],
            (1.0 - mix[k]) * own,
            (1.0 - mix_side) * side,
            (1.0 - edges[0, base + k : base + k + 1, :]) * north,
            (1.0 - edges[1, base + k : base + k + 1, :]) * south,
        )
        first = detrain[k] * own
        second = detrain[k] * (moved + now)
        at_first = first if at_first is None else at_first + first
        at_end = second if at_end is None else at_end + second
        ring = ring + detrain_side * side
        place = base + levels + k
        ring_north = ring_north + edges[0, place : place + 1, :] * north
        ring_south = ring_south + edges[1, place : place + 1, :] * south
    sums[:rows] = at_first
    sums[rows : 2 * rows] = at_end
    flat = jnp.transpose(jnp.concatenate([ring] + [jnp.zeros((rows, LANES), F32)] * (per - 1), axis=0))
    sums[2 * rows :] = jnp.concatenate(
        [ring_north, ring_south, flat[LANES - 1 :], flat[:1], jnp.zeros((4, LANES), F32)], axis=0
    )


def third_kernel(
    tracers, levels, rows, flags, field, mix, coefs, edges, turned, mine, other, moved_out, column_out, inverse_out, first,
):
    half = tracers // 2
    parity = flags[PARITY]
    first[parity] = mine[...]
    first[1 - parity] = other[...]
    total = jnp.concatenate([first[0, half * rows :, :], first[1, half * rows :, :]], axis=0)
    inverse = 1.0 / total
    inverse_out[...] = inverse
    around = turned[...]
    stay = [1.0 - mix[k] for k in range(levels)]
    five = [[coefs[i, k] for i in range(5)] for k in range(levels)]
    for t in range(tracers):
        column = first[t // half, (t % half) * rows : (t % half + 1) * rows, :] * inverse
        column_out[t] = column
        for k in range(levels):
            place = k * tracers + t
            moved = stencil(
                five[k],
                stay[k] * field[t, k] + mix[k] * column,
                side_of(around, place, rows),
                edges[0, place : place + 1, :],
                edges[1, place : place + 1, :],
            )
            moved_out[t, k] = stay[k] * moved


def fourth_kernel(
    tracers, levels, rows, flags, moved, column, inverse_in, mix, coefs, edges, turned, grids, edge_rows,
    mine, other, forced_1, forced_2, forced_3, forced_4, mixed_out, forward, back, columns, second, ring,
):
    half = tracers // 2
    slabs = tracers * levels
    base = slabs + tracers + 1
    per = LANES // rows
    group = -(-base // per)
    groups = tracers // per
    parity = flags[LATER_PARITY]
    second_rows = second.shape[1]
    second[parity] = mine[:second_rows]
    second[1 - parity] = other[:second_rows]
    late = mine[second_rows:] + other[second_rows:]
    forced = (forced_1[...] + forced_2[...]) + (forced_3[...] + forced_4[...])
    inverse = inverse_in[...]
    lane, row = lane_and_row(rows)
    at_side = jnp.logical_or(lane == 0, lane == LANES - 1)
    last, initial = row == rows - 1, row == 0

    at = 2 * (group - slabs // per)
    inverse_side = 1.0 / tiled(late[2 * groups : 2 * groups + 2], rows)
    forced_sides = tiled(forced[2 * rows + 2 : 2 * rows + 4], rows)
    side_rows = [(late[2 * g : 2 * g + 2] + forced_sides) * inverse_side for g in range(groups)]
    side_rows += [late[at : at + 2 * groups + 4]]
    at += 2 * groups + 4
    around_late = turn(jnp.concatenate(side_rows, axis=0))
    spread_side = side_of(around_late, 2 * groups * per, rows)
    less_side = side_of(around_late, (2 * groups + 1) * per, rows)
    north, south, less_north, less_south = [late[at + i : at + i + 1] for i in range(4)]
    at += 4
    add_ends = [late[at + e * tracers : at + (e + 1) * tracers] for e in range(2)]
    at += 2 * tracers
    column_ends = []
    for e in range(2):
        sums = late[at : at + tracers + 1]
        column_ends.append((sums[:tracers] + forced[2 * rows + e : 2 * rows + e + 1]) / sums[tracers:])
        at += tracers + 1

    spread = []
    start = half * rows
    for i in range(5):
        at = start + i * (rows // 2)
        spread.append(jnp.concatenate([second[h, at : at + rows // 2, :] for h in range(2)], axis=0))
    spread[0] = spread[0] + jnp.where(last, less_north, 0.0) + jnp.where(initial, less_south, 0.0)
    spread[0] = spread[0] + jnp.where(lane == 0, less_side, 0.0)
    spread[1] = jnp.where(lane == LANES - 1, spread_side, spread[1])
    spread[2] = spread[2] + jnp.where(lane == 0, spread_side, 0.0)
    spread[3] = jnp.where(last, north, spread[3])
    spread[4] = spread[4] + jnp.where(initial, south, 0.0)

    forced_column = forced[:rows] * inverse
    forced_later = forced[rows : 2 * rows]
    around = turned[...]
    stay = [1.0 - mix[k] for k in range(levels)]
    forced_moved, to_sides, to_ends = [], [], []
    for k in range(levels):
        five = [coefs[i, k] for i in range(5)]
        mix_side = side_of(around, group * per + k, rows)
        shares = [edges[e, base + k : base + k + 1, :] for e in range(2)]
        ends = [(1.0 - shares[e]) * edge_rows[e * levels + k : e * levels + k + 1, :] for e in range(2)]
        moved_forcing = stencil(
            five,
            stay[k] * grids[k] + mix[k] * forced_column,
            (1.0 - mix_side) * grids[2 * levels + k],
            ends[0],
            ends[1],
        )
        forced_moved.append(stay[k] * (moved_forcing + grids[levels + k]))
        to_side = jnp.where(lane == LANES - 1, five[1], jnp.where(lane == 0, five[2], 0.0))
        to_sides.append(stay[k] * to_side * mix_side)
        to_ends.append(
            [
                jnp.where(last, stay[k] * five[3] * shares[0], 0.0)[rows - 8 :],
                jnp.where(initial, stay[k] * five[4] * shares[1], 0.0)[:8],
            ]
        )

    cols = Columns(rows)
    ring[...] = jnp.zeros(ring.shape, F32)
    for t in range(tracers):
        h, at = t // half, (t % half) * rows
        column_side = side_of(around_late, t, rows)
        column_north, column_south = column_ends[0][t : t + 1], column_ends[1][t : t + 1]
        later = second[h, at : at + rows, :] + forced_later
        later = later + jnp.where(at_side, side_of(around_late, (groups + t // per) * per + t % per, rows), 0.0)
        later = later + jnp.where(last, add_ends[0][t : t + 1], 0.0)
        later = later + jnp.where(initial, add_ends[1][t : t + 1], 0.0)
        later = later + stencil(spread, column[t] + forced_column, column_side, column_north, column_south)
        later = later * inverse
        for k in range(levels):
            place = k * tracers + t
            mixed = moved[t, k] + forced_moved[k] + mix[k] * later + to_sides[k] * column_side
            mixed = jnp.concatenate(
                [
                    mixed[:8] + to_ends[k][1] * column_south,
                    mixed[8 : rows - 8],
                    mixed[rows - 8 :] + to_ends[k][0] * column_north,
                ],
                axis=0,
            )
            mixed_out[t, k] = mixed
            cols.put(place, mixed)
            ring[0, place : place + 1, :] = mixed[rows - 1 : rows]
            ring[1, place : place + 1, :] = mixed[:1]
    ascending = flags[ASCENDING]
    forward[...] = ring[1 - ascending]
    back[...] = ring[ascending]
    columns[...] = cols.get(columns.shape[0])


def inner_kernel(tracers, levels, rows, flags, mixed, coefs, out):
    lane, row = lane_and_row(rows)
    for k in range(levels):
        own, to_east, to_west, to_north, to_south = [coefs[i, k] for i in range(5)]
        five = [
            own,
            jnp.where(lane == LANES - 1, 0.0, to_east),
            jnp.where(lane == 0, 0.0, to_west),
            jnp.where(row == rows - 1, 0.0, to_north),
            jnp.where(row == 0, 0.0, to_south),
        ]
        for t in range(tracers):
            slab = mixed[t, k]
            total = None
            for c, x in zip(five, (slab,) + turned_round(slab)):
                total = c * x if total is None else total + c * x
            out[t, k] = total


def last_kernel(tracers, levels, rows, flags, inner, coefs, forward, back, eastern, western, out, result, sems):
    ascending = flags[ASCENDING] == 1
    from_north = jnp.where(ascending, back[...], forward[...])
    from_south = jnp.where(ascending, forward[...], back[...])
    around = turn(sides_of(eastern[...], western[...]))
    lane, row = lane_and_row(rows)
    last, initial = row == rows - 1, row == 0
    to_sides = [
        jnp.where(lane == LANES - 1, coefs[1, k], jnp.where(lane == 0, coefs[2, k], 0.0)) for k in range(levels)
    ]
    to_north = [jnp.where(last, coefs[3, k], 0.0)[rows - 8 :] for k in range(levels)]
    to_south = [jnp.where(initial, coefs[4, k], 0.0)[:8] for k in range(levels)]
    copies = []
    for t in range(tracers):
        for k in range(levels):
            place = k * tracers + t
            total = inner[t, k] + to_sides[k] * side_of(around, place, rows)
            result[t, k, :8, :] = total[:8] + to_south[k] * from_south[place : place + 1]
            result[t, k, 8 : rows - 8, :] = total[8 : rows - 8]
            result[t, k, rows - 8 :, :] = total[rows - 8 :] + to_north[k] * from_north[place : place + 1]
        copy = pltpu.make_async_copy(result.at[t], out.at[t], sems.at[t])
        copy.start()
        copies.append(copy)
    for copy in copies:
        copy.wait()


def up8(count):
    return -(-count // 8) * 8


def call(kernel, scalars, args, outs, scratch=(), placed=(), copies=0, placed_out=False, weight=0):
    vmem, free = pl.BlockSpec(memory_space=pltpu.VMEM), pl.BlockSpec(memory_space=pl.ANY)
    return pl.pallas_call(
        kernel,
        out_shape=[jax.ShapeDtypeStruct(shape, F32) for shape in outs],
        in_specs=[pl.BlockSpec(memory_space=pltpu.SMEM)] * len(scalars) + [free] * len(placed) + [vmem] * len(args),
        out_specs=[free if placed_out else vmem] * len(outs),
        scratch_shapes=[pltpu.VMEM(x.shape, x.dtype) if hasattr(x, "dtype") else pltpu.VMEM(x, F32) for x in scratch]
        + ([pltpu.SemaphoreType.DMA((copies,))] if copies else []),
        compiler_params=pltpu.CompilerParams(vmem_limit_bytes=16 * 1024 * 1024),
        cost_estimate=pl.CostEstimate(flops=int(weight * 1e9), bytes_accessed=0, transcendentals=0),
    )(*scalars, *placed, *args)


def on_device(
    adjoint_field,
    east_courant,
    north_courant,
    pole_courant,
    mix_fraction,
    detrain_share,
    sounding_owner,
    sounding_cell,
    sounding_count,
    sounding_forcing,
):
    lon_count, lat_count = lax.axis_size("lon"), lax.axis_size("lat")
    lon, lat, lev = lax.axis_index("lon"), lax.axis_index("lat"), lax.axis_index("lev")
    tracers, levels, rows, lanes = adjoint_field.shape
    steps, slot_count = sounding_cell.shape
    slabs = tracers * levels
    base = slabs + tracers + 1
    per = lanes // rows
    size = (tracers, levels, rows)

    top, bottom = lat == lat_count - 1, lat == 0
    partner = (lon + lon_count // 2) % lon_count
    flags = [
        top,
        bottom,
        lon < lon_count // 2,
        lev & 1,
        lon * lat_count + lat,
        jnp.where(top, partner * lat_count + lat, lon * lat_count + lat + 1),
        jnp.where(bottom, partner * lat_count + lat, lon * lat_count + lat - 1),
        (lon + 1) % lon_count * lat_count + lat,
        (lon + lon_count - 1) % lon_count * lat_count + lat,
        jnp.where(top, rows - 1, 0),
        jnp.where(bottom, 0, rows - 1),
        (lev ^ (lev >> 1)) & 1,
    ]
    flags = jnp.stack([jnp.asarray(flag, jnp.int32) for flag in flags])

    ring_rows = up8(base + 3 * levels)
    column_rows = up8(2 * (-(-base // per) + 3))
    slot_rows = up8(steps * (levels + 2))
    first_rows = tracers // 2 * rows + rows // 2
    second_rows = tracers // 2 * rows + 5 * (rows // 2)
    soundings = [
        jnp.swapaxes(sounding_count, 0, 1),
        jnp.swapaxes(sounding_owner, 1, 2),
        sounding_cell,
        jnp.swapaxes(sounding_forcing, 0, 1),
    ]
    inputs = [detrain_share, adjoint_field, mix_fraction, east_courant, north_courant, pole_courant]
    keep_first, send_first, slots, detrain, field, mix, east, north, pole = call(
        functools.partial(first_kernel, *size),
        [flags],
        [],
        [(first_rows, lanes)] * 2 + [(slot_count // lanes * slot_rows, lanes)] + [x.shape for x in inputs],
        [(2, first_rows, lanes)] + soundings,
        [pltpu.with_memory_space_constraint(x, pltpu.HBM) for x in soundings + inputs],
        tracers - 1 + len(soundings) + len(inputs),
    )
    static = [detrain, mix, east, north, pole]
    kept = (1.0 - mix)[None] * field
    own_forward, own_back, columns = call(
        functools.partial(edge_kernel, *size),
        [flags],
        [slots, field, kept] + static,
        [(ring_rows, lanes)] * 2 + [(column_rows + slots.shape[0], lanes)],
        [(2, ring_rows, lanes)],
        weight=WEIGHTS[1],
    )
    keep_second, send_second = call(
        functools.partial(inside_kernel, *size),
        [flags],
        [field, kept, detrain, mix, east, north],
        [(second_rows, lanes)] * 2,
        [(2, second_rows, lanes)],
        [columns],
        weight=WEIGHTS[0],
    )
    first = add(keep_first, swap_over(send_first, "lev", 1))
    second = add(keep_second, swap_over(send_second, "lev", 1))
    eastern, western = exchange_columns(columns)
    forward, back = exchange_rows(own_forward, own_back)
    other_first = swap_over(first, "lev", 2)

    late_rows = 2 * (-(-base // per) - slabs // per) + 2 * (tracers // per) + 8 + 4 * tracers + 2
    late, coefs, edges, turned = call(
        functools.partial(second_kernel, *size),
        [flags],
        static
        + [own_forward, own_back, columns[:column_rows]]
        + [forward, back, eastern[:column_rows], western[:column_rows]],
        [(up8(late_rows), lanes), (5, levels, rows, lanes), (2, ring_rows, lanes), (lanes, lanes)],
        placed=[first],
        weight=WEIGHTS[2],
    )
    second = jnp.concatenate([second, late], axis=0)
    other_second = swap_over(second, "lev", 3)
    slots = columns[column_rows:][None]
    if lon_count == 2:
        slots = pair(columns[column_rows:], eastern[column_rows:], first)
    else:
        slots = gather_blocks(slots, "lon")
    slots = gather_blocks(slots, "lat").reshape(-1, slot_rows, lanes)
    grids, edge_rows, sums = call(
        lambda *refs: forcing_kernel(levels, rows, steps, *refs[:7], base, *refs[7:]),
        [flags],
        [slots, detrain, mix, coefs, edges, turned],
        [(3 * levels, rows, lanes), (8, lanes), (2 * rows + 8, lanes)],
        weight=WEIGHTS[3],
    )
    sums = [sums] + [swap_over(sums, "lev", bit) for bit in (1, 2, 3)]
    first = add(first, other_first, sums[0])
    other_first = swap_over(first, "lev", 1)
    second = add(second, other_second, first)
    other_second = swap_over(second, "lev", 1)

    moved, column, inverse = call(
        functools.partial(third_kernel, *size),
        [flags],
        [field, mix, coefs, edges, turned, first, other_first],
        [adjoint_field.shape, (tracers, rows, lanes), (rows, lanes)],
        [(2, first_rows, lanes)],
        weight=WEIGHTS[4],
    )
    slab_rows = up8(slabs)
    mixed, forward, back, columns = call(
        functools.partial(fourth_kernel, *size),
        [flags],
        [
            moved, column, inverse, mix, coefs, edges, turned, grids, edge_rows,
            second, other_second, *sums,
        ],
        [adjoint_field.shape] + [(slab_rows, lanes)] * 2 + [(up8(2 * (slabs // per)), lanes)],
        [(2, second_rows, lanes), (2, slab_rows, lanes)],
    )
    eastern, western = exchange_columns(columns)
    forward, back = exchange_rows(forward, back)
    (inner,) = call(functools.partial(inner_kernel, *size), [flags], [mixed, coefs], [adjoint_field.shape])
    (out,) = call(
        functools.partial(last_kernel, *size),
        [flags],
        [inner, coefs, forward, back, eastern, western],
        [adjoint_field.shape],
        [adjoint_field.shape],
        copies=tracers,
        placed_out=True,
    )
    return out


def solution(mesh):
    return jax.shard_map(
        on_device,
        mesh=mesh,
        in_specs=(
            P(None, "lev", "lat", "lon"),
            P("lev", "lat", "lon"),
            P("lev", "lat", "lon"),
            P("lev", "lon"),
            P("lev", "lat", "lon"),
            P("lev", "lat", "lon"),
            P(None, ("lon", "lat"), None),
            P(None, ("lon", "lat")),
            P(None, ("lon", "lat")),
            P(None, "lev", ("lon", "lat")),
        ),
        out_specs=P(None, "lev", "lat", "lon"),
        check_vma=False,
    )
```

```python
import functools

import jax
import jax.numpy as jnp
from jax import lax
from jax.experimental import pallas as pl
from jax.experimental.pallas import tpu as pltpu
from jax.sharding import PartitionSpec as P

F32 = jnp.float32
WEIGHTS = [0, 0, 0, 20, 20]
LANES = 128
TOP, BOTTOM, ASCENDING, PARITY, SELF, NORTH, SOUTH, EAST, WEST, NORTH_ROW, SOUTH_ROW, LATER_PARITY = range(12)


def swap_over(value, axis, bit):
    return lax.ppermute(value, axis, [(i, i ^ bit) for i in range(lax.axis_size(axis))])


def shift_over(value, axis, steps):
    count = lax.axis_size(axis)
    return lax.ppermute(value, axis, [(i, (i + steps) % count) for i in range(count)])


def meridian_rings(lon_count, lat_count, steps):
    pairs = []
    for lon in range(lon_count // 2):
        ring = [lon * lat_count + lat for lat in range(lat_count)]
        ring += [(lon + lon_count // 2) * lat_count + lat for lat in reversed(range(lat_count))]
        pairs += [(ring[i], ring[(i + steps) % len(ring)]) for i in range(len(ring))]
    return pairs


def exchange_rows(forward, back):
    lon_count, lat_count = lax.axis_size("lon"), lax.axis_size("lat")
    return (
        lax.ppermute(forward, ("lon", "lat"), meridian_rings(lon_count, lat_count, 1)),
        lax.ppermute(back, ("lon", "lat"), meridian_rings(lon_count, lat_count, -1)),
    )


def exchange_columns(columns):
    if lax.axis_size("lon") == 2:
        other = swap_over(columns, "lon", 1)
        return other, other
    return shift_over(columns, "lon", -1), shift_over(columns, "lon", 1)


def pair_kernel(a, b, *refs):
    refs[-1][0] = a[...]
    refs[-1][1] = b[...]


def pair(a, b, *after):
    vmem = pl.BlockSpec(memory_space=pltpu.VMEM)
    return pl.pallas_call(
        pair_kernel,
        out_shape=jax.ShapeDtypeStruct((2, *a.shape), a.dtype),
        in_specs=[vmem, vmem] + [pl.BlockSpec(memory_space=pl.ANY)] * len(after),
        out_specs=vmem,
        compiler_params=pltpu.CompilerParams(vmem_limit_bytes=4 * 1024 * 1024),
    )(a, b, *after)


def gather_blocks(blocks, axis):
    count = lax.axis_size(axis)
    if count not in (2, 4):
        return lax.all_gather(blocks, axis, axis=0, tiled=True)
    return jnp.concatenate([blocks] + [swap_over(blocks, axis, bit) for bit in range(1, count)], axis=0)


def add_kernel(waited, a, b, *refs):
    refs[-1][...] = a[...] + b[...]


def add(a, b, *after):
    vmem = pl.BlockSpec(memory_space=pltpu.VMEM)
    return pl.pallas_call(
        functools.partial(add_kernel, len(after)),
        out_shape=jax.ShapeDtypeStruct(a.shape, a.dtype),
        in_specs=[vmem, vmem] + [pl.BlockSpec(memory_space=pl.ANY)] * len(after),
        out_specs=vmem,
        compiler_params=pltpu.CompilerParams(vmem_limit_bytes=4 * 1024 * 1024),
    )(a, b, *after)


def lane_and_row(rows):
    return (
        lax.broadcasted_iota(jnp.int32, (rows, LANES), 1),
        lax.broadcasted_iota(jnp.int32, (rows, LANES), 0),
    )


def shifted(x, side, north, south):
    rows = x.shape[0]
    lane, row = lane_and_row(rows)
    east = jnp.where(lane == LANES - 1, side, pltpu.roll(x, LANES - 1, 1))
    west = jnp.where(lane == 0, side, pltpu.roll(x, 1, 1))
    above = jnp.where(row == rows - 1, north, pltpu.roll(x, rows - 1, 0))
    below = jnp.where(row == 0, south, pltpu.roll(x, 1, 0))
    return east, west, above, below


def turned_round(x):
    rows = x.shape[0]
    return pltpu.roll(x, LANES - 1, 1), pltpu.roll(x, 1, 1), pltpu.roll(x, rows - 1, 0), pltpu.roll(x, 1, 0)


def stencil(coefs, x, side, north, south):
    east, west, above, below = shifted(x, side, north, south)
    own, to_east, to_west, to_north, to_south = coefs
    return own * x + to_east * east + to_west * west + to_north * above + to_south * below


class Columns:
    def __init__(self, rows):
        self.rows = rows
        self.per = LANES // rows
        self.blocks = [jnp.zeros((rows, LANES), F32)] * self.per
        self.lane = lane_and_row(rows)[0]

    def put(self, index, slab):
        group, place = divmod(index, self.per)
        turned = pltpu.roll(slab, 2 * group + 1, 1)
        self.blocks[place] = jnp.where(self.lane // 2 == group, turned, self.blocks[place])

    def get(self, rows):
        return jnp.transpose(jnp.concatenate(self.blocks, axis=0))[:rows]


def sides_of(eastern, western):
    rows = eastern.shape[0]
    row = lane_and_row(rows)[1]
    return jnp.where(row % 2 == 0, pltpu.roll(eastern, rows - 1, 0), pltpu.roll(western, 1, 0))


def turn(rows):
    pad = jnp.zeros((LANES - rows.shape[0], LANES), F32)
    return jnp.transpose(jnp.concatenate([rows, pad], axis=0))


def side_of(turned, index, rows):
    group, place = divmod(index, LANES // rows)
    return pltpu.roll(turned[place * rows : (place + 1) * rows], (LANES - 2 * group - 1) % LANES, 1)


def tiled(x, rows, block=0):
    if block:
        x = pltpu.roll(x, LANES - block * rows, 1)
    x = jnp.where(lax.broadcasted_iota(jnp.int32, x.shape, 1) < rows, x, 0.0)
    width = rows
    while width < LANES:
        x = x + pltpu.roll(x, width, 1)
        width *= 2
    return x


def first_kernel(
    tracers, levels, rows, flags, counts_in, owners_in, cells_in, forcing_in, detrain_in, field_in, mix_in, east_in,
    north_in, pole_in, keep, send, slots, detrain, field, mix, east, north, pole,
    halves, counts, owners, cells, forcing, sems,
):
    pairs = [(counts_in, counts), (owners_in, owners), (cells_in, cells), (forcing_in, forcing), (detrain_in, detrain)]
    pairs += [(field_in.at[t], field.at[t]) for t in range(tracers)]
    pairs += [(mix_in, mix), (east_in, east), (north_in, north), (pole_in, pole)]
    copies = [pltpu.make_async_copy(source, target, sems.at[i]) for i, (source, target) in enumerate(pairs)]
    for copy in copies[4 : 5 + tracers] + copies[:4] + copies[5 + tracers :]:
        copy.start()
    half = tracers // 2
    slots[...] = jnp.zeros(slots.shape, F32)
    for copy in copies[:5]:
        copy.wait()
    steps, slot_count = cells.shape
    slot_rows = slots.shape[0] * LANES // slot_count
    slot = lax.broadcasted_iota(jnp.int32, (levels, LANES), 1)
    for part in range(slot_count // LANES):
        lanes = slice(part * LANES, (part + 1) * LANES)
        for step in range(steps):
            at = part * slot_rows + step * (levels + 2)
            live = slot + part * LANES < jnp.broadcast_to(counts[:, step : step + 1], slot.shape)
            slots[at : at + levels, :] = jnp.where(live, forcing[:, step, lanes], 0.0)
            slots[at + levels : at + levels + 1, :] = owners[step, :, lanes].astype(F32)
            slots[at + levels + 1 : at + levels + 2, :] = cells[step : step + 1, lanes].astype(F32)
    weights = [detrain[k] for k in range(levels)]
    total = functools.reduce(lambda p, q: p + q, weights)
    for h in range(2):
        halves[h, half * rows :, :] = total[h * rows // 2 : (h + 1) * rows // 2]
    for t in range(tracers):
        copies[5 + t].wait()
        at = (t % half) * rows
        halves[t // half, at : at + rows, :] = functools.reduce(
            lambda p, q: p + q, [weights[k] * field[t, k] for k in range(levels)]
        )
    parity = flags[PARITY]
    keep[...] = halves[parity]
    send[...] = halves[1 - parity]
    for copy in copies[5 + tracers :]:
        copy.wait()


def inside_kernel(tracers, levels, rows, flags, after, field, kept, detrain, mix, east, north, keep, send, halves):
    half = tracers // 2
    lane, row = lane_and_row(rows)
    inside, spread = [], None
    for k in range(levels):
        weight = detrain[k]
        to_east = jnp.maximum(east[k], 0.0)
        to_west = jnp.where(lane == 0, 0.0, jnp.maximum(-pltpu.roll(east[k], 1, 1), 0.0))
        to_north = jnp.maximum(north[k], 0.0)
        to_south = jnp.where(row == 0, 0.0, jnp.maximum(-pltpu.roll(north[k], 1, 0), 0.0))
        five = [
            1.0 - to_east - to_west - to_north - to_south,
            jnp.where(lane == LANES - 1, 0.0, to_east),
            to_west,
            jnp.where(row == rows - 1, 0.0, to_north),
            to_south,
        ]
        inside.append([weight * c for c in five])
        terms = [c * s for c, s in zip(inside[k], (mix[k],) + turned_round(mix[k]))]
        spread = terms if spread is None else [p + q for p, q in zip(spread, terms)]
    for i in range(5):
        for h in range(2):
            at = half * rows + i * (rows // 2)
            halves[h, at : at + rows // 2, :] = spread[i][h * rows // 2 : (h + 1) * rows // 2]
    for t in range(tracers):
        total = None
        for k in range(levels):
            slab = kept[t, k]
            for c, x in zip(inside[k], (slab,) + turned_round(slab)):
                total = c * x if total is None else total + c * x
        at = (t % half) * rows
        halves[t // half, at : at + rows, :] = total
    parity = flags[LATER_PARITY]
    keep[...] = halves[parity]
    send[...] = halves[1 - parity]


def edge_kernel(
    tracers, levels, rows, flags, slots, field, kept, detrain, mix, east, north, pole, forward, back, columns, ring
):
    slabs = tracers * levels
    base = slabs + tracers + 1
    per = LANES // rows
    group = -(-base // per)
    column_rows = up8(2 * (group + 3))
    columns[column_rows:] = slots[...]
    ring[...] = jnp.zeros(ring.shape, F32)
    weights = [detrain[k] for k in range(levels)]
    cols = Columns(rows)

    def edge_rows(place, slab):
        ring[0, place : place + 1, :] = slab[rows - 1 : rows]
        ring[1, place : place + 1, :] = slab[:1]

    total = functools.reduce(lambda p, q: p + q, weights)
    cols.put(slabs + tracers, total)
    edge_rows(slabs + tracers, total)
    for k in range(levels):
        edge_rows(base + k, mix[k])
        edge_rows(base + levels + k, detrain[k])
        ring[0, base + 2 * levels + k : base + 2 * levels + k + 1, :] = north[k, rows - 1 : rows, :]
        ring[1, base + 2 * levels + k : base + 2 * levels + k + 1, :] = pole[k : k + 1, :]
        cols.put(group * per + k, mix[k])
        cols.put((group + 1) * per + k, detrain[k])
        cols.put((group + 2) * per + k, east[k])
    for t in range(tracers):
        partial = None
        for k in range(levels):
            term = weights[k] * field[t, k]
            partial = term if partial is None else partial + term
            slab = kept[t, k]
            cols.put(k * tracers + t, slab)
            edge_rows(k * tracers + t, slab)
        cols.put(slabs + t, partial)
        edge_rows(slabs + t, partial)
    ascending = flags[ASCENDING]
    forward[...] = ring[1 - ascending]
    back[...] = ring[ascending]
    columns[:column_rows] = cols.get(column_rows)


def second_kernel(
    tracers, levels, rows, flags, first, detrain, mix, east, north, pole,
    own_forward, own_back, own_columns, forward, back, eastern, western,
    late, coefs, edges, turned,
):
    slabs = tracers * levels
    base = slabs + tracers + 1
    per = LANES // rows
    group = -(-base // per)
    ascending = flags[ASCENDING] == 1
    from_north = jnp.where(ascending, back[...], forward[...])
    from_south = jnp.where(ascending, forward[...], back[...])
    own_north = jnp.where(ascending, own_forward[...], own_back[...])
    own_south = jnp.where(ascending, own_back[...], own_forward[...])
    edges[0] = from_north
    edges[1] = from_south
    sides = sides_of(eastern[...], western[...])
    mine = own_columns[...]
    around = turn(sides)
    turned[...] = around
    lane, row = lane_and_row(rows)
    top, bottom = flags[TOP] == 1, flags[BOTTOM] == 1
    is_top = jnp.logical_and(row == rows - 1, top)
    is_bottom = jnp.logical_and(row == 0, bottom)
    west_row = lane_and_row(2)[1] == 1
    groups = tracers // per
    zero = jnp.zeros((1, LANES), F32)
    add_north = add_south = spread_north = spread_south = less_north = less_south = 0.0
    add_sides = [0.0] * groups
    spread_sides = less_sides = 0.0
    for k in range(levels):
        place = base + 2 * levels + k
        wind = east[k]
        behind = jnp.where(lane == 0, side_of(around, (group + 2) * per + k, rows), pltpu.roll(wind, 1, 1))
        to_east = jnp.maximum(wind, 0.0)
        to_west = jnp.maximum(-behind, 0.0)
        wind = north[k]
        pole_north = jnp.where(top, jnp.maximum(-from_north[place : place + 1], 0.0), zero)
        to_north = jnp.maximum(wind, 0.0) + jnp.where(is_top, pole_north, 0.0)
        below = from_south[place : place + 1]
        pole_south = jnp.maximum(pole[k : k + 1, :], 0.0) + jnp.maximum(-below, 0.0)
        behind = jnp.where(row == 0, below, pltpu.roll(wind, 1, 0))
        to_south = jnp.where(is_bottom, pole_south, jnp.maximum(-behind, 0.0))
        for i, c in enumerate([1.0 - to_east - to_west - to_north - to_south, to_east, to_west, to_north, to_south]):
            coefs[i, k] = c

        level = slice(k * tracers, (k + 1) * tracers)
        weight = detrain[k, rows - 1 : rows, :]
        taken, given = weight * to_north[rows - 1 : rows], weight * pole_north
        add_north = add_north + taken * from_north[level] - given * own_north[level]
        spread_north = spread_north + taken * from_north[base + k : base + k + 1]
        less_north = less_north - given * mix[k, rows - 1 : rows, :]
        taken = detrain[k, :1, :] * to_south[:1]
        add_south = add_south + taken * (from_south[level] - own_south[level])
        spread_south = spread_south + taken * from_south[base + k : base + k + 1]
        less_south = less_south - taken * mix[k, :1, :]

        winds = slice(2 * (group + 2), 2 * (group + 3))
        shares = slice(2 * group, 2 * (group + 1))
        weight = tiled(mine[2 * (group + 1) : 2 * (group + 2)], rows, k)
        wind = jnp.where(west_row, jnp.maximum(-sides[winds], 0.0), jnp.maximum(mine[winds], 0.0))
        taken = weight * tiled(wind, rows, k)
        given = jnp.where(west_row, taken, 0.0)
        for g in range(groups):
            pair = slice(2 * (k * groups + g), 2 * (k * groups + g + 1))
            add_sides[g] = add_sides[g] + taken * sides[pair] - given * mine[pair]
        spread_sides = spread_sides + taken * tiled(sides[shares], rows, k)
        less_sides = less_sides - given * tiled(mine[shares], rows, k)
    parts = [sides[2 * (slabs // per) : 2 * group]] + add_sides
    parts += [spread_sides, less_sides, spread_north, spread_south, less_north, less_south]
    parts += [add_north, add_south, from_north[slabs : slabs + tracers + 1], from_south[slabs : slabs + tracers + 1]]
    at = 0
    for part in parts:
        late[at : at + part.shape[0]] = part
        at += part.shape[0]
    if at < late.shape[0]:
        late[at:] = jnp.zeros((late.shape[0] - at, LANES), F32)


def pieces(x):
    high = x.astype(jnp.bfloat16)
    return [high, (x - high.astype(F32)).astype(jnp.bfloat16)]


def product(a, b):
    return lax.dot_general(a, b, (((1,), (1,)), ((), ())), preferred_element_type=F32)


def forcing_kernel(levels, rows, steps, flags, slots, detrain, mix, coefs, edges, turned, base, grids, edge_rows, sums):
    parts = min(8, slots.shape[0])
    count = parts * LANES
    per = LANES // rows
    row_ids = lax.broadcasted_iota(jnp.int32, (rows, count), 0)
    lane_ids = lax.broadcasted_iota(jnp.int32, (LANES, count), 0)
    group = -(-base // per)

    def add_block(index, carry):
        late, early, ring_sides = carry
        block = jnp.concatenate([slots[parts * index + part] for part in range(parts)], axis=1)
        results = []
        for step in range(steps):
            first = step * (levels + 2)
            values = [block[first + k : first + k + 1] for k in range(levels)]
            owner = block[first + levels : first + levels + 1].astype(jnp.int32)
            cell = block[first + levels + 1 : first + levels + 2].astype(jnp.int32)
            slot_row, slot_lane = cell // LANES, cell % LANES
            lanes = (lane_ids == slot_lane).astype(F32).astype(jnp.bfloat16)
            here = jnp.logical_and(row_ids == slot_row, owner == flags[SELF])
            left = [jnp.where(here, value, 0.0) for value in values]
            if step == steps - 1:
                in_north = jnp.logical_and(owner == flags[NORTH], slot_row == flags[NORTH_ROW])
                in_south = jnp.logical_and(owner == flags[SOUTH], slot_row == flags[SOUTH_ROW])
                left += [jnp.where(in_north, value, 0.0) for value in values]
                left += [jnp.where(in_south, value, 0.0) for value in values]
                left += [jnp.zeros((8 - 2 * levels, count), F32)]
            left = jnp.concatenate(left, axis=0)
            results.append(sum(product(piece, lanes) for piece in pieces(left)))
            if step == steps - 1:
                in_east = jnp.logical_and(owner == flags[EAST], slot_lane == 0)
                in_west = jnp.logical_and(owner == flags[WEST], slot_lane == LANES - 1)
                right = [jnp.where(in_east, value, 0.0) for value in values]
                right += [jnp.where(in_west, value, 0.0) for value in values]
                right += [jnp.zeros((8 - 2 * levels, count), F32)]
                right = jnp.concatenate(right, axis=0)
                at_row = (row_ids == slot_row).astype(F32).astype(jnp.bfloat16)
                ring_sides = ring_sides + sum(product(at_row, piece) for piece in pieces(right))
        return late + results[1], early + results[0], ring_sides

    late, early, ring_sides = lax.fori_loop(
        0,
        slots.shape[0] // parts,
        add_block,
        (
            jnp.zeros((levels * rows + 8, LANES), F32),
            jnp.zeros((levels * rows, LANES), F32),
            jnp.zeros((rows, 8), F32),
        ),
        unroll=slots.shape[0] // parts <= 2,
    )
    lane, _ = lane_and_row(rows)
    north_rows = late[levels * rows : levels * rows + levels]
    south_rows = late[levels * rows + levels : levels * rows + 2 * levels]
    edge_rows[...] = late[levels * rows :]
    around = turned[...]
    at_end = at_first = None
    ring = jnp.zeros((rows, LANES), F32)
    ring_north = jnp.zeros((1, LANES), F32)
    ring_south = jnp.zeros((1, LANES), F32)
    for k in range(levels):
        own = late[k * rows : (k + 1) * rows]
        now = early[k * rows : (k + 1) * rows]
        east_side = jnp.broadcast_to(ring_sides[:, k : k + 1], (rows, LANES))
        west_side = jnp.broadcast_to(ring_sides[:, levels + k : levels + k + 1], (rows, LANES))
        side = jnp.where(lane == LANES - 1, east_side, jnp.where(lane == 0, west_side, 0.0))
        grids[k] = own
        grids[levels + k] = now
        grids[2 * levels + k] = side
        mix_side = side_of(around, group * per + k, rows)
        detrain_side = side_of(around, (group + 1) * per + k, rows)
        north, south = north_rows[k : k + 1], south_rows[k : k + 1]
        moved = stencil(
            [coefs[i, k] for i in range(5)],
            (1.0 - mix[k]) * own,
            (1.0 - mix_side) * side,
            (1.0 - edges[0, base + k : base + k + 1, :]) * north,
            (1.0 - edges[1, base + k : base + k + 1, :]) * south,
        )
        first = detrain[k] * own
        second = detrain[k] * (moved + now)
        at_first = first if at_first is None else at_first + first
        at_end = second if at_end is None else at_end + second
        ring = ring + detrain_side * side
        place = base + levels + k
        ring_north = ring_north + edges[0, place : place + 1, :] * north
        ring_south = ring_south + edges[1, place : place + 1, :] * south
    sums[:rows] = at_first
    sums[rows : 2 * rows] = at_end
    flat = jnp.transpose(jnp.concatenate([ring] + [jnp.zeros((rows, LANES), F32)] * (per - 1), axis=0))
    sums[2 * rows :] = jnp.concatenate(
        [ring_north, ring_south, flat[LANES - 1 :], flat[:1], jnp.zeros((4, LANES), F32)], axis=0
    )


def third_kernel(
    tracers, levels, rows, flags, field, mix, coefs, edges, turned, mine, other, moved_out, column_out, inverse_out, first,
):
    half = tracers // 2
    parity = flags[PARITY]
    first[parity] = mine[...]
    first[1 - parity] = other[...]
    total = jnp.concatenate([first[0, half * rows :, :], first[1, half * rows :, :]], axis=0)
    inverse = 1.0 / total
    inverse_out[...] = inverse
    around = turned[...]
    stay = [1.0 - mix[k] for k in range(levels)]
    five = [[coefs[i, k] for i in range(5)] for k in range(levels)]
    for t in range(tracers):
        column = first[t // half, (t % half) * rows : (t % half + 1) * rows, :] * inverse
        column_out[t] = column
        for k in range(levels):
            place = k * tracers + t
            moved = stencil(
                five[k],
                stay[k] * field[t, k] + mix[k] * column,
                side_of(around, place, rows),
                edges[0, place : place + 1, :],
                edges[1, place : place + 1, :],
            )
            moved_out[t, k] = stay[k] * moved


def fourth_kernel(
    tracers, levels, rows, flags, moved, column, inverse_in, mix, coefs, edges, turned, grids, edge_rows,
    mine, other, forced_1, forced_2, forced_3, forced_4, mixed_out, forward, back, columns, second, ring,
):
    half = tracers // 2
    slabs = tracers * levels
    base = slabs + tracers + 1
    per = LANES // rows
    group = -(-base // per)
    groups = tracers // per
    parity = flags[LATER_PARITY]
    second_rows = second.shape[1]
    second[parity] = mine[:second_rows]
    second[1 - parity] = other[:second_rows]
    late = mine[second_rows:] + other[second_rows:]
    forced = (forced_1[...] + forced_2[...]) + (forced_3[...] + forced_4[...])
    inverse = inverse_in[...]
    lane, row = lane_and_row(rows)
    at_side = jnp.logical_or(lane == 0, lane == LANES - 1)
    last, initial = row == rows - 1, row == 0

    at = 2 * (group - slabs // per)
    inverse_side = 1.0 / tiled(late[2 * groups : 2 * groups + 2], rows)
    forced_sides = tiled(forced[2 * rows + 2 : 2 * rows + 4], rows)
    side_rows = [(late[2 * g : 2 * g + 2] + forced_sides) * inverse_side for g in range(groups)]
    side_rows += [late[at : at + 2 * groups + 4]]
    at += 2 * groups + 4
    around_late = turn(jnp.concatenate(side_rows, axis=0))
    spread_side = side_of(around_late, 2 * groups * per, rows)
    less_side = side_of(around_late, (2 * groups + 1) * per, rows)
    north, south, less_north, less_south = [late[at + i : at + i + 1] for i in range(4)]
    at += 4
    add_ends = [late[at + e * tracers : at + (e + 1) * tracers] for e in range(2)]
    at += 2 * tracers
    column_ends = []
    for e in range(2):
        sums = late[at : at + tracers + 1]
        column_ends.append((sums[:tracers] + forced[2 * rows + e : 2 * rows + e + 1]) / sums[tracers:])
        at += tracers + 1

    spread = []
    start = half * rows
    for i in range(5):
        at = start + i * (rows // 2)
        spread.append(jnp.concatenate([second[h, at : at + rows // 2, :] for h in range(2)], axis=0))
    spread[0] = spread[0] + jnp.where(last, less_north, 0.0) + jnp.where(initial, less_south, 0.0)
    spread[0] = spread[0] + jnp.where(lane == 0, less_side, 0.0)
    spread[1] = jnp.where(lane == LANES - 1, spread_side, spread[1])
    spread[2] = spread[2] + jnp.where(lane == 0, spread_side, 0.0)
    spread[3] = jnp.where(last, north, spread[3])
    spread[4] = spread[4] + jnp.where(initial, south, 0.0)

    forced_column = forced[:rows] * inverse
    forced_later = forced[rows : 2 * rows]
    around = turned[...]
    stay = [1.0 - mix[k] for k in range(levels)]
    forced_moved, to_sides, to_ends = [], [], []
    for k in range(levels):
        five = [coefs[i, k] for i in range(5)]
        mix_side = side_of(around, group * per + k, rows)
        shares = [edges[e, base + k : base + k + 1, :] for e in range(2)]
        ends = [(1.0 - shares[e]) * edge_rows[e * levels + k : e * levels + k + 1, :] for e in range(2)]
        moved_forcing = stencil(
            five,
            stay[k] * grids[k] + mix[k] * forced_column,
            (1.0 - mix_side) * grids[2 * levels + k],
            ends[0],
            ends[1],
        )
        forced_moved.append(stay[k] * (moved_forcing + grids[levels + k]))
        to_side = jnp.where(lane == LANES - 1, five[1], jnp.where(lane == 0, five[2], 0.0))
        to_sides.append(stay[k] * to_side * mix_side)
        to_ends.append(
            [
                jnp.where(last, stay[k] * five[3] * shares[0], 0.0)[rows - 8 :],
                jnp.where(initial, stay[k] * five[4] * shares[1], 0.0)[:8],
            ]
        )

    cols = Columns(rows)
    ring[...] = jnp.zeros(ring.shape, F32)
    for t in range(tracers):
        h, at = t // half, (t % half) * rows
        column_side = side_of(around_late, t, rows)
        column_north, column_south = column_ends[0][t : t + 1], column_ends[1][t : t + 1]
        later = second[h, at : at + rows, :] + forced_later
        later = later + jnp.where(at_side, side_of(around_late, (groups + t // per) * per + t % per, rows), 0.0)
        later = later + jnp.where(last, add_ends[0][t : t + 1], 0.0)
        later = later + jnp.where(initial, add_ends[1][t : t + 1], 0.0)
        later = later + stencil(spread, column[t] + forced_column, column_side, column_north, column_south)
        later = later * inverse
        for k in range(levels):
            place = k * tracers + t
            mixed = moved[t, k] + forced_moved[k] + mix[k] * later + to_sides[k] * column_side
            mixed = jnp.concatenate(
                [
                    mixed[:8] + to_ends[k][1] * column_south,
                    mixed[8 : rows - 8],
                    mixed[rows - 8 :] + to_ends[k][0] * column_north,
                ],
                axis=0,
            )
            mixed_out[t, k] = mixed
            cols.put(place, mixed)
            ring[0, place : place + 1, :] = mixed[rows - 1 : rows]
            ring[1, place : place + 1, :] = mixed[:1]
    ascending = flags[ASCENDING]
    forward[...] = ring[1 - ascending]
    back[...] = ring[ascending]
    columns[...] = cols.get(columns.shape[0])


def inner_kernel(tracers, levels, rows, flags, mixed, coefs, out):
    lane, row = lane_and_row(rows)
    for k in range(levels):
        own, to_east, to_west, to_north, to_south = [coefs[i, k] for i in range(5)]
        five = [
            own,
            jnp.where(lane == LANES - 1, 0.0, to_east),
            jnp.where(lane == 0, 0.0, to_west),
            jnp.where(row == rows - 1, 0.0, to_north),
            jnp.where(row == 0, 0.0, to_south),
        ]
        for t in range(tracers):
            slab = mixed[t, k]
            total = None
            for c, x in zip(five, (slab,) + turned_round(slab)):
                total = c * x if total is None else total + c * x
            out[t, k] = total


def last_kernel(tracers, levels, rows, flags, inner, coefs, forward, back, eastern, western, out, result, sems):
    ascending = flags[ASCENDING] == 1
    from_north = jnp.where(ascending, back[...], forward[...])
    from_south = jnp.where(ascending, forward[...], back[...])
    around = turn(sides_of(eastern[...], western[...]))
    lane, row = lane_and_row(rows)
    last, initial = row == rows - 1, row == 0
    to_sides = [
        jnp.where(lane == LANES - 1, coefs[1, k], jnp.where(lane == 0, coefs[2, k], 0.0)) for k in range(levels)
    ]
    to_north = [jnp.where(last, coefs[3, k], 0.0)[rows - 8 :] for k in range(levels)]
    to_south = [jnp.where(initial, coefs[4, k], 0.0)[:8] for k in range(levels)]
    copies = []
    for t in range(tracers):
        for k in range(levels):
            place = k * tracers + t
            total = inner[t, k] + to_sides[k] * side_of(around, place, rows)
            result[t, k, :8, :] = total[:8] + to_south[k] * from_south[place : place + 1]
            result[t, k, 8 : rows - 8, :] = total[8 : rows - 8]
            result[t, k, rows - 8 :, :] = total[rows - 8 :] + to_north[k] * from_north[place : place + 1]
        copy = pltpu.make_async_copy(result.at[t], out.at[t], sems.at[t])
        copy.start()
        copies.append(copy)
    for copy in copies:
        copy.wait()


def up8(count):
    return -(-count // 8) * 8


def call(kernel, scalars, args, outs, scratch=(), placed=(), copies=0, placed_out=False, weight=0):
    vmem, free = pl.BlockSpec(memory_space=pltpu.VMEM), pl.BlockSpec(memory_space=pl.ANY)
    return pl.pallas_call(
        kernel,
        out_shape=[jax.ShapeDtypeStruct(shape, F32) for shape in outs],
        in_specs=[pl.BlockSpec(memory_space=pltpu.SMEM)] * len(scalars) + [free] * len(placed) + [vmem] * len(args),
        out_specs=[free if placed_out else vmem] * len(outs),
        scratch_shapes=[pltpu.VMEM(x.shape, x.dtype) if hasattr(x, "dtype") else pltpu.VMEM(x, F32) for x in scratch]
        + ([pltpu.SemaphoreType.DMA((copies,))] if copies else []),
        compiler_params=pltpu.CompilerParams(vmem_limit_bytes=16 * 1024 * 1024),
        cost_estimate=pl.CostEstimate(flops=int(weight * 1e9), bytes_accessed=0, transcendentals=0),
    )(*scalars, *placed, *args)


def on_device(
    adjoint_field,
    east_courant,
    north_courant,
    pole_courant,
    mix_fraction,
    detrain_share,
    sounding_owner,
    sounding_cell,
    sounding_count,
    sounding_forcing,
):
    lon_count, lat_count = lax.axis_size("lon"), lax.axis_size("lat")
    lon, lat, lev = lax.axis_index("lon"), lax.axis_index("lat"), lax.axis_index("lev")
    tracers, levels, rows, lanes = adjoint_field.shape
    steps, slot_count = sounding_cell.shape
    slabs = tracers * levels
    base = slabs + tracers + 1
    per = lanes // rows
    size = (tracers, levels, rows)

    top, bottom = lat == lat_count - 1, lat == 0
    partner = (lon + lon_count // 2) % lon_count
    flags = [
        top,
        bottom,
        lon < lon_count // 2,
        lev & 1,
        lon * lat_count + lat,
        jnp.where(top, partner * lat_count + lat, lon * lat_count + lat + 1),
        jnp.where(bottom, partner * lat_count + lat, lon * lat_count + lat - 1),
        (lon + 1) % lon_count * lat_count + lat,
        (lon + lon_count - 1) % lon_count * lat_count + lat,
        jnp.where(top, rows - 1, 0),
        jnp.where(bottom, 0, rows - 1),
        (lev ^ (lev >> 1)) & 1,
    ]
    flags = jnp.stack([jnp.asarray(flag, jnp.int32) for flag in flags])

    ring_rows = up8(base + 3 * levels)
    column_rows = up8(2 * (-(-base // per) + 3))
    slot_rows = up8(steps * (levels + 2))
    first_rows = tracers // 2 * rows + rows // 2
    second_rows = tracers // 2 * rows + 5 * (rows // 2)
    soundings = [
        jnp.swapaxes(sounding_count, 0, 1),
        jnp.swapaxes(sounding_owner, 1, 2),
        sounding_cell,
        jnp.swapaxes(sounding_forcing, 0, 1),
    ]
    inputs = [detrain_share, adjoint_field, mix_fraction, east_courant, north_courant, pole_courant]
    keep_first, send_first, slots, detrain, field, mix, east, north, pole = call(
        functools.partial(first_kernel, *size),
        [flags],
        [],
        [(first_rows, lanes)] * 2 + [(slot_count // lanes * slot_rows, lanes)] + [x.shape for x in inputs],
        [(2, first_rows, lanes)] + soundings,
        [pltpu.with_memory_space_constraint(x, pltpu.HBM) for x in soundings + inputs],
        tracers - 1 + len(soundings) + len(inputs),
    )
    static = [detrain, mix, east, north, pole]
    kept = (1.0 - mix)[None] * field
    own_forward, own_back, columns = call(
        functools.partial(edge_kernel, *size),
        [flags],
        [slots, field, kept] + static,
        [(ring_rows, lanes)] * 2 + [(column_rows + slots.shape[0], lanes)],
        [(2, ring_rows, lanes)],
        weight=WEIGHTS[1],
    )
    keep_second, send_second = call(
        functools.partial(inside_kernel, *size),
        [flags],
        [field, kept, detrain, mix, east, north],
        [(second_rows, lanes)] * 2,
        [(2, second_rows, lanes)],
        [columns],
        weight=WEIGHTS[0],
    )
    first = add(keep_first, swap_over(send_first, "lev", 1))
    second = add(keep_second, swap_over(send_second, "lev", 1))
    eastern, western = exchange_columns(columns)
    forward, back = exchange_rows(own_forward, own_back)
    other_first = swap_over(first, "lev", 2)

    late_rows = 2 * (-(-base // per) - slabs // per) + 2 * (tracers // per) + 8 + 4 * tracers + 2
    late, coefs, edges, turned = call(
        functools.partial(second_kernel, *size),
        [flags],
        static
        + [own_forward, own_back, columns[:column_rows]]
        + [forward, back, eastern[:column_rows], western[:column_rows]],
        [(up8(late_rows), lanes), (5, levels, rows, lanes), (2, ring_rows, lanes), (lanes, lanes)],
        placed=[first],
        weight=WEIGHTS[2],
    )
    second = jnp.concatenate([second, late], axis=0)
    other_second = swap_over(second, "lev", 3)
    slots = columns[column_rows:][None]
    if lon_count == 2:
        slots = pair(columns[column_rows:], eastern[column_rows:], first)
    else:
        slots = gather_blocks(slots, "lon")
    slots = gather_blocks(slots, "lat").reshape(-1, slot_rows, lanes)
    grids, edge_rows, sums = call(
        lambda *refs: forcing_kernel(levels, rows, steps, *refs[:7], base, *refs[7:]),
        [flags],
        [slots, detrain, mix, coefs, edges, turned],
        [(3 * levels, rows, lanes), (8, lanes), (2 * rows + 8, lanes)],
        weight=WEIGHTS[3],
    )
    sums = [sums] + [swap_over(sums, "lev", bit) for bit in (3, 2, 1)]
    first = add(first, other_first, sums[0])
    other_first = swap_over(first, "lev", 1)
    second = add(second, other_second, first)
    other_second = swap_over(second, "lev", 1)

    moved, column, inverse = call(
        functools.partial(third_kernel, *size),
        [flags],
        [field, mix, coefs, edges, turned, first, other_first],
        [adjoint_field.shape, (tracers, rows, lanes), (rows, lanes)],
        [(2, first_rows, lanes)],
        weight=WEIGHTS[4],
    )
    slab_rows = up8(slabs)
    mixed, forward, back, columns = call(
        functools.partial(fourth_kernel, *size),
        [flags],
        [
            moved, column, inverse, mix, coefs, edges, turned, grids, edge_rows,
            second, other_second, *sums,
        ],
        [adjoint_field.shape] + [(slab_rows, lanes)] * 2 + [(up8(2 * (slabs // per)), lanes)],
        [(2, second_rows, lanes), (2, slab_rows, lanes)],
    )
    eastern, western = exchange_columns(columns)
    forward, back = exchange_rows(forward, back)
    (inner,) = call(functools.partial(inner_kernel, *size), [flags], [mixed, coefs], [adjoint_field.shape])
    (out,) = call(
        functools.partial(last_kernel, *size),
        [flags],
        [inner, coefs, forward, back, eastern, western],
        [adjoint_field.shape],
        [adjoint_field.shape],
        copies=tracers,
        placed_out=True,
    )
    return out


def solution(mesh):
    return jax.shard_map(
        on_device,
        mesh=mesh,
        in_specs=(
            P(None, "lev", "lat", "lon"),
            P("lev", "lat", "lon"),
            P("lev", "lat", "lon"),
            P("lev", "lon"),
            P("lev", "lat", "lon"),
            P("lev", "lat", "lon"),
            P(None, ("lon", "lat"), None),
            P(None, ("lon", "lat")),
            P(None, ("lon", "lat")),
            P(None, "lev", ("lon", "lat")),
        ),
        out_specs=P(None, "lev", "lat", "lon"),
        check_vma=False,
    )
```
